512 devices in a mesh: ctx: 64 (over y, z), ch: 8 (over x, core).
Axes of the slice: x: 4, y: 8, z: 8, core: 2. Of those that a mesh axis runs over, the one named last changes fastest.
Arguments:
- query_field: bfloat16 [8192, 4096], P('ctx', 'ch'), may hold values from -6 to 6
- key_field: bfloat16 [8192, 4096], P('ctx', 'ch'), may hold values from -6 to 6
- value_field: bfloat16 [8192, 4096], P('ctx', 'ch'), may hold values from -6 to 6
- short_taps: float32 [3, 7, 4096], P(None, None, 'ch'), may hold values from -2 to 2
- filt_in: float32 [33, 64], replicated, may hold values from -1 to 1
- filt_mid: float32 [64, 64], replicated, may hold values from -0.75 to 0.75
- filt_out: float32 [64, 4096], P(None, 'ch'), may hold values from -0.75 to 0.75
- decay_rate: float32 [4096], P('ch'), may hold values from 3.0517578e-05 to 0.041666668
- skip_gain: float32 [4096], P('ch'), may hold values from -4 to 4
- out_weight: bfloat16 [4096, 2048], P('ch'), may hold values from -0.09375 to 0.09375
Outputs:
- projected: bfloat16 [8192, 2048], P(('ctx', 'ch'))
The draws below stay inside these ranges and needn't reach their ends.
All inputs are finite; a program needn't handle non-finite values.
Results may differ from the reference program's by a relative error of at most 0.017.
Values may be sent and summed in bfloat16 or wider, within the bound.
No kernel may reach another device: no remote copies, remote signals or barrier semaphores. Data moves between devices by JAX's collectives and lax.ppermute only.
A program may use at most 64 MiB of HBM per device.

```python
import math
import jax
import jax.numpy as jnp
from jax import lax

D = 4096
DOUT = 2048
ORDER = 64
BANDS = 16
TAPS = 7
TOKENS = 8192
EMB = 33
D_CH = 512
N_CH = 8


def levels(key, extent, shards, low, top_value):
    def one(axis_at, shards_of):
        steps = jax.random.uniform(jax.random.fold_in(jax.random.fold_in(key, 6), axis_at), (shards_of,), jnp.float32, low / len(shards), top_value / len(shards))
        return jnp.repeat(jnp.exp(steps), extent[axis_at] // shards_of).reshape((-1,) + (1,) * (len(extent) - axis_at - 1))

    gain = one(*shards[0])
    for cut in shards[1:]:
        gain = gain * one(*cut)
    return gain


def noise(own_key, dims, scale, bound, split=(), held_as=jnp.bfloat16):
    gain = levels(own_key, dims, split, -0.22, 0.18) if split else 1.0
    result = jax.random.normal(own_key, dims, jnp.float32) * scale * gain
    return jnp.minimum(jnp.maximum(result, -bound), bound).astype(held_as)


def setup_inputs(seed: int = 0) -> dict:
    seeds = jax.random.split(jax.random.key(seed), 11)
    query_field = noise(seeds[0], (TOKENS, D), 1.0, 6.0, ((0, 64), (1, 8)))
    key_field = noise(seeds[1], (TOKENS, D), 1.0, 6.0, ((0, 64), (1, 8)))
    value_field = noise(seeds[2], (TOKENS, D), 1.0, 6.0, ((0, 64), (1, 8)))
    short_taps = noise(seeds[3], (3, TAPS, D), TAPS ** -0.5, 2.0, ((2, 8),), jnp.float32)
    filt_in = noise(seeds[4], (EMB, ORDER), EMB ** -0.5, 1.0, (), jnp.float32)
    filt_mid = noise(seeds[5], (ORDER, ORDER), ORDER ** -0.5, 0.75, (), jnp.float32)
    filt_out = noise(seeds[6], (ORDER, D), ORDER ** -0.5, 0.75, ((1, 8),), jnp.float32)
    decay_rate = jnp.clip(jnp.exp(math.log(0.041666668) - 7.219154 * jax.random.uniform(seeds[7], (D,), jnp.float32) ** levels(seeds[7], (D,), ((0, 8),), -0.2, 0.2)), 3.0517578125e-05, 0.041666668)
    skip_gain = noise(seeds[8], (D,), 1.0, 4.0, ((0, 8),), jnp.float32)
    out_weight = noise(seeds[9], (D, DOUT), D ** -0.5, 0.09375, ((0, 8),))
    return dict(query_field=query_field, key_field=key_field, value_field=value_field, short_taps=short_taps, filt_in=filt_in, filt_mid=filt_mid, filt_out=filt_out, decay_rate=decay_rate, skip_gain=skip_gain, out_weight=out_weight)


highest = lax.Precision.HIGHEST

def position_features(tokens, band_count):
    steps_t = jnp.arange(tokens, dtype=jnp.int32)
    band_ids = jnp.arange(band_count, dtype=jnp.int32)
    frequency = 1 + band_ids * band_ids * (tokens // 4 - 1) // ((band_count - 1) * (band_count - 1))
    phase_idx = frequency[:, None] * steps_t[None, :] % tokens
    angles = phase_idx.astype(jnp.float32) * (2.0 * math.pi / tokens)
    ramp_time = (steps_t.astype(jnp.float32) / tokens)[None, :]
    return jnp.concatenate([ramp_time, jnp.cos(angles), jnp.sin(angles)], 0)

def short_mix(padded, taps_set, lead_rows):
    length = padded.shape[2] - lead_rows
    running = jnp.zeros(padded.shape[:2] + (length,), jnp.float32)
    for tap_pos in range(lead_rows + 1):
        window = padded[:, :, lead_rows - tap_pos:lead_rows - tap_pos + length].astype(jnp.float32)
        running = running + taps_set[:, tap_pos, :, None] * window
    return running.astype(jnp.bfloat16)

def reference(query_field, key_field, value_field, short_taps, filt_in, filt_mid, filt_out, decay_rate, skip_gain, out_weight):
    features = position_features(TOKENS, BANDS)
    layer_one = jnp.sin(jnp.dot(filt_in.T, features, precision=highest, preferred_element_type=jnp.float32))
    layer_two = jnp.sin(jnp.dot(filt_mid.T, layer_one, precision=highest, preferred_element_type=jnp.float32))
    ramp_time = jnp.arange(TOKENS, dtype=jnp.int32).astype(jnp.float32)
    width_blk = 128 if D % 128 == 0 else D
    lead_rows = TAPS - 1
    points = 2 * TOKENS

    def one_block(block_id):
        first_col = (block_id * width_blk).astype(jnp.int32)

        def cut_block(source_arr, along_dim):
            return lax.dynamic_slice_in_dim(source_arr, first_col, width_blk, along_dim)
        stacked = jnp.stack([cut_block(query_field, 1).T, cut_block(key_field, 1).T, cut_block(value_field, 1).T], 0)
        padded = jnp.pad(stacked, ((0, 0), (0, 0), (lead_rows, 0)))
        fields = short_mix(padded, cut_block(short_taps, 2), lead_rows)
        product = fields[1].astype(jnp.float32) * fields[2].astype(jnp.float32)
        rates_blk = cut_block(decay_rate, 0)
        shape_rows = jnp.dot(cut_block(filt_out, 1).T, layer_two, precision=highest, preferred_element_type=jnp.float32)
        long_filter = jnp.sqrt(2.0 * rates_blk)[:, None] * jnp.exp(-rates_blk[:, None] * ramp_time[None, :]) * shape_rows
        spectrum = jnp.fft.rfft(product, n=points, axis=1) * jnp.fft.rfft(long_filter, n=points, axis=1)
        convolved = jnp.fft.irfft(spectrum, n=points, axis=1)[:, :TOKENS]
        gated_out = fields[0].astype(jnp.float32) * (convolved + cut_block(skip_gain, 0)[:, None] * product)
        return gated_out.astype(jnp.bfloat16)
    blocks = lax.map(one_block, jnp.arange(D // width_blk, dtype=jnp.int32))
    gated_out = blocks.reshape(D, TOKENS)
    running = jnp.zeros((TOKENS, DOUT), jnp.float32)
    for group_id in range(N_CH):
        group_rows = gated_out[group_id * D_CH:(group_id + 1) * D_CH]
        partial_value = lax.dot_general(group_rows, out_weight[group_id * D_CH:(group_id + 1) * D_CH], (((0,), (0,)), ((), ())), preferred_element_type=jnp.float32)
        rounded = lax.optimization_barrier(partial_value.astype(jnp.bfloat16))
        running = running + rounded.astype(jnp.float32)
    return running.astype(jnp.bfloat16)
```

```python
import math

import jax
import jax.numpy as jnp
import numpy as np
from jax import lax
from jax.experimental import pallas as pl
from jax.experimental.pallas import tpu as pltpu
from jax.sharding import PartitionSpec as P

TOKENS = 8192
BLK = 128
NBLK = 64
CH = 8
BANDS = 16
FEAT = 33
FEAT_PAD = 48
TAPS = 7
UNITS = 64
CHUNK = 1024
bf16 = jnp.bfloat16
f32 = jnp.float32
highest = lax.Precision.HIGHEST


def split_np(table):
    table = np.asarray(table, np.float32)
    top = table.astype(jnp.bfloat16)
    low = (table - top.astype(np.float32)).astype(jnp.bfloat16)
    return top, low


def feature_table():
    steps = np.arange(TOKENS, dtype=np.int64)
    bands = np.arange(BANDS, dtype=np.int64)
    freq = 1 + bands * bands * (TOKENS // 4 - 1) // ((BANDS - 1) * (BANDS - 1))
    ang = (freq[:, None] * steps[None, :] % TOKENS) * (2.0 * math.pi / TOKENS)
    rows = np.concatenate([(steps / TOKENS)[None, :], np.cos(ang), np.sin(ang)], 0)
    rows = np.concatenate([rows, np.zeros((FEAT_PAD - FEAT, TOKENS))], 0)
    top, low = split_np(rows)
    return np.concatenate([top, low, top], 0)


def dft_tables():
    shifted = np.arange(NBLK) - 0.25
    block = np.arange(NBLK)
    inner = np.arange(BLK)
    outer_ang = 2.0 * math.pi * shifted[:, None] * block[None, :] / NBLK
    first = np.concatenate([np.cos(outer_ang), -np.sin(outer_ang)], 0)
    top, low = split_np(first)
    first_stack = np.concatenate([top, top, low], 1)
    last = np.concatenate([np.cos(outer_ang).T, -np.sin(outer_ang).T], 1) / TOKENS
    top, low = split_np(last)
    last_stack = np.concatenate([top, top, low], 1)
    tw_ang = 2.0 * math.pi * shifted[:, None] * inner[None, :] / TOKENS
    twiddle = np.stack([np.cos(tw_ang), -np.sin(tw_ang)], 0).astype(np.float32)
    in_ang = 2.0 * math.pi * (inner[:, None] * inner[None, :] % BLK) / BLK
    cos_in, sin_in = np.cos(in_ang), np.sin(in_ang)
    fwd = np.block([[cos_in, -sin_in], [sin_in, cos_in]])
    bwd = np.block([[cos_in, sin_in], [-sin_in, cos_in]])
    fwd_pair = np.stack(split_np(fwd), 0)
    bwd_pair = np.stack(split_np(bwd), 0)
    return first_stack, last_stack, twiddle, fwd_pair, bwd_pair


def sine_coefs():
    grid = 0.25 * np.cos((np.arange(400) + 0.5) * math.pi / 400)
    grid = np.concatenate([grid, 0.5 * np.cos((np.arange(800) + 0.5) * math.pi / 800)])
    grid = grid[np.abs(grid) > 1e-3]
    powers = np.stack([grid ** (2 * k + 1) for k in range(7)], 1)
    coef, *_ = np.linalg.lstsq(powers, np.sin(2.0 * math.pi * grid), rcond=None)
    return [float(c) for c in coef]


SINE = sine_coefs()


def sine_turns(turns):
    rest = turns - jnp.round(turns)
    sq = rest * rest
    acc = jnp.full_like(sq, SINE[-1])
    for c in SINE[-2::-1]:
        acc = acc * sq + c
    return acc * rest


def split(value):
    top = value.astype(bf16)
    return top, (value - top.astype(f32)).astype(bf16)


def mm(left, right):
    return jnp.dot(left, right, preferred_element_type=f32)


def mm_split(value, pair_ref):
    top, low = split(value)
    return mm(top, pair_ref[0]) + mm(low, pair_ref[0]) + mm(top, pair_ref[1])


def forward(rows_ref, first_ref, tw_ref, fwd_ref):
    cols = jnp.concatenate([rows_ref[pl.ds(c, NBLK, stride=CH), :] for c in range(CH)], 1)
    top, low = split(cols)
    outer = mm(first_ref[...], jnp.concatenate([top, low, top], 0))
    tw_re, tw_im = tw_ref[0], tw_ref[1]
    out = []
    for c in range(CH):
        lanes = slice(c * BLK, (c + 1) * BLK)
        re, im = outer[:NBLK, lanes], outer[NBLK:, lanes]
        out.append(jnp.concatenate([re * tw_re - im * tw_im, re * tw_im + im * tw_re], 1))
    return mm_split(jnp.concatenate(out, 0), fwd_ref)


def filter_kernel(feat_ref, w_in_ref, w_mid_ref, w_out_ref, taps_ref, rate_ref, skip_ref,
                  first_ref, tw_ref, fwd_ref, spec_ref, par_ref, rows_ref):
    first_chan = lax.axis_index("ctx") * CH
    chans = rate_ref.shape[1]
    pick = (lax.broadcasted_iota(jnp.int32, (CH, chans), 1)
            == lax.broadcasted_iota(jnp.int32, (CH, chans), 0) + first_chan).astype(f32)

    def mine(table):
        return lax.dot_general(pick, table, (((1,), (1,)), ((), ())), precision=highest,
                               preferred_element_type=f32)

    taps = mine(taps_ref[...])
    rate = mine(jnp.broadcast_to(rate_ref[...], (8, chans)))[:, :1]
    skip = mine(jnp.broadcast_to(skip_ref[...], (8, chans)))[:, :1]
    par_ref[...] = jnp.concatenate(
        [taps, skip, jnp.zeros((CH, 128 - 3 * TAPS - 1), f32)], 1)
    out_mine = mine(w_out_ref[...])

    def stack(weights):
        top, low = split(weights)
        return jnp.concatenate([top, top, low], 1)

    per_turn = 1.0 / (2.0 * math.pi)
    w_in = stack(w_in_ref[...] * per_turn)
    w_mid = stack(w_mid_ref[...] * per_turn)
    w_out = stack(out_mine)
    gain = jnp.sqrt(2.0 * rate)
    lane = lax.broadcasted_iota(jnp.int32, (CH, CHUNK), 1).astype(f32)
    for chunk in range(TOKENS // CHUNK):
        one = sine_turns(mm(w_in, feat_ref[:, chunk * CHUNK:(chunk + 1) * CHUNK]))
        top, low = split(one)
        two = sine_turns(mm(w_mid, jnp.concatenate([top, low, top], 0)))
        top, low = split(two)
        shape = mm(w_out, jnp.concatenate([top, low, top], 0))
        taper = gain * jnp.exp(-rate * (lane + float(chunk * CHUNK))) * shape
        for a in range(CHUNK // BLK):
            at = (chunk * (CHUNK // BLK) + a) * CH
            rows_ref[at:at + CH, :] = taper[:, a * BLK:(a + 1) * BLK]
    spec_ref[...] = forward(rows_ref, first_ref, tw_ref, fwd_ref)


def conv_kernel(field_ref, spec_ref, par_ref, first_ref, last_ref, tw_ref, fwd_ref, bwd_ref,
                out_ref, query_ref, prod_ref, conv_ref):
    par = par_ref[...]
    span = 8
    lane = lax.broadcasted_iota(jnp.int32, (span, CH, BLK), 2)
    for start in range(0, NBLK, span):
        if start == 0:
            block = field_ref[0:span].astype(f32)
            block = jnp.concatenate([jnp.zeros_like(block[:1]), block], 0)
        else:
            block = field_ref[start - 1:start + span].astype(f32)
        mixed = []
        for f in range(3):
            field = block[:, f * CH:(f + 1) * CH, :]
            total = par[:, f * TAPS:f * TAPS + 1][None] * field[1:]
            for j in range(1, TAPS):
                turned = pltpu.roll(field, j, 2)
                moved = jnp.where(lane < j, turned[:-1], turned[1:])
                total = total + par[:, f * TAPS + j:f * TAPS + j + 1][None] * moved
            mixed.append(total.astype(bf16).astype(f32).reshape(span * CH, BLK))
        at = slice(start * CH, (start + span) * CH)
        query_ref[at, :] = mixed[0]
        prod_ref[at, :] = mixed[1] * mixed[2]
    spec = forward(prod_ref, first_ref, tw_ref, fwd_ref)
    s_re, s_im = spec[:, :BLK], spec[:, BLK:]
    h_re, h_im = spec_ref[:, :BLK], spec_ref[:, BLK:]
    both = jnp.concatenate([s_re * h_re - s_im * h_im, s_re * h_im + s_im * h_re], 1)
    back = mm_split(both, bwd_ref)
    tw_re, tw_im = tw_ref[0], tw_ref[1]
    cols = []
    for c in range(CH):
        re, im = back[c * NBLK:(c + 1) * NBLK, :BLK], back[c * NBLK:(c + 1) * NBLK, BLK:]
        cols.append(jnp.concatenate([re * tw_re + im * tw_im, im * tw_re - re * tw_im], 0))
    top, low = split(jnp.concatenate(cols, 1))
    conv = mm(last_ref[...], jnp.concatenate([top, low, top], 0))
    for c in range(CH):
        conv_ref[pl.ds(c, NBLK, stride=CH), :] = conv[:, c * BLK:(c + 1) * BLK]
    skip = par[:, 3 * TAPS:3 * TAPS + 1][None]
    prod = prod_ref[...].reshape(NBLK, CH, BLK)
    total = conv_ref[...].reshape(NBLK, CH, BLK) + skip * prod
    gated = query_ref[...].reshape(NBLK, CH, BLK) * total
    out_ref[...] = gated.reshape(NBLK * CH, BLK).astype(bf16)


def per_device(query_field, key_field, value_field, short_taps, filt_in, filt_mid, filt_out,
               decay_rate, skip_gain, out_weight):
    tok, chans = query_field.shape
    groups = lax.axis_size("ch")
    first, last, twiddle, fwd, bwd = (jnp.asarray(t) for t in dft_tables())
    stacked = jnp.stack([query_field, key_field, value_field], 0)
    parts = jnp.transpose(stacked.reshape(3, tok, NBLK, CH), (2, 0, 3, 1)).reshape(NBLK, 3 * CH, tok)
    fields = lax.all_to_all(parts, "ctx", 0, 0, tiled=True)
    w_in = jnp.pad(filt_in.T, ((0, 0), (0, FEAT_PAD - FEAT)))
    params = pltpu.CompilerParams(vmem_limit_bytes=48 * 1024 * 1024)
    spec, par = pl.pallas_call(
        filter_kernel,
        out_shape=(jax.ShapeDtypeStruct((CH * NBLK, 2 * BLK), f32),
                   jax.ShapeDtypeStruct((CH, 128), f32)),
        scratch_shapes=[pltpu.VMEM((NBLK * CH, BLK), f32)],
        compiler_params=params,
        cost_estimate=pl.CostEstimate(flops=2 * 10**9, bytes_accessed=5 * 10**6, transcendentals=10**6),
        name="filter",
    )(jnp.asarray(feature_table()), w_in, filt_mid.T, filt_out, short_taps.reshape(3 * TAPS, chans),
      decay_rate.reshape(1, chans), skip_gain.reshape(1, chans), first, twiddle, fwd)
    gated = pl.pallas_call(
        conv_kernel,
        out_shape=jax.ShapeDtypeStruct((NBLK * CH, BLK), bf16),
        scratch_shapes=[pltpu.VMEM((NBLK * CH, BLK), f32)] * 3,
        compiler_params=params,
        name="convolve",
    )(fields, spec, par, first, last, twiddle, fwd, bwd)
    returned = lax.all_to_all(gated.reshape(NBLK, CH, BLK), "ctx", 0, 0, tiled=True)
    partial = lax.dot_general(returned.reshape(chans, tok), out_weight, (((0,), (0,)), ((), ())),
                              preferred_element_type=f32).astype(bf16)
    shares = lax.all_to_all(partial.reshape(groups, tok // groups, -1), "ch", 0, 0, tiled=True)
    return jnp.sum(shares.astype(f32), 0).astype(bf16)


def solution(mesh):
    return jax.shard_map(
        per_device,
        mesh=mesh,
        in_specs=(
            P("ctx", "ch"),
            P("ctx", "ch"),
            P("ctx", "ch"),
            P(None, None, "ch"),
            P(),
            P(),
            P(None, "ch"),
            P("ch"),
            P("ch"),
            P("ch", None),
        ),
        out_specs=P(("ctx", "ch"), None),
        check_vma=False,
    )
```

```python
import math

import jax
import jax.numpy as jnp
import numpy as np
from jax import lax
from jax.experimental import pallas as pl
from jax.experimental.pallas import tpu as pltpu
from jax.sharding import PartitionSpec as P

TOKENS = 8192
BLK = 128
NBLK = 64
CH = 8
BANDS = 16
FEAT = 33
FEAT_PAD = 48
HALF = 64
SHARE = 16
TAPS = 7
UNITS = 64
CHUNK = 1024
bf16 = jnp.bfloat16
f32 = jnp.float32
highest = lax.Precision.HIGHEST


def split_np(table):
    table = np.asarray(table, np.float32)
    top = table.astype(jnp.bfloat16)
    low = (table - top.astype(np.float32)).astype(jnp.bfloat16)
    return top, low


def feature_table():
    steps = np.arange(TOKENS, dtype=np.int64)
    bands = np.arange(BANDS, dtype=np.int64)
    freq = 1 + bands * bands * (TOKENS // 4 - 1) // ((BANDS - 1) * (BANDS - 1))
    ang = (freq[:, None] * steps[None, :] % TOKENS) * (2.0 * math.pi / TOKENS)
    rows = np.concatenate([(steps / TOKENS)[None, :], np.cos(ang), np.sin(ang)], 0)
    rows = np.concatenate([rows, np.zeros((FEAT_PAD - FEAT, TOKENS))], 0)
    return np.concatenate(split_np(rows), 0)


def token_order(cores):
    at = np.arange(BLK).reshape(BLK // SHARE // cores, cores, SHARE)
    return at.transpose(1, 0, 2).reshape(-1)


def dft_tables(cores):
    shifted = np.arange(NBLK) - 0.25
    block = np.arange(NBLK)
    inner = np.arange(BLK)
    order = token_order(cores)
    outer_ang = 2.0 * math.pi * shifted[:, None] * block[None, :] / NBLK
    first = np.concatenate([np.cos(outer_ang), -np.sin(outer_ang)], 0)
    top, low = split_np(first)
    first_stack = np.concatenate([top, top, low], 1)
    last = np.concatenate([np.cos(outer_ang).T, -np.sin(outer_ang).T], 1) / TOKENS
    top, low = split_np(last)
    last_stack = np.concatenate([top, top, low], 1)
    tw_ang = 2.0 * math.pi * shifted[:, None] * inner[None, :] / TOKENS
    back_ang = tw_ang[:, order]
    twiddle = np.stack([np.cos(tw_ang), -np.sin(tw_ang), np.cos(back_ang), np.sin(back_ang)], 0)
    in_ang = 2.0 * math.pi * (inner[:, None] * inner[None, :] % BLK) / BLK
    cos_in, sin_in = np.cos(in_ang), np.sin(in_ang)
    fwd = np.block([[cos_in, -sin_in], [sin_in, cos_in]])
    cos_back, sin_back = cos_in[:, order], sin_in[:, order]
    bwd = np.block([[cos_back, sin_back], [-sin_back, cos_back]])
    mats = np.stack(split_np(fwd) + split_np(bwd), 0)
    reorder = np.zeros((BLK, BLK), np.float32)
    reorder[order, inner] = 1.0
    return first_stack, last_stack, twiddle.astype(np.float32), mats, reorder.astype(jnp.bfloat16)


def sine_coefs():
    grid = 0.25 * np.cos((np.arange(400) + 0.5) * math.pi / 400)
    grid = np.concatenate([grid, 0.5 * np.cos((np.arange(800) + 0.5) * math.pi / 800)])
    grid = grid[np.abs(grid) > 1e-3]
    powers = np.stack([grid ** (2 * k + 1) for k in range(7)], 1)
    coef, *_ = np.linalg.lstsq(powers, np.sin(2.0 * math.pi * grid), rcond=None)
    return [float(c) for c in coef]


SINE = sine_coefs()


def sine_turns(turns):
    rest = turns - jnp.round(turns)
    sq = rest * rest
    acc = jnp.full_like(sq, SINE[-1])
    for c in SINE[-2::-1]:
        acc = acc * sq + c
    return acc * rest


def split(value):
    top = value.astype(bf16)
    return top, (value - top.astype(f32)).astype(bf16)


def mm(left, right):
    return jnp.dot(left, right, preferred_element_type=f32)


def mm_split(value, top_mat, low_mat):
    top, low = split(value)
    return mm(top, top_mat) + mm(low, top_mat) + mm(top, low_mat)


def lift(rows, low_half):
    return jnp.where(low_half, rows[0], pltpu.roll(rows[1], 4, 1))


def drop(rows, low_half):
    return jnp.where(low_half, pltpu.roll(rows[0], 4, 1), rows[1])


def prep_kernel(query_hbm, key_hbm, value_hbm, out_ref, held, sems):
    copies = [pltpu.make_async_copy(src, held.at[f], sems.at[f])
              for f, src in enumerate((query_hbm, key_hbm, value_hbm))]
    for copy in copies:
        copy.start()
    low_half = lax.broadcasted_iota(jnp.int32, (NBLK // 2, CH, BLK), 1) < 4
    sets = []
    for f in range(3):
        copies[f].wait()
        turned = held[f].astype(f32).T.reshape(2, NBLK // 2, CH, BLK)
        pairs = jnp.stack([lift(turned, low_half), drop(turned, low_half)], 1)
        sets.append(pairs.reshape(NBLK, CH, BLK))
    out_ref[...] = jnp.concatenate(sets, 1).astype(bf16)


def forward(rows_ref, first_ref, tw_ref, mats_ref):
    cols = jnp.concatenate([rows_ref[pl.ds(c, NBLK, stride=CH), :] for c in range(CH)], 1)
    top, low = split(cols)
    outer = mm(first_ref[...], jnp.concatenate([top, low, top], 0))
    tw_re, tw_im = tw_ref[0], tw_ref[1]
    out = []
    for c in range(CH):
        lanes = slice(c * BLK, (c + 1) * BLK)
        re, im = outer[:NBLK, lanes], outer[NBLK:, lanes]
        out.append(jnp.concatenate([re * tw_re - im * tw_im, re * tw_im + im * tw_re], 1))
    return mm_split(jnp.concatenate(out, 0), mats_ref[0], mats_ref[1])


def filter_kernel(feat_hbm, w_in_hbm, w_mid_hbm, w_out_hbm, taps_hbm, rate_hbm, skip_hbm,
                  first_hbm, last_hbm, tw_hbm, mats_hbm, reorder_hbm,
                  spec_ref, par_ref, first_ref, last_ref, tw_ref, mats_ref, reorder_ref,
                  rows_ref, feat_ref, w_in_ref, w_mid_ref, w_out_ref, taps_ref, rate_ref, skip_ref,
                  sems):
    sources = (w_in_hbm, w_mid_hbm, rate_hbm, w_out_hbm, skip_hbm, taps_hbm, feat_hbm,
               first_hbm, tw_hbm, mats_hbm, last_hbm, reorder_hbm)
    targets = (w_in_ref, w_mid_ref, rate_ref, w_out_ref, skip_ref, taps_ref, feat_ref,
               first_ref, tw_ref, mats_ref, last_ref, reorder_ref)
    copies = [pltpu.make_async_copy(src, dst, sems.at[n])
              for n, (src, dst) in enumerate(zip(sources, targets))]
    for copy in copies:
        copy.start()
    chans = rate_ref.shape[1]
    row = lax.broadcasted_iota(jnp.int32, (CH, chans), 0)
    wanted = lax.axis_index("ctx") * 4 + row % 4 + row // 4 * (chans // 2)
    pick = (lax.broadcasted_iota(jnp.int32, (CH, chans), 1) == wanted).astype(f32)

    def mine(table):
        return lax.dot_general(pick, table, (((1,), (1,)), ((), ())), precision=highest,
                               preferred_element_type=f32)

    def stack(weights):
        top, low = split(weights)
        return jnp.concatenate([top, top, low], 1)

    for copy in copies[:7]:
        copy.wait()
    taps = jnp.concatenate([mine(taps_ref[f]) for f in range(3)], 1)
    rate = mine(jnp.broadcast_to(rate_ref[...], (8, chans)))[:, :1]
    skip = mine(jnp.broadcast_to(skip_ref[...], (8, chans)))[:, :1]
    par_ref[...] = jnp.concatenate([taps, jnp.zeros((CH, 128 - 3 * TAPS), f32)], 1)
    per_turn = 1.0 / (2.0 * math.pi)
    padded = jnp.concatenate([w_in_ref[...], jnp.zeros((FEAT_PAD - FEAT, UNITS), f32)], 0)
    w_in = stack(padded.T * per_turn)
    w_mid = stack(w_mid_ref[...].T * per_turn)
    w_out = stack(mine(w_out_ref[...]))
    gain = jnp.sqrt(2.0 * rate)
    lane = lax.broadcasted_iota(jnp.int32, (CH, CHUNK), 1).astype(f32)
    for chunk in range(TOKENS // CHUNK):
        feat = feat_ref[:, chunk * CHUNK:(chunk + 1) * CHUNK]
        one = sine_turns(mm(w_in, jnp.concatenate([feat, feat[:FEAT_PAD]], 0)))
        top, low = split(one)
        two = sine_turns(mm(w_mid, jnp.concatenate([top, low, top], 0)))
        top, low = split(two)
        shape = mm(w_out, jnp.concatenate([top, low, top], 0))
        taper = gain * jnp.exp(-rate * (lane + float(chunk * CHUNK))) * shape
        for a in range(CHUNK // BLK):
            at = (chunk * (CHUNK // BLK) + a) * CH
            rows_ref[at:at + CH, :] = taper[:, a * BLK:(a + 1) * BLK]
    for copy in copies[7:]:
        copy.wait()
    spec = forward(rows_ref, first_ref, tw_ref, mats_ref)
    direct = jnp.concatenate([jnp.broadcast_to(skip[c:c + 1], (NBLK, BLK)) for c in range(CH)], 0)
    spec_ref[:, :BLK] = spec[:, :BLK] + direct
    spec_ref[:, BLK:] = spec[:, BLK:]


def conv_kernel(field_ref, spec_ref, par_ref, first_ref, last_ref, tw_ref, mats_ref, reorder_ref,
                out_ref, query_ref, prod_ref, conv_ref):
    par = par_ref[...]
    span = 8
    lane = lax.broadcasted_iota(jnp.int32, (span, CH, BLK), 2)
    for start in range(0, NBLK, span):
        if start == 0:
            block = field_ref[0:span].astype(f32)
            block = jnp.concatenate([jnp.zeros_like(block[:1]), block], 0)
        else:
            block = field_ref[start - 1:start + span].astype(f32)
        mixed = []
        for f in range(3):
            field = block[:, f * CH:(f + 1) * CH, :]
            total = par[:, f * TAPS:f * TAPS + 1][None] * field[1:]
            for j in range(1, TAPS):
                turned = pltpu.roll(field, j, 2)
                moved = jnp.where(lane < j, turned[:-1], turned[1:])
                total = total + par[:, f * TAPS + j:f * TAPS + j + 1][None] * moved
            mixed.append(total.astype(bf16).reshape(span * CH, BLK))
        at = slice(start * CH, (start + span) * CH)
        prod_ref[at, :] = mixed[1].astype(f32) * mixed[2].astype(f32)
        query_ref[at, :] = mm(mixed[0], reorder_ref[...])
    spec = forward(prod_ref, first_ref, tw_ref, mats_ref)
    s_re, s_im = spec[:, :BLK], spec[:, BLK:]
    h_re, h_im = spec_ref[:, :BLK], spec_ref[:, BLK:]
    both = jnp.concatenate([s_re * h_re - s_im * h_im, s_re * h_im + s_im * h_re], 1)
    back = mm_split(both, mats_ref[2], mats_ref[3])
    tw_re, tw_im = tw_ref[2], tw_ref[3]
    cols = []
    for c in range(CH):
        re, im = back[c * NBLK:(c + 1) * NBLK, :BLK], back[c * NBLK:(c + 1) * NBLK, BLK:]
        cols.append(jnp.concatenate([re * tw_re - im * tw_im, im * tw_re + re * tw_im], 0))
    top, low = split(jnp.concatenate(cols, 1))
    conv = mm(last_ref[...], jnp.concatenate([top, low, top], 0))
    for c in range(CH):
        conv_ref[pl.ds(c, NBLK, stride=CH), :] = conv[:, c * BLK:(c + 1) * BLK]
    gated = (query_ref[...] * conv_ref[...]).reshape(NBLK, CH, BLK)
    sub = lax.broadcasted_iota(jnp.int32, (NBLK, CH, BLK), 1) < 4
    left = lax.broadcasted_iota(jnp.int32, (NBLK, CH, BLK), 2) < HALF
    crossed = pltpu.roll(pltpu.roll(gated, 4, 1), HALF, 2)
    sorted_rows = jnp.where(sub == left, gated, crossed).reshape(NBLK // 2, 2, CH, BLK)
    pairs = (sorted_rows[:, 0], sorted_rows[:, 1])
    half = sub[:NBLK // 2]
    both = jnp.concatenate([lift(pairs, half), drop(pairs, half)], 0)
    out_ref[...] = both.reshape(NBLK * CH, BLK).astype(bf16)


def project_kernel(rows_ref, own_ref, other_ref, out_ref):
    core = lax.axis_index("ch") % 2
    depth = rows_ref.shape[0] // 2
    total = None
    for weight_ref, part in ((own_ref, core), (other_ref, 1 - core)):
        rows = rows_ref[pl.ds(pl.multiple_of(part * depth, depth), depth), :]
        turned = rows.astype(f32).T.astype(bf16)
        for half in range(2):
            term = mm(turned[half * HALF:(half + 1) * HALF], weight_ref[half * depth:(half + 1) * depth, :])
            total = term if total is None else total + term
    out_ref[...] = total.astype(bf16)


def per_device(query_field, key_field, value_field, short_taps, filt_in, filt_mid, filt_out,
               decay_rate, skip_gain, out_weight):
    chans = query_field.shape[1]
    cores = 2
    groups = lax.axis_size("ch")
    chips = groups // cores
    dout = out_weight.shape[1]
    first, last, twiddle, mats, reorder = (jnp.asarray(t) for t in dft_tables(cores))
    params = pltpu.CompilerParams(vmem_limit_bytes=48 * 1024 * 1024)
    far = pl.BlockSpec(memory_space=pltpu.HBM)
    parts = pl.pallas_call(
        prep_kernel,
        out_shape=jax.ShapeDtypeStruct((NBLK, 3 * CH, BLK), bf16),
        in_specs=[far] * 3,
        scratch_shapes=[pltpu.VMEM((3,) + query_field.shape, bf16), pltpu.SemaphoreType.DMA((3,))],
        compiler_params=params,
        name="prep",
    )(query_field, key_field, value_field)
    fields = lax.all_to_all(parts, "ctx", 0, 0, tiled=True)
    sources = (jnp.asarray(feature_table()), filt_in, filt_mid, filt_out, short_taps,
               decay_rate.reshape(1, chans), skip_gain.reshape(1, chans),
               first, last, twiddle, mats, reorder)
    passed = [jax.ShapeDtypeStruct(t.shape, t.dtype) for t in sources[7:]]
    spec, par, *tables = pl.pallas_call(
        filter_kernel,
        out_shape=[jax.ShapeDtypeStruct((CH * NBLK, 2 * BLK), f32),
                   jax.ShapeDtypeStruct((CH, 128), f32)] + passed,
        in_specs=[far] * len(sources),
        scratch_shapes=[pltpu.VMEM((NBLK * CH, BLK), f32)]
        + [pltpu.VMEM(t.shape, t.dtype) for t in sources[:7]]
        + [pltpu.SemaphoreType.DMA((len(sources),))],
        compiler_params=params,
        cost_estimate=pl.CostEstimate(flops=2 * 10**9, bytes_accessed=5 * 10**6, transcendentals=10**6),
        name="filter",
    )(*sources)
    own_weight, par = lax.optimization_barrier((out_weight, par))
    other_weight = lax.ppermute(own_weight, "ch", [(d, d ^ 1) for d in range(groups)])
    gated = pl.pallas_call(
        conv_kernel,
        out_shape=jax.ShapeDtypeStruct((NBLK * CH, BLK), bf16),
        scratch_shapes=[pltpu.VMEM((NBLK * CH, BLK), f32)] * 3,
        compiler_params=params,
        name="convolve",
    )(fields, spec, par, *tables)
    on_chip = [[c * groups + x * cores + k for k in range(cores) for c in range(NBLK)] for x in range(chips)]
    returned = lax.all_to_all(gated.reshape(NBLK * cores, CH // cores, BLK), ("ctx", "ch"), 0, 0,
                              tiled=True, axis_index_groups=on_chip)
    partial = pl.pallas_call(
        project_kernel,
        out_shape=jax.ShapeDtypeStruct((BLK // cores, dout), bf16),
        compiler_params=params,
        name="project",
    )(returned.reshape(NBLK * CH, BLK), own_weight, other_weight)
    along_x = [[x * cores + k for x in range(chips)] for k in range(cores)]
    shares = lax.all_to_all(partial.reshape(chips, SHARE, dout), "ch", 0, 0, tiled=True,
                            axis_index_groups=along_x)
    return jnp.sum(shares.astype(f32), 0).astype(bf16)


def solution(mesh):
    return jax.shard_map(
        per_device,
        mesh=mesh,
        in_specs=(
            P("ctx", "ch"),
            P("ctx", "ch"),
            P("ctx", "ch"),
            P(None, None, "ch"),
            P(),
            P(),
            P(None, "ch"),
            P("ch"),
            P("ch"),
            P("ch", None),
        ),
        out_specs=P(("ctx", "ch"), None),
        check_vma=False,
    )
```

```python
import math

import jax
import jax.numpy as jnp
import numpy as np
from jax import lax
from jax.experimental import pallas as pl
from jax.experimental.pallas import tpu as pltpu
from jax.sharding import PartitionSpec as P

TOKENS = 8192
BLK = 128
NBLK = 64
CH = 8
BANDS = 16
FEAT = 33
FEAT_PAD = 48
TAPS = 7
UNITS = 64
CHUNK = 2048
STEP = 27
BACK = 19
PACK = (0, 64, 88, 96, 104, 168)
PACK_ROWS = 208
bf16 = jnp.bfloat16
f32 = jnp.float32
highest = lax.Precision.HIGHEST


def first_order():
    return [STEP * n % NBLK for n in range(NBLK)]


def second_place(ctx):
    return BACK * ctx % NBLK


def sine_coefs():
    grid = 0.25 * np.cos((np.arange(400) + 0.5) * math.pi / 400)
    grid = np.concatenate([grid, 0.5 * np.cos((np.arange(800) + 0.5) * math.pi / 800)])
    grid = grid[np.abs(grid) > 1e-3]
    powers = np.stack([grid ** (2 * k + 1) for k in range(7)], 1)
    coef, *_ = np.linalg.lstsq(powers, np.sin(2.0 * math.pi * grid), rcond=None)
    return [float(c) for c in coef]


SINE = sine_coefs()
NEAREST = 1.5 * 2.0**23


def sine_turns(turns):
    rest = turns - ((turns + NEAREST) - NEAREST)
    sq = rest * rest
    acc = sq * SINE[-1] + SINE[-2]
    for c in SINE[-3::-1]:
        acc = acc * sq + c
    return acc * rest


def split(value):
    top = value.astype(bf16)
    return top, (value - top.astype(f32)).astype(bf16)


def mm(left, right):
    return jnp.dot(left, right, preferred_element_type=f32)


def mm_split(value, top_mat, low_mat):
    top, low = split(value)
    return mm(top, top_mat) + mm(low, top_mat) + mm(top, low_mat)


def prep_kernel(query_hbm, key_hbm, value_hbm, w_in_hbm, w_mid_hbm, w_out_hbm, taps_hbm, rate_hbm,
                skip_hbm, out_ref, pack_ref, held, w_in_ref, w_mid_ref, w_out_ref, taps_ref, rate_ref,
                skip_ref, sems):
    sources = (query_hbm, key_hbm, value_hbm, w_out_hbm, taps_hbm, w_mid_hbm, w_in_hbm, rate_hbm, skip_hbm)
    targets = (held.at[0], held.at[1], held.at[2], w_out_ref, taps_ref, w_mid_ref, w_in_ref, rate_ref, skip_ref)
    copies = [pltpu.make_async_copy(src, dst, sems.at[n])
              for n, (src, dst) in enumerate(zip(sources, targets))]
    for copy in copies:
        copy.start()
    sets = []
    for f in range(3):
        copies[f].wait()
        sets.append(held[f].astype(f32).T)
    for slot, ctx in enumerate(first_order()):
        place = second_place(ctx)
        rows = slice(place * CH, (place + 1) * CH)
        out_ref[slot] = jnp.concatenate([turned[rows] for turned in sets], 0).astype(bf16)
    for copy in copies[3:]:
        copy.wait()
    chans = rate_ref.shape[1]
    at_out, at_taps, at_rate, at_skip, at_mid, at_in = PACK
    pack_ref[at_out:at_out + UNITS, :] = w_out_ref[...]
    for f in range(3):
        pack_ref[at_taps + f * 8:at_taps + f * 8 + TAPS, :] = taps_ref[f]
    pack_ref[at_rate:at_rate + 8, :] = jnp.broadcast_to(rate_ref[...], (8, chans))
    pack_ref[at_skip:at_skip + 8, :] = jnp.broadcast_to(skip_ref[...], (8, chans))
    pack_ref[at_mid:at_mid + UNITS, 0:UNITS] = w_mid_ref[...]
    pack_ref[at_in:at_in + FEAT, 0:UNITS] = w_in_ref[...]


def forward(rows_ref, first_ref, tw_ref, mats_ref):
    cols = jnp.concatenate([rows_ref[pl.ds(c, NBLK, stride=CH), :] for c in range(CH)], 1)
    top, low = split(cols)
    outer = mm(first_ref[...], jnp.concatenate([top, low, top], 0))
    tw_re, tw_im = tw_ref[0][...], tw_ref[1][...]
    out = []
    for c in range(CH):
        lanes = slice(c * BLK, (c + 1) * BLK)
        re, im = outer[:NBLK, lanes], outer[NBLK:, lanes]
        out.append(jnp.concatenate([re * tw_re - im * tw_im, re * tw_im + im * tw_re], 1))
    return mm_split(jnp.concatenate(out, 0), mats_ref[0][...], mats_ref[1][...])


def views(wide_ref, table_ref):
    half = 2 * BLK
    spec = wide_ref.at[0:CH * NBLK]
    tw = [wide_ref.at[CH * NBLK:CH * NBLK + NBLK, n * BLK:(n + 1) * BLK] for n in range(2)]
    par = wide_ref.at[CH * NBLK + NBLK:CH * NBLK + NBLK + CH, 0:BLK]
    mats = [table_ref.at[n * half:(n + 1) * half] for n in range(4)]
    first = table_ref.at[4 * half:4 * half + BLK, 0:3 * NBLK]
    last = [table_ref.at[4 * half + BLK + n * NBLK:4 * half + BLK + (n + 1) * NBLK, 0:3 * NBLK]
            for n in range(2)]
    return spec, tw, par, mats, first, last


def fill_tables(first_ref, last_ref, tw_ref, mats_ref):
    def grid(shape, axis):
        return lax.broadcasted_iota(jnp.int32, shape, axis)

    def wave(turns):
        turns = turns - jnp.round(turns)
        return sine_turns(turns + 0.25), sine_turns(turns)

    shape = (NBLK, NBLK)
    cos, sin = wave((grid(shape, 0).astype(f32) - 0.25) * grid(shape, 1).astype(f32) / NBLK)
    top, low = split(jnp.concatenate([cos, -sin], 0))
    first_ref[...] = jnp.concatenate([top, top, low], 1)
    cos, sin = wave((grid(shape, 1).astype(f32) - 0.25) * grid(shape, 0).astype(f32) / NBLK)
    top, low = split(jnp.concatenate([cos, -sin], 1) / TOKENS)
    wide = jnp.concatenate([top, top, low], 1)
    last_ref[0][...], last_ref[1][...] = wide[:, :3 * NBLK], wide[:, 3 * NBLK:]
    shape = (NBLK, BLK)
    shifted = grid(shape, 0).astype(f32) - 0.25
    cos, sin = wave(shifted * grid(shape, 1).astype(f32) / TOKENS)
    tw_ref[0][...], tw_ref[1][...] = cos, -sin
    shape = (BLK, BLK)
    cos, sin = wave((grid(shape, 0) * grid(shape, 1)).astype(f32) / BLK)
    mats = jnp.concatenate([jnp.concatenate([cos, -sin], 1), jnp.concatenate([sin, cos], 1)], 0)
    mats_ref[0][...], mats_ref[1][...] = split(mats)
    mats = jnp.concatenate([jnp.concatenate([cos, sin], 1), jnp.concatenate([-sin, cos], 1)], 0)
    mats_ref[2][...], mats_ref[3][...] = split(mats)


def filter_kernel(pack_ref, wide_ref, table_ref, rows_ref):
    at_out, at_taps, at_rate, at_skip, at_mid, at_in = PACK
    spec_ref, tw_ref, par_ref, mats_ref, first_ref, last_ref = views(wide_ref, table_ref)
    fill_tables(first_ref, last_ref, tw_ref, mats_ref)
    chans = pack_ref.shape[1]
    wanted = second_place(lax.axis_index("ctx")) * CH + lax.broadcasted_iota(jnp.int32, (CH, chans), 0)
    pick = (lax.broadcasted_iota(jnp.int32, (CH, chans), 1) == wanted).astype(f32)

    def mine(table):
        return lax.dot_general(pick, table, (((1,), (1,)), ((), ())), precision=highest,
                               preferred_element_type=f32)

    def stack(weights):
        top, low = split(weights)
        return jnp.concatenate([top, top, low], 1)

    taps = jnp.concatenate([mine(pack_ref[at_taps + f * 8:at_taps + (f + 1) * 8, :])[:, :TAPS]
                            for f in range(3)], 1)
    rate = mine(pack_ref[at_rate:at_rate + 8, :])[:, :1]
    skip = mine(pack_ref[at_skip:at_skip + 8, :])[:, :1]
    par_ref[...] = jnp.concatenate([taps, jnp.zeros((CH, 128 - 3 * TAPS), f32)], 1)
    per_turn = 1.0 / (2.0 * math.pi)
    padded = jnp.concatenate([pack_ref[at_in + 1:at_in + FEAT, 0:UNITS], pack_ref[at_in:at_in + 1, 0:UNITS],
                              jnp.zeros((FEAT_PAD - FEAT, UNITS), f32)], 0)
    w_in = stack(padded.T * per_turn)
    w_mid = stack(pack_ref[at_mid:at_mid + UNITS, 0:UNITS].T * per_turn)
    w_out = stack(mine(pack_ref[at_out:at_out + UNITS, :]))
    gain = jnp.sqrt(2.0 * rate)

    band = lax.broadcasted_iota(jnp.int32, (BANDS, BLK), 0).astype(f32)
    at = lax.broadcasted_iota(jnp.int32, (BANDS, BLK), 1).astype(f32)
    span = float((BANDS - 1) * (BANDS - 1))
    freq = 1.0 + jnp.floor((band * band * (TOKENS // 4 - 1) + 0.5) * (1.0 / span))
    inner = freq * at * (1.0 / TOKENS)
    inner = inner - jnp.round(inner)
    inner_cos, inner_sin = sine_turns(inner + 0.25), sine_turns(inner)
    outer = freq * at * (1.0 / NBLK)
    outer = outer - jnp.round(outer)
    outer_cos, outer_sin = sine_turns(outer + 0.25), sine_turns(outer)
    ramp_row = lax.broadcasted_iota(jnp.int32, (FEAT_PAD - 2 * BANDS, BLK), 0) == 0
    ramp_at = lax.broadcasted_iota(jnp.int32, (FEAT_PAD - 2 * BANDS, BLK), 1).astype(f32)

    def features(a):
        turn_cos, turn_sin = outer_cos[:, a:a + 1], outer_sin[:, a:a + 1]
        ramp = jnp.where(ramp_row, (ramp_at + float(a * BLK)) * (1.0 / TOKENS), 0.0)
        return jnp.concatenate([inner_cos * turn_cos - inner_sin * turn_sin,
                                inner_sin * turn_cos + inner_cos * turn_sin, ramp], 0)

    lane = lax.broadcasted_iota(jnp.int32, (CH, CHUNK), 1).astype(f32)
    per_chunk = CHUNK // BLK
    for chunk in range(TOKENS // CHUNK):
        feat = jnp.concatenate([features(chunk * per_chunk + n) for n in range(per_chunk)], 1)
        top, low = split(feat)
        one = sine_turns(mm(w_in, jnp.concatenate([top, low, top], 0)))
        top, low = split(one)
        two = sine_turns(mm(w_mid, jnp.concatenate([top, low, top], 0)))
        top, low = split(two)
        shape = mm(w_out, jnp.concatenate([top, low, top], 0))
        taper = gain * jnp.exp(-rate * (lane + float(chunk * CHUNK))) * shape
        for n in range(per_chunk):
            first_row = (chunk * per_chunk + n) * CH
            rows_ref[first_row:first_row + CH, :] = taper[:, n * BLK:(n + 1) * BLK]
    spec = forward(rows_ref, first_ref, tw_ref, mats_ref)
    direct = jnp.concatenate([jnp.broadcast_to(skip[c:c + 1], (NBLK, BLK)) for c in range(CH)], 0)
    spec_ref[:, :BLK] = spec[:, :BLK] + direct
    spec_ref[:, BLK:] = spec[:, BLK:]


def conv_kernel(field_ref, wide_ref, table_ref, out_ref, query_ref, prod_ref, conv_ref):
    spec_ref, tw_ref, par_ref, mats_ref, first_ref, last_ref = views(wide_ref, table_ref)
    par = par_ref[...]
    taps = [jnp.broadcast_to(par[:, n:n + 1], (CH, BLK))[None] for n in range(3 * TAPS)]
    span = 8
    lane = lax.broadcasted_iota(jnp.int32, (span + 1, CH, BLK), 2)

    def later(value, steps):
        turned = pltpu.roll(value, steps, 2)
        return jnp.where(lane < steps, jnp.concatenate([turned[:1], turned[:-1]], 0), turned)

    for start in range(0, NBLK, span):
        block = [field_ref[BACK * n % NBLK].astype(f32) for n in range(max(start - 1, 0), start + span)]
        if start == 0:
            block = [jnp.zeros_like(block[0])] + block
        block = jnp.stack(block, 0)
        mixed = []
        for f in range(3):
            now = block[:, f * CH:(f + 1) * CH, :]
            past = later(now, 1)
            t = taps[f * TAPS:(f + 1) * TAPS]
            total = later(t[6] * now, 2) + (t[4] * now + t[5] * past)
            total = later(total, 2) + (t[2] * now + t[3] * past)
            total = later(total, 2) + (t[0] * now + t[1] * past)
            mixed.append(total[1:].astype(bf16).reshape(span * CH, BLK))
        at = slice(start * CH, (start + span) * CH)
        prod_ref[at, :] = mixed[1].astype(f32) * mixed[2].astype(f32)
        query_ref[at, :] = mixed[0].astype(f32)
    spec = forward(prod_ref, first_ref, tw_ref, mats_ref)
    s_re, s_im = spec[:, :BLK], spec[:, BLK:]
    h_re, h_im = spec_ref[:, :BLK], spec_ref[:, BLK:]
    both = jnp.concatenate([s_re * h_re - s_im * h_im, s_re * h_im + s_im * h_re], 1)
    back = mm_split(both, mats_ref[2][...], mats_ref[3][...])
    tw_re, tw_im = tw_ref[0][...], tw_ref[1][...]
    cols = []
    for c in range(CH):
        re, im = back[c * NBLK:(c + 1) * NBLK, :BLK], back[c * NBLK:(c + 1) * NBLK, BLK:]
        cols.append(jnp.concatenate([re * tw_re + im * tw_im, im * tw_re - re * tw_im], 0))
    top, low = split(jnp.concatenate(cols, 1))
    last = jnp.concatenate([last_ref[0][...], last_ref[1][...]], 1)
    conv = mm(last, jnp.concatenate([top, low, top], 0))
    for c in range(CH):
        conv_ref[pl.ds(c, NBLK, stride=CH), :] = conv[:, c * BLK:(c + 1) * BLK]
    order = first_order()
    for slot in range(0, NBLK, 2):
        gated = []
        for ctx in order[slot:slot + 2]:
            rows = slice(ctx * CH, (ctx + 1) * CH)
            gated.append(query_ref[rows, :] * conv_ref[rows, :])
        out_ref[slot * CH:(slot + 2) * CH, :] = jnp.concatenate(gated, 0).astype(bf16)


def per_device(query_field, key_field, value_field, short_taps, filt_in, filt_mid, filt_out,
               decay_rate, skip_gain, out_weight):
    chans = query_field.shape[1]
    groups = lax.axis_size("ch")
    params = pltpu.CompilerParams(vmem_limit_bytes=32 * 1024 * 1024)
    far = pl.BlockSpec(memory_space=pltpu.HBM)
    operands = (query_field, key_field, value_field, filt_in, filt_mid, filt_out, short_taps,
                decay_rate.reshape(1, chans), skip_gain.reshape(1, chans))
    parts, pack = pl.pallas_call(
        prep_kernel,
        out_shape=[jax.ShapeDtypeStruct((NBLK, 3 * CH, BLK), bf16),
                   jax.ShapeDtypeStruct((PACK_ROWS, chans), f32)],
        in_specs=[far] * len(operands),
        scratch_shapes=[pltpu.VMEM((3,) + query_field.shape, bf16)]
        + [pltpu.VMEM(t.shape, t.dtype) for t in operands[3:]]
        + [pltpu.SemaphoreType.DMA((len(operands),))],
        compiler_params=pltpu.CompilerParams(vmem_limit_bytes=62 * 1024 * 1024),
        name="prep",
    )(*operands)
    fields = lax.all_to_all(parts, "ctx", 0, 0, tiled=True, axis_index_groups=[first_order()])
    wide, table = pl.pallas_call(
        filter_kernel,
        out_shape=[jax.ShapeDtypeStruct((CH * NBLK + NBLK + CH, 2 * BLK), f32),
                   jax.ShapeDtypeStruct((8 * BLK + 2 * BLK, 2 * BLK), bf16)],
        scratch_shapes=[pltpu.VMEM((NBLK * CH, BLK), f32)],
        compiler_params=params,
        cost_estimate=pl.CostEstimate(flops=2 * 10**9, bytes_accessed=5 * 10**6, transcendentals=10**6),
        name="filter",
    )(pack)
    gated = pl.pallas_call(
        conv_kernel,
        out_shape=jax.ShapeDtypeStruct((NBLK * CH, BLK), bf16),
        scratch_shapes=[pltpu.VMEM((NBLK * CH, BLK), f32)] * 3,
        compiler_params=params,
        cost_estimate=pl.CostEstimate(flops=10**11, bytes_accessed=10**9, transcendentals=0),
        name="convolve",
    )(fields, wide, table)
    returned = lax.all_to_all(gated.reshape(NBLK, CH, BLK), "ctx", 0, 0, tiled=True,
                              axis_index_groups=[first_order()])
    partial = lax.dot_general(returned.reshape(chans, BLK), out_weight, (((0,), (0,)), ((), ())),
                              preferred_element_type=f32).astype(bf16)
    shares = lax.all_to_all(partial.reshape(groups, BLK // groups, -1), "ch", 0, 0, tiled=True,
                            axis_index_groups=None)
    return jnp.sum(shares.astype(f32), 0).astype(bf16)


def solution(mesh):
    return jax.shard_map(
        per_device,
        mesh=mesh,
        in_specs=(
            P("ctx", "ch"),
            P("ctx", "ch"),
            P("ctx", "ch"),
            P(None, None, "ch"),
            P(),
            P(),
            P(None, "ch"),
            P("ch"),
            P("ch"),
            P("ch", None),
        ),
        out_specs=P(("ctx", "ch"), None),
        check_vma=False,
    )
```

```python
import math

import jax
import jax.numpy as jnp
import numpy as np
from jax import lax
from jax.experimental import pallas as pl
from jax.experimental.pallas import tpu as pltpu
from jax.sharding import PartitionSpec as P

TOKENS = 8192
BLK = 128
NBLK = 64
CH = 8
BANDS = 16
FEAT = 33
FEAT_PAD = 48
HALF = 64
SHARE = 16
TAPS = 7
UNITS = 64
CHUNK = 2048
STEP = 27
BACK = 19
PACK = (0, 64, 88, 96, 104, 168)
PACK_ROWS = 208
bf16 = jnp.bfloat16
f32 = jnp.float32
highest = lax.Precision.HIGHEST


def first_order():
    return [STEP * n % NBLK for n in range(NBLK)]


def second_order():
    order = []
    for n in range(NBLK):
        turned = int(format(n, "06b")[::-1], 2)
        order.append(turned % 8 * 8 + turned // 8)
    return order


def second_place(ctx):
    return sum((ctx // 2 ** src % 2) * 2 ** dst for src, dst in enumerate((2, 1, 0, 5, 4, 3)))


def sine_coefs():
    grid = 0.25 * np.cos((np.arange(400) + 0.5) * math.pi / 400)
    grid = np.concatenate([grid, 0.5 * np.cos((np.arange(800) + 0.5) * math.pi / 800)])
    grid = grid[np.abs(grid) > 1e-3]
    powers = np.stack([grid ** (2 * k + 1) for k in range(7)], 1)
    coef, *_ = np.linalg.lstsq(powers, np.sin(2.0 * math.pi * grid), rcond=None)
    return [float(c) for c in coef]


SINE = sine_coefs()
NEAREST = 1.5 * 2.0**23


def sine_turns(turns):
    rest = turns - ((turns + NEAREST) - NEAREST)
    sq = rest * rest
    acc = sq * SINE[-1] + SINE[-2]
    for c in SINE[-3::-1]:
        acc = acc * sq + c
    return acc * rest


def split(value):
    top = value.astype(bf16)
    return top, (value - top.astype(f32)).astype(bf16)


def mm(left, right):
    return jnp.dot(left, right, preferred_element_type=f32)


def mm_split(value, top_mat, low_mat):
    top, low = split(value)
    return mm(top, top_mat) + mm(low, top_mat) + mm(top, low_mat)


def lift(rows, low_half):
    return jnp.where(low_half, rows[0], pltpu.roll(rows[1], 4, 1))


def drop(rows, low_half):
    return jnp.where(low_half, pltpu.roll(rows[0], 4, 1), rows[1])


def prep_kernel(query_hbm, key_hbm, value_hbm, w_in_hbm, w_mid_hbm, w_out_hbm, taps_hbm, rate_hbm,
                skip_hbm, out_ref, pack_ref, held, w_in_ref, w_mid_ref, w_out_ref, taps_ref, rate_ref,
                skip_ref, sems):
    sources = (query_hbm, key_hbm, value_hbm, w_out_hbm, taps_hbm, w_mid_hbm, w_in_hbm, rate_hbm, skip_hbm)
    targets = (held.at[0], held.at[1], held.at[2], w_out_ref, taps_ref, w_mid_ref, w_in_ref, rate_ref, skip_ref)
    copies = [pltpu.make_async_copy(src, dst, sems.at[n])
              for n, (src, dst) in enumerate(zip(sources, targets))]
    for copy in copies:
        copy.start()
    low_half = lax.broadcasted_iota(jnp.int32, (NBLK // 2, CH, BLK), 1) < 4
    sets = []
    for f in range(3):
        copies[f].wait()
        turned = held[f].astype(f32).T.reshape(2, NBLK // 2, CH, BLK)
        sets.append((lift(turned, low_half), drop(turned, low_half)))
    for slot, ctx in enumerate(first_order()):
        place = second_place(ctx)
        out_ref[slot] = jnp.concatenate([pair[place % 2][place // 2] for pair in sets], 0).astype(bf16)
    for copy in copies[3:]:
        copy.wait()
    chans = rate_ref.shape[1]
    at_out, at_taps, at_rate, at_skip, at_mid, at_in = PACK
    pack_ref[at_out:at_out + UNITS, :] = w_out_ref[...]
    for f in range(3):
        pack_ref[at_taps + f * 8:at_taps + f * 8 + TAPS, :] = taps_ref[f]
    pack_ref[at_rate:at_rate + 8, :] = jnp.broadcast_to(rate_ref[...], (8, chans))
    pack_ref[at_skip:at_skip + 8, :] = jnp.broadcast_to(skip_ref[...], (8, chans))
    pack_ref[at_mid:at_mid + UNITS, 0:UNITS] = w_mid_ref[...]
    pack_ref[at_in:at_in + FEAT, 0:UNITS] = w_in_ref[...]


def forward(rows_ref, first_ref, tw_ref, mats_ref):
    cols = jnp.concatenate([rows_ref[pl.ds(c, NBLK, stride=CH), :] for c in range(CH)], 1)
    top, low = split(cols)
    outer = mm(first_ref[...], jnp.concatenate([top, low, top], 0))
    tw_re, tw_im = tw_ref[0][...], tw_ref[1][...]
    out = []
    for c in range(CH):
        lanes = slice(c * BLK, (c + 1) * BLK)
        re, im = outer[:NBLK, lanes], outer[NBLK:, lanes]
        out.append(jnp.concatenate([re * tw_re - im * tw_im, re * tw_im + im * tw_re], 1))
    return mm_split(jnp.concatenate(out, 0), mats_ref[0][...], mats_ref[1][...])


def views(wide_ref, table_ref):
    half = 2 * BLK
    spec = wide_ref.at[0:CH * NBLK]
    tw = [wide_ref.at[CH * NBLK:CH * NBLK + NBLK, n * BLK:(n + 1) * BLK] for n in range(2)]
    par = wide_ref.at[CH * NBLK + NBLK:CH * NBLK + NBLK + CH, 0:BLK]
    mats = [table_ref.at[n * half:(n + 1) * half] for n in range(2)]
    first = table_ref.at[2 * half:2 * half + BLK, 0:3 * NBLK]
    last = [table_ref.at[2 * half + BLK + n * NBLK:2 * half + BLK + (n + 1) * NBLK, 0:3 * NBLK]
            for n in range(2)]
    return spec, tw, par, mats, first, last


def fill_tables(first_ref, last_ref, tw_ref, mats_ref):
    def grid(shape, axis):
        return lax.broadcasted_iota(jnp.int32, shape, axis)

    def wave(turns):
        turns = turns - jnp.round(turns)
        return sine_turns(turns + 0.25), sine_turns(turns)

    shape = (NBLK, NBLK)
    cos, sin = wave((grid(shape, 0).astype(f32) - 0.25) * grid(shape, 1).astype(f32) / NBLK)
    top, low = split(jnp.concatenate([cos, -sin], 0))
    first_ref[...] = jnp.concatenate([top, top, low], 1)
    cos, sin = wave((grid(shape, 1).astype(f32) - 0.25) * grid(shape, 0).astype(f32) / NBLK)
    top, low = split(jnp.concatenate([cos, -sin], 1) / TOKENS)
    wide = jnp.concatenate([top, top, low], 1)
    last_ref[0][...], last_ref[1][...] = wide[:, :3 * NBLK], wide[:, 3 * NBLK:]
    shape = (NBLK, BLK)
    shifted = grid(shape, 0).astype(f32) - 0.25
    cos, sin = wave(shifted * grid(shape, 1).astype(f32) / TOKENS)
    tw_ref[0][...], tw_ref[1][...] = cos, -sin
    shape = (BLK, BLK)
    cos, sin = wave((grid(shape, 0) * grid(shape, 1)).astype(f32) / BLK)
    mats = jnp.concatenate([jnp.concatenate([cos, -sin], 1), jnp.concatenate([sin, cos], 1)], 0)
    mats_ref[0][...], mats_ref[1][...] = split(mats)


def weights_kernel(pack_ref, small_ref, stack_ref):
    at_out, at_taps, at_rate, at_skip, at_mid, at_in = PACK
    chans = pack_ref.shape[1]
    row = lax.broadcasted_iota(jnp.int32, (CH, chans), 0)
    wanted = second_place(lax.axis_index("ctx")) * 4 + row % 4 + row // 4 * (chans // 2)
    pick = (lax.broadcasted_iota(jnp.int32, (CH, chans), 1) == wanted).astype(f32)

    def stack(weights):
        top, low = split(weights)
        return jnp.concatenate([top, top, low], 1)

    mine = lax.dot_general(pick, pack_ref[:at_mid, :], (((1,), (1,)), ((), ())), precision=highest,
                           preferred_element_type=f32)
    per_turn = 1.0 / (2.0 * math.pi)
    padded = jnp.concatenate([pack_ref[at_in + 1:at_in + FEAT, 0:UNITS], pack_ref[at_in:at_in + 1, 0:UNITS],
                              jnp.zeros((FEAT_PAD - FEAT, UNITS), f32)], 0)
    small_ref[:, 0:at_mid] = mine
    stack_ref[0:UNITS, 0:3 * FEAT_PAD] = stack(padded.T * per_turn)
    stack_ref[UNITS:2 * UNITS, 0:3 * UNITS] = stack(pack_ref[at_mid:at_mid + UNITS, 0:UNITS].T * per_turn)
    wide = stack(mine[:, at_out:at_out + UNITS])
    stack_ref[2 * UNITS:2 * UNITS + 2 * CH, 0:3 * UNITS] = jnp.concatenate([wide, wide], 0)


def filter_kernel(small_ref, stack_ref, wide_ref, table_ref, rows_ref):
    at_out, at_taps, at_rate, at_skip, at_mid, at_in = PACK
    spec_ref, tw_ref, par_ref, mats_ref, first_ref, last_ref = views(wide_ref, table_ref)
    fill_tables(first_ref, last_ref, tw_ref, mats_ref)
    w_in = stack_ref[0:UNITS, 0:3 * FEAT_PAD]
    w_mid = stack_ref[UNITS:2 * UNITS, 0:3 * UNITS]
    w_out = stack_ref[2 * UNITS:2 * UNITS + 2 * CH, 0:3 * UNITS]
    taps = [small_ref[:, at_taps + f * 8:at_taps + f * 8 + TAPS] for f in range(3)]
    rate = small_ref[:, at_rate:at_rate + 1]
    skip = small_ref[:, at_skip:at_skip + 1]
    par_ref[...] = jnp.concatenate(taps + [jnp.zeros((CH, 128 - 3 * TAPS), f32)], 1)
    gain = jnp.sqrt(2.0 * rate)

    band = lax.broadcasted_iota(jnp.int32, (BANDS, BLK), 0).astype(f32)
    at = lax.broadcasted_iota(jnp.int32, (BANDS, BLK), 1).astype(f32)
    span = float((BANDS - 1) * (BANDS - 1))
    freq = 1.0 + jnp.floor((band * band * (TOKENS // 4 - 1) + 0.5) * (1.0 / span))
    inner = freq * at * (1.0 / TOKENS)
    inner = inner - jnp.round(inner)
    inner_cos, inner_sin = sine_turns(inner + 0.25), sine_turns(inner)
    outer = freq * at * (1.0 / NBLK)
    outer = outer - jnp.round(outer)
    outer_cos, outer_sin = sine_turns(outer + 0.25), sine_turns(outer)
    ramp_row = lax.broadcasted_iota(jnp.int32, (FEAT_PAD - 2 * BANDS, BLK), 0) == 0
    ramp_at = lax.broadcasted_iota(jnp.int32, (FEAT_PAD - 2 * BANDS, BLK), 1).astype(f32)

    def features(a):
        turn_cos, turn_sin = outer_cos[:, a:a + 1], outer_sin[:, a:a + 1]
        ramp = jnp.where(ramp_row, (ramp_at + float(a * BLK)) * (1.0 / TOKENS), 0.0)
        return jnp.concatenate([inner_cos * turn_cos - inner_sin * turn_sin,
                                inner_sin * turn_cos + inner_cos * turn_sin, ramp], 0)

    lane = lax.broadcasted_iota(jnp.int32, (CH, CHUNK), 1).astype(f32)
    per_chunk = CHUNK // BLK
    for chunk in range(TOKENS // CHUNK):
        feat = jnp.concatenate([features(chunk * per_chunk + n) for n in range(per_chunk)], 1)
        top, low = split(feat)
        one = sine_turns(mm(w_in, jnp.concatenate([top, low, top], 0)))
        top, low = split(one)
        two = sine_turns(mm(w_mid, jnp.concatenate([top, low, top], 0)))
        top, low = split(two)
        shape = mm(w_out, jnp.concatenate([top, low, top], 0))[:CH]
        taper = gain * jnp.exp(-rate * (lane + float(chunk * CHUNK))) * shape
        for n in range(per_chunk):
            first_row = (chunk * per_chunk + n) * CH
            rows_ref[first_row:first_row + CH, :] = taper[:, n * BLK:(n + 1) * BLK]
    spec = forward(rows_ref, first_ref, tw_ref, mats_ref)
    direct = jnp.concatenate([jnp.broadcast_to(skip[c:c + 1], (NBLK, BLK)) for c in range(CH)], 0)
    spec_ref[:, :BLK] = spec[:, :BLK] + direct
    spec_ref[:, BLK:] = spec[:, BLK:]


def conv_kernel(field_ref, wide_ref, table_ref, other_hbm, out_ref, other_ref, query_ref, prod_ref, conv_ref, sem):
    swap = pltpu.make_async_copy(other_hbm, other_ref, sem)
    swap.start()
    spec_ref, tw_ref, par_ref, mats_ref, first_ref, last_ref = views(wide_ref, table_ref)
    par = par_ref[...]
    taps = [jnp.broadcast_to(par[:, n:n + 1], (CH, BLK))[None] for n in range(3 * TAPS)]
    span = 8
    lane = lax.broadcasted_iota(jnp.int32, (span + 1, CH, BLK), 2)

    def later(value, steps):
        turned = pltpu.roll(value, steps, 2)
        return jnp.where(lane < steps, jnp.concatenate([turned[:1], turned[:-1]], 0), turned)

    for start in range(0, NBLK, span):
        block = [field_ref[BACK * n % NBLK].astype(f32) for n in range(max(start - 1, 0), start + span)]
        if start == 0:
            block = [jnp.zeros_like(block[0])] + block
        block = jnp.stack(block, 0)
        mixed = []
        for f in range(3):
            now = block[:, f * CH:(f + 1) * CH, :]
            past = later(now, 1)
            t = taps[f * TAPS:(f + 1) * TAPS]
            total = later(t[6] * now, 2) + (t[4] * now + t[5] * past)
            total = later(total, 2) + (t[2] * now + t[3] * past)
            total = later(total, 2) + (t[0] * now + t[1] * past)
            mixed.append(total[1:].astype(bf16).reshape(span * CH, BLK))
        at = slice(start * CH, (start + span) * CH)
        prod_ref[at, :] = mixed[1].astype(f32) * mixed[2].astype(f32)
        query_ref[at, :] = mixed[0].astype(f32)
    spec = forward(prod_ref, first_ref, tw_ref, mats_ref)
    s_re, s_im = spec[:, :BLK], spec[:, BLK:]
    h_re, h_im = spec_ref[:, :BLK], spec_ref[:, BLK:]
    both = jnp.concatenate([s_re * h_re - s_im * h_im, -(s_re * h_im + s_im * h_re)], 1)
    back = mm_split(both, mats_ref[0][...], mats_ref[1][...])
    tw_re, tw_im = tw_ref[0][...], tw_ref[1][...]
    cols = []
    for c in range(CH):
        re, im = back[c * NBLK:(c + 1) * NBLK, :BLK], back[c * NBLK:(c + 1) * NBLK, BLK:]
        cols.append(jnp.concatenate([re * tw_re - im * tw_im, -(re * tw_im + im * tw_re)], 0))
    top, low = split(jnp.concatenate(cols, 1))
    last = jnp.concatenate([last_ref[0][...], last_ref[1][...]], 1)
    conv = mm(last, jnp.concatenate([top, low, top], 0))
    for c in range(CH):
        conv_ref[pl.ds(c, NBLK, stride=CH), :] = conv[:, c * BLK:(c + 1) * BLK]
    sub = lax.broadcasted_iota(jnp.int32, (CH, BLK), 0) < 4
    same = sub == (lax.broadcasted_iota(jnp.int32, (CH, BLK), 1) < HALF)
    order = second_order()
    lane = lax.broadcasted_iota(jnp.int32, (BLK, BLK), 1)
    token = lane // HALF * SHARE + lane % HALF // SHARE * (2 * SHARE) + lane % SHARE
    reorder = (lax.broadcasted_iota(jnp.int32, (BLK, BLK), 0) == token).astype(f32).astype(bf16)

    for slot in range(0, NBLK, 8):
        gated = []
        for ctx in order[slot:slot + 8]:
            rows = slice(ctx * CH, (ctx + 1) * CH)
            gated.append(query_ref[rows, :] * conv_ref[rows, :])
        gated = mm(jnp.concatenate(gated, 0).astype(bf16), reorder)
        tops, lows = [], []
        for n in range(0, 8, 2):
            pair = []
            for at in (n * CH, (n + 1) * CH):
                rows = gated[at:at + CH]
                pair.append(jnp.where(same, rows, pltpu.roll(pltpu.roll(rows, 4, 0), HALF, 1)))
            tops.append(jnp.where(sub, pair[0], pltpu.roll(pair[1], 4, 0)))
            lows.append(jnp.where(sub, pltpu.roll(pair[0], 4, 0), pair[1]))
        at = slot * 4
        out_ref[at:at + 32, :] = jnp.concatenate(tops, 0).astype(bf16)
        out_ref[at + NBLK * 4:at + NBLK * 4 + 32, :] = jnp.concatenate(lows, 0).astype(bf16)
    swap.wait()


def project_kernel(rows_ref, own_ref, other_ref, out_ref):
    core = lax.axis_index("ch") % 2
    depth = rows_ref.shape[0] // 2

    def turned(part):
        rows = rows_ref[pl.ds(pl.multiple_of(part * depth, depth), depth), :]
        return rows.astype(f32).T.astype(bf16)

    own, other = turned(core), turned(1 - core)
    total = mm(own[:HALF], own_ref[:depth, :]) + mm(own[HALF:], own_ref[depth:, :])
    total = total + mm(other[:HALF], other_ref[:depth, :]) + mm(other[HALF:], other_ref[depth:, :])
    out_ref[...] = total.astype(bf16)


def per_device(query_field, key_field, value_field, short_taps, filt_in, filt_mid, filt_out,
               decay_rate, skip_gain, out_weight):
    chans = query_field.shape[1]
    cores = 2
    groups = lax.axis_size("ch")
    chips = groups // cores
    dout = out_weight.shape[1]
    params = pltpu.CompilerParams(vmem_limit_bytes=32 * 1024 * 1024)
    far = pl.BlockSpec(memory_space=pltpu.HBM)
    operands = (query_field, key_field, value_field, filt_in, filt_mid, filt_out, short_taps,
                decay_rate.reshape(1, chans), skip_gain.reshape(1, chans))
    parts, pack = pl.pallas_call(
        prep_kernel,
        out_shape=[jax.ShapeDtypeStruct((NBLK, 3 * CH, BLK), bf16),
                   jax.ShapeDtypeStruct((PACK_ROWS, chans), f32)],
        in_specs=[far] * len(operands),
        scratch_shapes=[pltpu.VMEM((3,) + query_field.shape, bf16)]
        + [pltpu.VMEM(t.shape, t.dtype) for t in operands[3:]]
        + [pltpu.SemaphoreType.DMA((len(operands),))],
        compiler_params=pltpu.CompilerParams(vmem_limit_bytes=62 * 1024 * 1024),
        name="prep",
    )(*operands)
    fields = lax.all_to_all(parts, "ctx", 0, 0, tiled=True, axis_index_groups=[first_order()])
    small, stack = pl.pallas_call(
        weights_kernel,
        out_shape=[jax.ShapeDtypeStruct((CH, 128), f32),
                   jax.ShapeDtypeStruct((2 * UNITS + 2 * CH, 2 * BLK), bf16)],
        compiler_params=params,
        name="weights",
    )(pack)
    own_weight, small = lax.optimization_barrier((out_weight, small))
    other_weight = lax.ppermute(own_weight, "ch", [(d, d ^ 1) for d in range(groups)])
    wide, table = pl.pallas_call(
        filter_kernel,
        out_shape=[jax.ShapeDtypeStruct((CH * NBLK + NBLK + CH, 2 * BLK), f32),
                   jax.ShapeDtypeStruct((4 * BLK + 2 * BLK, 2 * BLK), bf16)],
        scratch_shapes=[pltpu.VMEM((NBLK * CH, BLK), f32)],
        compiler_params=params,
        cost_estimate=pl.CostEstimate(flops=10**11, bytes_accessed=10**9, transcendentals=10**6),
        name="filter",
    )(small, stack)
    gated, other_weight = pl.pallas_call(
        conv_kernel,
        out_shape=[jax.ShapeDtypeStruct((NBLK * CH, BLK), bf16),
                   jax.ShapeDtypeStruct(out_weight.shape, bf16)],
        in_specs=[pl.BlockSpec(memory_space=pltpu.VMEM)] * 3 + [far],
        scratch_shapes=[pltpu.VMEM((NBLK * CH, BLK), f32)] * 3 + [pltpu.SemaphoreType.DMA],
        compiler_params=params,
        name="convolve",
    )(fields, wide, table, other_weight)
    on_chip = [[c * groups + x * cores + k for k in range(cores) for c in second_order()] for x in range(chips)]
    returned = lax.all_to_all(gated.reshape(NBLK * cores, CH // cores, BLK), ("ctx", "ch"), 0, 0,
                              tiled=True, axis_index_groups=on_chip)
    partial = pl.pallas_call(
        project_kernel,
        out_shape=jax.ShapeDtypeStruct((BLK // cores, dout), bf16),
        compiler_params=params,
        name="project",
    )(returned.reshape(NBLK * CH, BLK), own_weight, other_weight)
    along_x = [[x * cores + k for x in range(chips)] for k in range(cores)]
    shares = lax.all_to_all(partial.reshape(chips, SHARE, dout), "ch", 0, 0, tiled=True,
                            axis_index_groups=along_x)
    return jnp.sum(shares.astype(f32), 0).astype(bf16)


def solution(mesh):
    return jax.shard_map(
        per_device,
        mesh=mesh,
        in_specs=(
            P("ctx", "ch"),
            P("ctx", "ch"),
            P("ctx", "ch"),
            P(None, None, "ch"),
            P(),
            P(),
            P(None, "ch"),
            P("ch"),
            P("ch"),
            P("ch", None),
        ),
        out_specs=P(("ctx", "ch"), None),
        check_vma=False,
    )
```

```python
import math

import jax
import jax.numpy as jnp
import numpy as np
from jax import lax
from jax.experimental import pallas as pl
from jax.experimental.pallas import tpu as pltpu
from jax.sharding import PartitionSpec as P

TOKENS = 8192
BLK = 128
NBLK = 64
CH = 8
BANDS = 16
FEAT = 33
FEAT_PAD = 48
HALF = 64
SHARE = 16
TAPS = 7
UNITS = 64
CHUNK = 2048
STEP = 27
BACK = 19
PACK = (0, 64, 88, 96, 104, 112)
PACK_ROWS = 120
bf16 = jnp.bfloat16
f32 = jnp.float32
highest = lax.Precision.HIGHEST


def first_order():
    return [STEP * n % NBLK for n in range(NBLK)]


def second_order():
    order = []
    for n in range(NBLK):
        turned = int(format(n, "06b")[::-1], 2)
        order.append(turned % 8 * 8 + turned // 8)
    return order


def second_place(ctx):
    return sum((ctx // 2 ** src % 2) * 2 ** dst for src, dst in enumerate((2, 1, 0, 5, 4, 3)))


def sine_coefs():
    grid = 0.25 * np.cos((np.arange(400) + 0.5) * math.pi / 400)
    grid = np.concatenate([grid, 0.5 * np.cos((np.arange(800) + 0.5) * math.pi / 800)])
    grid = grid[np.abs(grid) > 1e-3]
    powers = np.stack([grid ** (2 * k + 1) for k in range(7)], 1)
    coef, *_ = np.linalg.lstsq(powers, np.sin(2.0 * math.pi * grid), rcond=None)
    return [float(c) for c in coef]


SINE = sine_coefs()
NEAREST = 1.5 * 2.0**23


def sine_turns(turns):
    rest = turns - ((turns + NEAREST) - NEAREST)
    sq = rest * rest
    acc = sq * SINE[-1] + SINE[-2]
    for c in SINE[-3::-1]:
        acc = acc * sq + c
    return acc * rest


def split(value):
    top = value.astype(bf16)
    return top, (value - top.astype(f32)).astype(bf16)


def mm(left, right):
    return jnp.dot(left, right, preferred_element_type=f32)


def mm_split(value, top_mat, low_mat):
    top = value.astype(bf16)
    return mm(top, top_mat) + mm(top, low_mat)


def lift(rows, low_half):
    return jnp.where(low_half, rows[0], pltpu.roll(rows[1], 4, 1))


def drop(rows, low_half):
    return jnp.where(low_half, pltpu.roll(rows[0], 4, 1), rows[1])


def prep_kernel(query_hbm, key_hbm, value_hbm, w_in_hbm, w_mid_hbm, w_out_hbm, taps_hbm, rate_hbm,
                skip_hbm, out_ref, pack_ref, held, w_in_ref, w_mid_ref, w_out_ref, taps_ref, rate_ref,
                skip_ref, sems):
    sources = (query_hbm, key_hbm, value_hbm, w_out_hbm, taps_hbm, w_mid_hbm, w_in_hbm, rate_hbm, skip_hbm)
    targets = (held.at[0], held.at[1], held.at[2], w_out_ref, taps_ref, w_mid_ref, w_in_ref, rate_ref, skip_ref)
    copies = [pltpu.make_async_copy(src, dst, sems.at[n])
              for n, (src, dst) in enumerate(zip(sources, targets))]
    for copy in copies:
        copy.start()
    low_half = lax.broadcasted_iota(jnp.int32, (NBLK // 2, CH, BLK), 1) < 4
    sets = []
    for f in range(3):
        copies[f].wait()
        turned = held[f].astype(f32).T.reshape(2, NBLK // 2, CH, BLK)
        sets.append((lift(turned, low_half), drop(turned, low_half)))
    for slot, ctx in enumerate(first_order()):
        place = second_place(ctx)
        out_ref[slot] = jnp.concatenate([pair[place % 2][place // 2] for pair in sets], 0).astype(bf16)
    for copy in copies[3:]:
        copy.wait()
    chans = rate_ref.shape[1]
    at_out, at_taps, at_rate, at_skip, at_mid, at_in = PACK
    pack_ref[at_out:at_out + UNITS, :] = w_out_ref[...]
    for f in range(3):
        pack_ref[at_taps + f * 8:at_taps + f * 8 + TAPS, :] = taps_ref[f]
    pack_ref[at_rate:at_rate + 8, :] = jnp.broadcast_to(rate_ref[...], (8, chans))
    pack_ref[at_skip:at_skip + 8, :] = jnp.broadcast_to(skip_ref[...], (8, chans))
    for n in range(8):
        pack_ref[at_mid:at_mid + 8, n * UNITS:(n + 1) * UNITS] = w_mid_ref[n * 8:(n + 1) * 8, :]
    for n in range(4):
        pack_ref[at_in:at_in + 8, n * UNITS:(n + 1) * UNITS] = w_in_ref[n * 8:(n + 1) * 8, :]
    pack_ref[at_in:at_in + 1, 4 * UNITS:5 * UNITS] = w_in_ref[FEAT - 1:FEAT, :]


def forward(rows_ref, first_ref, tw_ref, mats_ref):
    cols = jnp.concatenate([rows_ref[pl.ds(c, NBLK, stride=CH), :] for c in range(CH)], 1)
    top, low = split(cols)
    outer = mm(first_ref[...], jnp.concatenate([top, low, top], 0))
    tw_re, tw_im = tw_ref[0][...], tw_ref[1][...]
    out = []
    for c in range(CH):
        lanes = slice(c * BLK, (c + 1) * BLK)
        re, im = outer[:NBLK, lanes], outer[NBLK:, lanes]
        out.append(jnp.concatenate([re * tw_re - im * tw_im, re * tw_im + im * tw_re], 1))
    return mm_split(jnp.concatenate(out, 0), mats_ref[0][...], mats_ref[1][...])


def views(wide_ref, table_ref):
    half = 2 * BLK
    spec = wide_ref.at[0:CH * NBLK]
    tw = [wide_ref.at[CH * NBLK:CH * NBLK + NBLK, n * BLK:(n + 1) * BLK] for n in range(2)]
    par = wide_ref.at[CH * NBLK + NBLK:CH * NBLK + NBLK + CH, 0:BLK]
    mats = [table_ref.at[n * half:(n + 1) * half] for n in range(2)]
    first = table_ref.at[2 * half:2 * half + BLK, 0:3 * NBLK]
    last = [table_ref.at[2 * half + BLK + n * NBLK:2 * half + BLK + (n + 1) * NBLK, 0:3 * NBLK]
            for n in range(2)]
    return spec, tw, par, mats, first, last


def fill_tables(first_ref, last_ref, tw_ref, mats_ref):
    def grid(shape, axis):
        return lax.broadcasted_iota(jnp.int32, shape, axis)

    def wave(turns):
        turns = turns - jnp.round(turns)
        return sine_turns(turns + 0.25), sine_turns(turns)

    shape = (NBLK, NBLK)
    cos, sin = wave((grid(shape, 0).astype(f32) - 0.25) * grid(shape, 1).astype(f32) / NBLK)
    top, low = split(jnp.concatenate([cos, -sin], 0))
    first_ref[...] = jnp.concatenate([top, top, low], 1)
    cos, sin = wave((grid(shape, 1).astype(f32) - 0.25) * grid(shape, 0).astype(f32) / NBLK)
    top, low = split(jnp.concatenate([cos, -sin], 1) / TOKENS)
    wide = jnp.concatenate([top, top, low], 1)
    last_ref[0][...], last_ref[1][...] = wide[:, :3 * NBLK], wide[:, 3 * NBLK:]
    shape = (NBLK, BLK)
    shifted = grid(shape, 0).astype(f32) - 0.25
    cos, sin = wave(shifted * grid(shape, 1).astype(f32) / TOKENS)
    tw_ref[0][...], tw_ref[1][...] = cos, -sin
    shape = (BLK, BLK)
    cos, sin = wave((grid(shape, 0) * grid(shape, 1)).astype(f32) / BLK)
    mats = jnp.concatenate([jnp.concatenate([cos, -sin], 1), jnp.concatenate([sin, cos], 1)], 0)
    mats_ref[0][...], mats_ref[1][...] = split(mats)


def weights_kernel(pack_ref, small_ref, stack_ref):
    at_out, at_taps, at_rate, at_skip, at_mid, at_in = PACK
    chans = pack_ref.shape[1]
    row = lax.broadcasted_iota(jnp.int32, (CH, chans), 0)
    wanted = second_place(lax.axis_index("ctx")) * 4 + row % 4 + row // 4 * (chans // 2)
    pick = (lax.broadcasted_iota(jnp.int32, (CH, chans), 1) == wanted).astype(f32)

    def stack(weights):
        top, low = split(weights)
        return jnp.concatenate([top, top, low], 1)

    mine = lax.dot_general(pick, pack_ref[:at_mid, :], (((1,), (1,)), ((), ())), precision=highest,
                           preferred_element_type=f32)
    per_turn = 1.0 / (2.0 * math.pi)
    w_in = jnp.concatenate([pack_ref[at_in:at_in + 8, n * UNITS:(n + 1) * UNITS] for n in range(4)]
                           + [pack_ref[at_in:at_in + 1, 4 * UNITS:5 * UNITS]], 0)
    padded = jnp.concatenate([w_in[1:FEAT], w_in[0:1], jnp.zeros((FEAT_PAD - FEAT, UNITS), f32)], 0)
    w_mid = jnp.concatenate([pack_ref[at_mid:at_mid + 8, n * UNITS:(n + 1) * UNITS] for n in range(8)], 0)
    small_ref[:, 0:at_mid] = mine
    stack_ref[0:UNITS, 0:3 * FEAT_PAD] = stack(padded.T * per_turn)
    stack_ref[UNITS:2 * UNITS, 0:3 * UNITS] = stack(w_mid.T * per_turn)
    wide = stack(mine[:, at_out:at_out + UNITS])
    stack_ref[2 * UNITS:2 * UNITS + 2 * CH, 0:3 * UNITS] = jnp.concatenate([wide, wide], 0)


def filter_kernel(small_ref, stack_ref, wide_ref, table_ref, rows_ref):
    at_out, at_taps, at_rate, at_skip, at_mid, at_in = PACK
    spec_ref, tw_ref, par_ref, mats_ref, first_ref, last_ref = views(wide_ref, table_ref)
    fill_tables(first_ref, last_ref, tw_ref, mats_ref)
    w_in = stack_ref[0:UNITS, 0:3 * FEAT_PAD]
    w_mid = stack_ref[UNITS:2 * UNITS, 0:3 * UNITS]
    w_out = stack_ref[2 * UNITS:2 * UNITS + 2 * CH, 0:3 * UNITS]
    taps = [small_ref[:, at_taps + f * 8:at_taps + f * 8 + TAPS] for f in range(3)]
    rate = small_ref[:, at_rate:at_rate + 1]
    skip = small_ref[:, at_skip:at_skip + 1]
    par_ref[...] = jnp.concatenate(taps + [jnp.zeros((CH, 128 - 3 * TAPS), f32)], 1)
    gain = jnp.sqrt(2.0 * rate)

    band = lax.broadcasted_iota(jnp.int32, (BANDS, BLK), 0).astype(f32)
    at = lax.broadcasted_iota(jnp.int32, (BANDS, BLK), 1).astype(f32)
    span = float((BANDS - 1) * (BANDS - 1))
    freq = 1.0 + jnp.floor((band * band * (TOKENS // 4 - 1) + 0.5) * (1.0 / span))
    inner = freq * at * (1.0 / TOKENS)
    inner = inner - jnp.round(inner)
    inner_cos, inner_sin = sine_turns(inner + 0.25), sine_turns(inner)
    outer = freq * at * (1.0 / NBLK)
    outer = outer - jnp.round(outer)
    outer_cos, outer_sin = sine_turns(outer + 0.25), sine_turns(outer)
    ramp_row = lax.broadcasted_iota(jnp.int32, (FEAT_PAD - 2 * BANDS, BLK), 0) == 0
    ramp_at = lax.broadcasted_iota(jnp.int32, (FEAT_PAD - 2 * BANDS, BLK), 1).astype(f32)

    def features(a):
        turn_cos, turn_sin = outer_cos[:, a:a + 1], outer_sin[:, a:a + 1]
        ramp = jnp.where(ramp_row, (ramp_at + float(a * BLK)) * (1.0 / TOKENS), 0.0)
        return jnp.concatenate([inner_cos * turn_cos - inner_sin * turn_sin,
                                inner_sin * turn_cos + inner_cos * turn_sin, ramp], 0)

    lane = lax.broadcasted_iota(jnp.int32, (CH, CHUNK), 1).astype(f32)
    per_chunk = CHUNK // BLK
    for chunk in range(TOKENS // CHUNK):
        feat = jnp.concatenate([features(chunk * per_chunk + n) for n in range(per_chunk)], 1)
        top, low = split(feat)
        one = sine_turns(mm(w_in, jnp.concatenate([top, low, top], 0)))
        top, low = split(one)
        two = sine_turns(mm(w_mid, jnp.concatenate([top, low, top], 0)))
        top, low = split(two)
        shape = mm(w_out, jnp.concatenate([top, low, top], 0))[:CH]
        taper = gain * jnp.exp(-rate * (lane + float(chunk * CHUNK))) * shape
        for n in range(per_chunk):
            first_row = (chunk * per_chunk + n) * CH
            rows_ref[first_row:first_row + CH, :] = taper[:, n * BLK:(n + 1) * BLK]
    spec = forward(rows_ref, first_ref, tw_ref, mats_ref)
    direct = jnp.concatenate([jnp.broadcast_to(skip[c:c + 1], (NBLK, BLK)) for c in range(CH)], 0)
    spec_ref[:, :BLK] = spec[:, :BLK] + direct
    spec_ref[:, BLK:] = spec[:, BLK:]


def conv_kernel(field_ref, wide_ref, table_ref, other_hbm, out_ref, other_ref, query_ref, prod_ref, conv_ref, sem):
    swap = pltpu.make_async_copy(other_hbm, other_ref, sem)
    swap.start()
    spec_ref, tw_ref, par_ref, mats_ref, first_ref, last_ref = views(wide_ref, table_ref)
    par = par_ref[...]
    taps = [jnp.broadcast_to(par[:, n:n + 1], (CH, BLK))[None] for n in range(3 * TAPS)]
    span = 8
    lane = lax.broadcasted_iota(jnp.int32, (span + 1, CH, BLK), 2)

    def later(value, steps):
        turned = pltpu.roll(value, steps, 2)
        return jnp.where(lane < steps, jnp.concatenate([turned[:1], turned[:-1]], 0), turned)

    for start in range(0, NBLK, span):
        block = [field_ref[BACK * n % NBLK].astype(f32) for n in range(max(start - 1, 0), start + span)]
        if start == 0:
            block = [jnp.zeros_like(block[0])] + block
        block = jnp.stack(block, 0)
        mixed = []
        for f in range(3):
            now = block[:, f * CH:(f + 1) * CH, :]
            past = later(now, 1)
            t = taps[f * TAPS:(f + 1) * TAPS]
            total = later(t[6] * now, 2) + (t[4] * now + t[5] * past)
            total = later(total, 2) + (t[2] * now + t[3] * past)
            total = later(total, 2) + (t[0] * now + t[1] * past)
            mixed.append(total[1:].astype(bf16).reshape(span * CH, BLK))
        at = slice(start * CH, (start + span) * CH)
        prod_ref[at, :] = mixed[1].astype(f32) * mixed[2].astype(f32)
        query_ref[at, :] = mixed[0].astype(f32)
    spec = forward(prod_ref, first_ref, tw_ref, mats_ref)
    s_re, s_im = spec[:, :BLK], spec[:, BLK:]
    h_re, h_im = spec_ref[:, :BLK], spec_ref[:, BLK:]
    both = jnp.concatenate([s_re * h_re - s_im * h_im, -(s_re * h_im + s_im * h_re)], 1)
    back = mm_split(both, mats_ref[0][...], mats_ref[1][...])
    tw_re, tw_im = tw_ref[0][...], tw_ref[1][...]
    cols = []
    for c in range(CH):
        re, im = back[c * NBLK:(c + 1) * NBLK, :BLK], back[c * NBLK:(c + 1) * NBLK, BLK:]
        cols.append(jnp.concatenate([re * tw_re - im * tw_im, -(re * tw_im + im * tw_re)], 0))
    top, low = split(jnp.concatenate(cols, 1))
    last = jnp.concatenate([last_ref[0][...], last_ref[1][...]], 1)
    conv = mm(last, jnp.concatenate([top, low, top], 0))
    for c in range(CH):
        conv_ref[pl.ds(c, NBLK, stride=CH), :] = conv[:, c * BLK:(c + 1) * BLK]
    sub = lax.broadcasted_iota(jnp.int32, (CH, BLK), 0) < 4
    same = sub == (lax.broadcasted_iota(jnp.int32, (CH, BLK), 1) < HALF)
    order = second_order()
    lane = lax.broadcasted_iota(jnp.int32, (BLK, BLK), 1)
    slot = lane % HALF // SHARE
    token = lane // HALF * SHARE + (slot ^ slot // 2) * (2 * SHARE) + lane % SHARE
    reorder = (lax.broadcasted_iota(jnp.int32, (BLK, BLK), 0) == token).astype(f32).astype(bf16)

    for slot in range(0, NBLK, 8):
        gated = []
        for ctx in order[slot:slot + 8]:
            rows = slice(ctx * CH, (ctx + 1) * CH)
            gated.append(query_ref[rows, :] * conv_ref[rows, :])
        gated = mm(jnp.concatenate(gated, 0).astype(bf16), reorder)
        tops, lows = [], []
        for n in range(0, 8, 2):
            pair = []
            for at in (n * CH, (n + 1) * CH):
                rows = gated[at:at + CH]
                pair.append(jnp.where(same, rows, pltpu.roll(pltpu.roll(rows, 4, 0), HALF, 1)))
            tops.append(jnp.where(sub, pair[0], pltpu.roll(pair[1], 4, 0)))
            lows.append(jnp.where(sub, pltpu.roll(pair[0], 4, 0), pair[1]))
        at = slot * 4
        out_ref[at:at + 32, :] = jnp.concatenate(tops, 0).astype(bf16)
        out_ref[at + NBLK * 4:at + NBLK * 4 + 32, :] = jnp.concatenate(lows, 0).astype(bf16)
    swap.wait()


def project_kernel(rows_ref, own_ref, other_ref, out_ref):
    core = lax.axis_index("ch") % 2
    depth = rows_ref.shape[0] // 2

    def turned(part):
        rows = rows_ref[pl.ds(pl.multiple_of(part * depth, depth), depth), :]
        return rows.astype(f32).T.astype(bf16)

    own, other = turned(core), turned(1 - core)
    total = mm(own[:HALF], own_ref[:depth, :]) + mm(own[HALF:], own_ref[depth:, :])
    total = total + mm(other[:HALF], other_ref[:depth, :]) + mm(other[HALF:], other_ref[depth:, :])
    out_ref[...] = total.astype(bf16)


def per_device(query_field, key_field, value_field, short_taps, filt_in, filt_mid, filt_out,
               decay_rate, skip_gain, out_weight):
    chans = query_field.shape[1]
    cores = 2
    groups = lax.axis_size("ch")
    chips = groups // cores
    dout = out_weight.shape[1]
    params = pltpu.CompilerParams(vmem_limit_bytes=32 * 1024 * 1024)
    far = pl.BlockSpec(memory_space=pltpu.HBM)
    operands = (query_field, key_field, value_field, filt_in, filt_mid, filt_out, short_taps,
                decay_rate.reshape(1, chans), skip_gain.reshape(1, chans))
    parts, pack = pl.pallas_call(
        prep_kernel,
        out_shape=[jax.ShapeDtypeStruct((NBLK, 3 * CH, BLK), bf16),
                   jax.ShapeDtypeStruct((PACK_ROWS, chans), f32)],
        in_specs=[far] * len(operands),
        scratch_shapes=[pltpu.VMEM((3,) + query_field.shape, bf16)]
        + [pltpu.VMEM(t.shape, t.dtype) for t in operands[3:]]
        + [pltpu.SemaphoreType.DMA((len(operands),))],
        compiler_params=pltpu.CompilerParams(vmem_limit_bytes=62 * 1024 * 1024),
        name="prep",
    )(*operands)
    fields = lax.all_to_all(parts, "ctx", 0, 0, tiled=True, axis_index_groups=[first_order()])
    small, stack = pl.pallas_call(
        weights_kernel,
        out_shape=[jax.ShapeDtypeStruct((CH, 128), f32),
                   jax.ShapeDtypeStruct((2 * UNITS + 2 * CH, 2 * BLK), bf16)],
        compiler_params=params,
        name="weights",
    )(pack)
    own_weight, small = lax.optimization_barrier((out_weight, small))
    other_weight = lax.ppermute(own_weight, "ch", [(d, d ^ 1) for d in range(groups)])
    wide, table = pl.pallas_call(
        filter_kernel,
        out_shape=[jax.ShapeDtypeStruct((CH * NBLK + NBLK + CH, 2 * BLK), f32),
                   jax.ShapeDtypeStruct((4 * BLK + 2 * BLK, 2 * BLK), bf16)],
        scratch_shapes=[pltpu.VMEM((NBLK * CH, BLK), f32)],
        compiler_params=params,
        cost_estimate=pl.CostEstimate(flops=10**11, bytes_accessed=10**9, transcendentals=10**6),
        name="filter",
    )(small, stack)
    gated, other_weight = pl.pallas_call(
        conv_kernel,
        out_shape=[jax.ShapeDtypeStruct((NBLK * CH, BLK), bf16),
                   jax.ShapeDtypeStruct(out_weight.shape, bf16)],
        in_specs=[pl.BlockSpec(memory_space=pltpu.VMEM)] * 3 + [far],
        scratch_shapes=[pltpu.VMEM((NBLK * CH, BLK), f32)] * 3 + [pltpu.SemaphoreType.DMA],
        compiler_params=params,
        name="convolve",
    )(fields, wide, table, other_weight)
    on_chip = [[c * groups + x * cores + k for k in range(cores) for c in second_order()] for x in range(chips)]
    returned = lax.all_to_all(gated.reshape(NBLK * cores, CH // cores, BLK), ("ctx", "ch"), 0, 0,
                              tiled=True, axis_index_groups=on_chip)
    partial = pl.pallas_call(
        project_kernel,
        out_shape=jax.ShapeDtypeStruct((BLK // cores, dout), bf16),
        compiler_params=params,
        name="project",
    )(returned.reshape(NBLK * CH, BLK), own_weight, other_weight)
    along_x = [[(x ^ x // 2) * cores + k for x in range(chips)] for k in range(cores)]
    shares = lax.all_to_all(partial.reshape(chips, SHARE, dout), "ch", 0, 0, tiled=True,
                            axis_index_groups=along_x)
    return jnp.sum(shares.astype(f32), 0).astype(bf16)


def solution(mesh):
    return jax.shard_map(
        per_device,
        mesh=mesh,
        in_specs=(
            P("ctx", "ch"),
            P("ctx", "ch"),
            P("ctx", "ch"),
            P(None, None, "ch"),
            P(),
            P(),
            P(None, "ch"),
            P("ch"),
            P("ch"),
            P("ch", None),
        ),
        out_specs=P(("ctx", "ch"), None),
        check_vma=False,
    )
```

```python
import math

import jax
import jax.numpy as jnp
import numpy as np
from jax import lax
from jax.experimental import pallas as pl
from jax.experimental.pallas import tpu as pltpu
from jax.sharding import PartitionSpec as P

TOKENS = 8192
BLK = 128
NBLK = 64
CH = 8
BANDS = 16
FEAT = 33
FEAT_PAD = 48
HALF = 64
SHARE = 16
TAPS = 7
EDGE = TAPS - 1
PIECE = 20
UNITS = 64
CHUNK = 2048
PACK = (0, 64, 88, 96, 104, 112)
PACK_ROWS = 120
bf16 = jnp.bfloat16
f32 = jnp.float32
highest = lax.Precision.HIGHEST


def second_order():
    order = []
    for n in range(NBLK):
        turned = int(format(n, "06b")[::-1], 2)
        order.append(turned % 8 * 8 + turned // 8)
    return order


def second_place(ctx):
    return sum((ctx // 2 ** src % 2) * 2 ** dst for src, dst in enumerate((2, 1, 0, 5, 4, 3)))


def sine_coefs():
    grid = 0.25 * np.cos((np.arange(400) + 0.5) * math.pi / 400)
    grid = np.concatenate([grid, 0.5 * np.cos((np.arange(800) + 0.5) * math.pi / 800)])
    grid = grid[np.abs(grid) > 1e-3]
    powers = np.stack([grid ** (2 * k + 1) for k in range(7)], 1)
    coef, *_ = np.linalg.lstsq(powers, np.sin(2.0 * math.pi * grid), rcond=None)
    return [float(c) for c in coef]


SINE = sine_coefs()
NEAREST = 1.5 * 2.0**23


def sine_turns(turns):
    rest = turns - ((turns + NEAREST) - NEAREST)
    sq = rest * rest
    acc = sq * SINE[-1] + SINE[-2]
    for c in SINE[-3::-1]:
        acc = acc * sq + c
    return acc * rest


def split(value):
    top = value.astype(bf16)
    return top, (value - top.astype(f32)).astype(bf16)


def mm(left, right):
    return jnp.dot(left, right, preferred_element_type=f32)


def mm_split(value, top_mat, low_mat):
    top = value.astype(bf16)
    return mm(top, top_mat) + mm(top, low_mat)


def prep_kernel(query_hbm, key_hbm, value_hbm, w_in_hbm, w_mid_hbm, w_out_hbm, taps_hbm, rate_hbm,
                skip_hbm, out_ref, pack_ref, held, w_in_ref, w_mid_ref, w_out_ref, taps_ref, rate_ref,
                skip_ref, lead_ref, edge_ref, sems):
    sources = (taps_hbm, key_hbm, value_hbm, query_hbm, w_out_hbm, w_mid_hbm, w_in_hbm, rate_hbm, skip_hbm)
    targets = (taps_ref, held.at[1], held.at[2], held.at[0], w_out_ref, w_mid_ref, w_in_ref, rate_ref, skip_ref)
    copies = [pltpu.make_async_copy(src, dst, sems.at[n])
              for n, (src, dst) in enumerate(zip(sources, targets))]
    for copy in copies:
        copy.start()
    low_half = lax.broadcasted_iota(jnp.int32, (NBLK // 2, CH, BLK), 1) < 4
    half = edge_ref.shape[1]
    edge_ref[...] = jnp.zeros_like(edge_ref)
    copies[0].wait()
    mixed = []
    blocks = range(2 * half // BLK)
    for f in (1, 2):
        copies[f].wait()
        parts = []
        for n in blocks:
            lead = lead_ref.at[(f - 1) * len(blocks) + n]
            lanes = slice(n * BLK, (n + 1) * BLK)
            lead[0:8, :] = jnp.zeros((8, BLK), f32)
            lead[8:8 + BLK, :] = held[f, :, lanes].astype(f32)
            total = taps_ref[f, 0:1, lanes] * lead[8:8 + BLK, :]
            for j in range(1, TAPS):
                total = total + taps_ref[f, j:j + 1, lanes] * lead[8 - j:8 - j + BLK, :]
            parts.append(total.astype(bf16).astype(f32))
            at = n * BLK // half * HALF + (f - 1) * (HALF // 2)
            lanes = slice(n * BLK % half, n * BLK % half + BLK)
            edge_ref[at:at + EDGE, lanes] = lead[8 + BLK - EDGE:8 + BLK, :]
            edge_ref[at + EDGE:at + 2 * EDGE, lanes] = lead[8:8 + EDGE, :]
        mixed.append(jnp.concatenate(parts, 1))

    def pairs(field):
        rows = field.T.reshape(2, NBLK // 2, CH, BLK)
        up = pltpu.roll(rows[1], 4, 1)
        return jnp.where(low_half, rows[0], up), jnp.where(low_half, up, rows[0])

    prod_even, prod_odd = pairs(mixed[0] * mixed[1])
    copies[3].wait()
    query_even, query_odd = pairs(held[0].astype(f32))
    edges = edge_ref[...].T.reshape(NBLK // 2, CH, BLK)
    rows = jnp.concatenate([prod_even, query_even, jnp.where(low_half, edges, prod_odd),
                            jnp.where(low_half, prod_odd, query_odd),
                            jnp.where(low_half, query_odd, edges)], 1)
    out_ref[...] = rows.reshape(NBLK * PIECE, BLK).astype(bf16)
    for copy in copies[4:]:
        copy.wait()
    chans = rate_ref.shape[1]
    at_out, at_taps, at_rate, at_skip, at_mid, at_in = PACK
    pack_ref[at_out:at_out + UNITS, :] = w_out_ref[...]
    for f in range(3):
        pack_ref[at_taps + f * 8:at_taps + f * 8 + TAPS, :] = taps_ref[f]
    pack_ref[at_rate:at_rate + 8, :] = jnp.broadcast_to(rate_ref[...], (8, chans))
    pack_ref[at_skip:at_skip + 8, :] = jnp.broadcast_to(skip_ref[...], (8, chans))
    for n in range(8):
        pack_ref[at_mid:at_mid + 8, n * UNITS:(n + 1) * UNITS] = w_mid_ref[n * 8:(n + 1) * 8, :]
    for n in range(4):
        pack_ref[at_in:at_in + 8, n * UNITS:(n + 1) * UNITS] = w_in_ref[n * 8:(n + 1) * 8, :]
    pack_ref[at_in:at_in + 1, 4 * UNITS:5 * UNITS] = w_in_ref[FEAT - 1:FEAT, :]


def forward(rows_ref, first_ref, tw_ref, mats_ref):
    cols = jnp.concatenate([rows_ref[pl.ds(c, NBLK, stride=CH), :] for c in range(CH)], 1)
    top, low = split(cols)
    outer = mm(first_ref[...], jnp.concatenate([top, low, top], 0))
    tw_re, tw_im = tw_ref[0][...], tw_ref[1][...]
    out = []
    for c in range(CH):
        lanes = slice(c * BLK, (c + 1) * BLK)
        re, im = outer[:NBLK, lanes], outer[NBLK:, lanes]
        out.append(jnp.concatenate([re * tw_re - im * tw_im, re * tw_im + im * tw_re], 1))
    return mm_split(jnp.concatenate(out, 0), mats_ref[0][...], mats_ref[1][...])


def views(wide_ref, table_ref):
    half = 2 * BLK
    spec = wide_ref.at[0:CH * NBLK]
    tw = [wide_ref.at[CH * NBLK:CH * NBLK + NBLK, n * BLK:(n + 1) * BLK] for n in range(2)]
    par = wide_ref.at[CH * NBLK + NBLK:CH * NBLK + NBLK + CH, 0:BLK]
    mats = [table_ref.at[n * half:(n + 1) * half] for n in range(2)]
    first = table_ref.at[2 * half:2 * half + BLK, 0:3 * NBLK]
    last = [table_ref.at[2 * half + BLK + n * NBLK:2 * half + BLK + (n + 1) * NBLK, 0:3 * NBLK]
            for n in range(2)]
    return spec, tw, par, mats, first, last


def fill_tables(first_ref, last_ref, tw_ref, mats_ref):
    def grid(shape, axis):
        return lax.broadcasted_iota(jnp.int32, shape, axis)

    def wave(turns):
        turns = turns - jnp.round(turns)
        return sine_turns(turns + 0.25), sine_turns(turns)

    shape = (NBLK, NBLK)
    cos, sin = wave((grid(shape, 0).astype(f32) - 0.25) * grid(shape, 1).astype(f32) / NBLK)
    top, low = split(jnp.concatenate([cos, -sin], 0))
    first_ref[...] = jnp.concatenate([top, top, low], 1)
    cos, sin = wave((grid(shape, 1).astype(f32) - 0.25) * grid(shape, 0).astype(f32) / NBLK)
    top, low = split(jnp.concatenate([cos, -sin], 1) / TOKENS)
    wide = jnp.concatenate([top, top, low], 1)
    last_ref[0][...], last_ref[1][...] = wide[:, :3 * NBLK], wide[:, 3 * NBLK:]
    shape = (NBLK, BLK)
    shifted = grid(shape, 0).astype(f32) - 0.25
    cos, sin = wave(shifted * grid(shape, 1).astype(f32) / TOKENS)
    tw_ref[0][...], tw_ref[1][...] = cos, -sin
    shape = (BLK, BLK)
    cos, sin = wave((grid(shape, 0) * grid(shape, 1)).astype(f32) / BLK)
    mats = jnp.concatenate([jnp.concatenate([cos, -sin], 1), jnp.concatenate([sin, cos], 1)], 0)
    mats_ref[0][...], mats_ref[1][...] = split(mats)


def weights_kernel(pack_ref, small_ref, stack_ref):
    at_out, at_taps, at_rate, at_skip, at_mid, at_in = PACK
    chans = pack_ref.shape[1]
    row = lax.broadcasted_iota(jnp.int32, (CH, chans), 0)
    wanted = second_place(lax.axis_index("ctx")) * 4 + row % 4 + row // 4 * (chans // 2)
    pick = (lax.broadcasted_iota(jnp.int32, (CH, chans), 1) == wanted).astype(f32)

    def stack(weights):
        top, low = split(weights)
        return jnp.concatenate([top, top, low], 1)

    mine = lax.dot_general(pick, pack_ref[:at_mid, :], (((1,), (1,)), ((), ())), precision=highest,
                           preferred_element_type=f32)
    per_turn = 1.0 / (2.0 * math.pi)
    w_in = jnp.concatenate([pack_ref[at_in:at_in + 8, n * UNITS:(n + 1) * UNITS] for n in range(4)]
                           + [pack_ref[at_in:at_in + 1, 4 * UNITS:5 * UNITS]], 0)
    padded = jnp.concatenate([w_in[1:FEAT], w_in[0:1], jnp.zeros((FEAT_PAD - FEAT, UNITS), f32)], 0)
    w_mid = jnp.concatenate([pack_ref[at_mid:at_mid + 8, n * UNITS:(n + 1) * UNITS] for n in range(8)], 0)
    small_ref[:, 0:at_mid] = mine
    stack_ref[0:UNITS, 0:3 * FEAT_PAD] = stack(padded.T * per_turn)
    stack_ref[UNITS:2 * UNITS, 0:3 * UNITS] = stack(w_mid.T * per_turn)
    wide = stack(mine[:, at_out:at_out + UNITS])
    stack_ref[2 * UNITS:2 * UNITS + 2 * CH, 0:3 * UNITS] = jnp.concatenate([wide, wide], 0)


def filter_kernel(small_ref, stack_ref, wide_ref, table_ref, rows_ref):
    at_out, at_taps, at_rate, at_skip, at_mid, at_in = PACK
    spec_ref, tw_ref, par_ref, mats_ref, first_ref, last_ref = views(wide_ref, table_ref)
    fill_tables(first_ref, last_ref, tw_ref, mats_ref)
    w_in = stack_ref[0:UNITS, 0:3 * FEAT_PAD]
    w_mid = stack_ref[UNITS:2 * UNITS, 0:3 * UNITS]
    w_out = stack_ref[2 * UNITS:2 * UNITS + 2 * CH, 0:3 * UNITS]
    taps = [small_ref[:, at_taps + f * 8:at_taps + f * 8 + TAPS] for f in range(3)]
    rate = small_ref[:, at_rate:at_rate + 1]
    skip = small_ref[:, at_skip:at_skip + 1]
    par_ref[...] = jnp.concatenate(taps + [jnp.zeros((CH, 128 - 3 * TAPS), f32)], 1)
    gain = jnp.sqrt(2.0 * rate)

    band = lax.broadcasted_iota(jnp.int32, (BANDS, BLK), 0).astype(f32)
    at = lax.broadcasted_iota(jnp.int32, (BANDS, BLK), 1).astype(f32)
    span = float((BANDS - 1) * (BANDS - 1))
    freq = 1.0 + jnp.floor((band * band * (TOKENS // 4 - 1) + 0.5) * (1.0 / span))
    inner = freq * at * (1.0 / TOKENS)
    inner = inner - jnp.round(inner)
    inner_cos, inner_sin = sine_turns(inner + 0.25), sine_turns(inner)
    outer = freq * at * (1.0 / NBLK)
    outer = outer - jnp.round(outer)
    outer_cos, outer_sin = sine_turns(outer + 0.25), sine_turns(outer)
    ramp_row = lax.broadcasted_iota(jnp.int32, (FEAT_PAD - 2 * BANDS, BLK), 0) == 0
    ramp_at = lax.broadcasted_iota(jnp.int32, (FEAT_PAD - 2 * BANDS, BLK), 1).astype(f32)

    def features(a):
        turn_cos, turn_sin = outer_cos[:, a:a + 1], outer_sin[:, a:a + 1]
        ramp = jnp.where(ramp_row, (ramp_at + float(a * BLK)) * (1.0 / TOKENS), 0.0)
        return jnp.concatenate([inner_cos * turn_cos - inner_sin * turn_sin,
                                inner_sin * turn_cos + inner_cos * turn_sin, ramp], 0)

    lane = lax.broadcasted_iota(jnp.int32, (CH, CHUNK), 1).astype(f32)
    per_chunk = CHUNK // BLK
    for chunk in range(TOKENS // CHUNK):
        feat = jnp.concatenate([features(chunk * per_chunk + n) for n in range(per_chunk)], 1)
        top, low = split(feat)
        one = sine_turns(mm(w_in, jnp.concatenate([top, low, top], 0)))
        top, low = split(one)
        two = sine_turns(mm(w_mid, jnp.concatenate([top, low, top], 0)))
        top, low = split(two)
        shape = mm(w_out, jnp.concatenate([top, low, top], 0))[:CH]
        taper = gain * jnp.exp(-rate * (lane + float(chunk * CHUNK))) * shape
        for n in range(per_chunk):
            first_row = (chunk * per_chunk + n) * CH
            rows_ref[first_row:first_row + CH, :] = taper[:, n * BLK:(n + 1) * BLK]
    spec = forward(rows_ref, first_ref, tw_ref, mats_ref)
    direct = jnp.concatenate([jnp.broadcast_to(skip[c:c + 1], (NBLK, BLK)) for c in range(CH)], 0)
    spec_ref[:, :BLK] = spec[:, :BLK] + direct
    spec_ref[:, BLK:] = spec[:, BLK:]


def conv_kernel(field_ref, wide_ref, table_ref, other_hbm, out_ref, other_ref, query_ref, prod_ref,
                conv_ref, raw_ref, edge_ref, sem):
    swap = pltpu.make_async_copy(other_hbm, other_ref, sem)
    swap.start()
    spec_ref, tw_ref, par_ref, mats_ref, first_ref, last_ref = views(wide_ref, table_ref)
    par = par_ref[...]
    order = second_order()
    sub = lax.broadcasted_iota(jnp.int32, (CH, BLK), 0) < 4
    at_lane = lax.broadcasted_iota(jnp.int32, (CH, BLK), 1)
    raw_ref[0:CH, :] = jnp.zeros((CH, BLK), f32)
    edge_ref[0:CH, :] = jnp.zeros((CH, BLK), f32)
    for quad in range(0, NBLK, 4):
        rows = field_ref[quad * PIECE:(quad + 4) * PIECE, :].astype(f32)
        for pair in range(2):
            five = [rows[pair * 2 * PIECE + n * CH:pair * 2 * PIECE + (n + 1) * CH] for n in range(5)]
            even, odd = order[quad + pair * 2], order[quad + pair * 2 + 1]
            prod_ref[even * CH:(even + 1) * CH, :] = five[0]
            prod_ref[odd * CH:(odd + 1) * CH, :] = pltpu.roll(jnp.where(sub, five[3], five[2]), 4, 0)
            raw_ref[(even + 1) * CH:(even + 2) * CH, :] = five[1]
            raw_ref[(odd + 1) * CH:(odd + 2) * CH, :] = pltpu.roll(jnp.where(sub, five[4], five[3]), 4, 0)
            edge_ref[4 + even * 4:8 + even * 4, :] = five[2][0:4]
            edge_ref[4 + odd * 4:8 + odd * 4, :] = five[4][4:8]

    both_taps = []
    for j in range(TAPS):
        mine = jnp.where(at_lane % HALF < HALF // 2, par[:, TAPS + j:TAPS + j + 1],
                         par[:, 2 * TAPS + j:2 * TAPS + j + 1])
        both_taps.append(jnp.where(sub == (at_lane < HALF), mine, pltpu.roll(mine, 4, 0))[None])
    shape = (NBLK // 2, CH, BLK)
    from_past = lax.broadcasted_iota(jnp.int32, shape, 2) % (HALF // 2) < EDGE
    now = jnp.where(from_past, edge_ref[0:4 * NBLK, :].reshape(shape), edge_ref[4:4 + 4 * NBLK, :].reshape(shape))
    past = pltpu.roll(now, 1, 2)
    total = pltpu.roll(both_taps[6] * now, 2, 2) + (both_taps[4] * now + both_taps[5] * past)
    total = pltpu.roll(total, 2, 2) + (both_taps[2] * now + both_taps[3] * past)
    total = pltpu.roll(total, 2, 2) + (both_taps[0] * now + both_taps[1] * past)
    total = total.astype(bf16).astype(f32)
    total = total * pltpu.roll(total, BLK - HALF // 2, 2)
    left, right = pltpu.roll(total, BLK - EDGE, 2), pltpu.roll(total, BLK - HALF - EDGE, 2)
    subs = lax.broadcasted_iota(jnp.int32, shape, 1) < 4
    fixed = jnp.stack([jnp.where(subs, left, pltpu.roll(right, 4, 1)),
                       jnp.where(subs, pltpu.roll(left, 4, 1), right)], 1).reshape(NBLK * CH, BLK)
    head = lax.broadcasted_iota(jnp.int32, (NBLK * CH, BLK), 1) < EDGE
    prod_ref[...] = jnp.where(head, fixed, prod_ref[...])

    taps = [jnp.broadcast_to(par[:, n:n + 1], (CH, BLK))[None] for n in range(TAPS)]
    span = 8
    lane = lax.broadcasted_iota(jnp.int32, (span + 1, CH, BLK), 2)

    def later(value, steps):
        turned = pltpu.roll(value, steps, 2)
        return jnp.where(lane < steps, jnp.concatenate([turned[:1], turned[:-1]], 0), turned)

    for start in range(0, NBLK, span):
        now = raw_ref[start * CH:(start + span + 1) * CH, :].reshape(span + 1, CH, BLK)
        past = later(now, 1)
        total = later(taps[6] * now, 2) + (taps[4] * now + taps[5] * past)
        total = later(total, 2) + (taps[2] * now + taps[3] * past)
        total = later(total, 2) + (taps[0] * now + taps[1] * past)
        total = total[1:].astype(bf16).astype(f32)
        query_ref[start * CH:(start + span) * CH, :] = total.reshape(span * CH, BLK)
    spec = forward(prod_ref, first_ref, tw_ref, mats_ref)
    s_re, s_im = spec[:, :BLK], spec[:, BLK:]
    h_re, h_im = spec_ref[:, :BLK], spec_ref[:, BLK:]
    both = jnp.concatenate([s_re * h_re - s_im * h_im, -(s_re * h_im + s_im * h_re)], 1)
    back = mm_split(both, mats_ref[0][...], mats_ref[1][...])
    tw_re, tw_im = tw_ref[0][...], tw_ref[1][...]
    cols = []
    for c in range(CH):
        re, im = back[c * NBLK:(c + 1) * NBLK, :BLK], back[c * NBLK:(c + 1) * NBLK, BLK:]
        cols.append(jnp.concatenate([re * tw_re - im * tw_im, -(re * tw_im + im * tw_re)], 0))
    top, low = split(jnp.concatenate(cols, 1))
    last = jnp.concatenate([last_ref[0][...], last_ref[1][...]], 1)
    conv = mm(last, jnp.concatenate([top, low, top], 0))
    for c in range(CH):
        conv_ref[pl.ds(c, NBLK, stride=CH), :] = conv[:, c * BLK:(c + 1) * BLK]
    same = sub == (at_lane < HALF)
    lane = lax.broadcasted_iota(jnp.int32, (BLK, BLK), 1)
    slot = lane % HALF // SHARE
    token = lane // HALF * SHARE + (slot ^ slot // 2) * (2 * SHARE) + lane % SHARE
    reorder = (lax.broadcasted_iota(jnp.int32, (BLK, BLK), 0) == token).astype(f32).astype(bf16)

    for slot in range(0, NBLK, 8):
        gated = []
        for ctx in order[slot:slot + 8]:
            rows = slice(ctx * CH, (ctx + 1) * CH)
            gated.append(query_ref[rows, :] * conv_ref[rows, :])
        gated = mm(jnp.concatenate(gated, 0).astype(bf16), reorder)
        tops, lows = [], []
        for n in range(0, 8, 2):
            pair = []
            for at in (n * CH, (n + 1) * CH):
                rows = gated[at:at + CH]
                pair.append(jnp.where(same, rows, pltpu.roll(pltpu.roll(rows, 4, 0), HALF, 1)))
            tops.append(jnp.where(sub, pair[0], pltpu.roll(pair[1], 4, 0)))
            lows.append(jnp.where(sub, pltpu.roll(pair[0], 4, 0), pair[1]))
        at = slot * 4
        out_ref[at:at + 32, :] = jnp.concatenate(tops, 0).astype(bf16)
        out_ref[at + NBLK * 4:at + NBLK * 4 + 32, :] = jnp.concatenate(lows, 0).astype(bf16)
    swap.wait()


def project_kernel(rows_ref, own_ref, other_ref, out_ref):
    core = lax.axis_index("ch") % 2
    depth = rows_ref.shape[0] // 2

    def turned(part):
        rows = rows_ref[pl.ds(pl.multiple_of(part * depth, depth), depth), :]
        return rows.astype(f32).T.astype(bf16)

    own, other = turned(core), turned(1 - core)
    total = mm(own[:HALF], own_ref[:depth, :]) + mm(own[HALF:], own_ref[depth:, :])
    total = total + mm(other[:HALF], other_ref[:depth, :]) + mm(other[HALF:], other_ref[depth:, :])
    out_ref[...] = total.astype(bf16)


def per_device(query_field, key_field, value_field, short_taps, filt_in, filt_mid, filt_out,
               decay_rate, skip_gain, out_weight):
    chans = query_field.shape[1]
    cores = 2
    groups = lax.axis_size("ch")
    chips = groups // cores
    dout = out_weight.shape[1]
    params = pltpu.CompilerParams(vmem_limit_bytes=32 * 1024 * 1024)
    far = pl.BlockSpec(memory_space=pltpu.HBM)
    operands = (query_field, key_field, value_field, filt_in, filt_mid, filt_out, short_taps,
                decay_rate.reshape(1, chans), skip_gain.reshape(1, chans))
    parts, pack = pl.pallas_call(
        prep_kernel,
        out_shape=[jax.ShapeDtypeStruct((NBLK * PIECE, BLK), bf16),
                   jax.ShapeDtypeStruct((PACK_ROWS, chans), f32)],
        in_specs=[far] * len(operands),
        scratch_shapes=[pltpu.VMEM((3,) + query_field.shape, bf16)]
        + [pltpu.VMEM(t.shape, t.dtype) for t in operands[3:]]
        + [pltpu.VMEM((2 * chans // BLK, 8 + BLK, BLK), f32), pltpu.VMEM((BLK, chans // 2), f32),
           pltpu.SemaphoreType.DMA((len(operands),))],
        compiler_params=pltpu.CompilerParams(vmem_limit_bytes=62 * 1024 * 1024),
        name="prep",
    )(*operands)
    fields = lax.all_to_all(parts.reshape(NBLK, PIECE // 4, 4, BLK), "ctx", 0, 0, tiled=True,
                            axis_index_groups=[second_order()]).reshape(NBLK * PIECE, BLK)
    small, stack = pl.pallas_call(
        weights_kernel,
        out_shape=[jax.ShapeDtypeStruct((CH, 128), f32),
                   jax.ShapeDtypeStruct((2 * UNITS + 2 * CH, 2 * BLK), bf16)],
        compiler_params=params,
        name="weights",
    )(pack)
    own_weight, small = lax.optimization_barrier((out_weight, small))
    other_weight = lax.ppermute(own_weight, "ch", [(d, d ^ 1) for d in range(groups)])
    wide, table = pl.pallas_call(
        filter_kernel,
        out_shape=[jax.ShapeDtypeStruct((CH * NBLK + NBLK + CH, 2 * BLK), f32),
                   jax.ShapeDtypeStruct((4 * BLK + 2 * BLK, 2 * BLK), bf16)],
        scratch_shapes=[pltpu.VMEM((NBLK * CH, BLK), f32)],
        compiler_params=params,
        cost_estimate=pl.CostEstimate(flops=10**11, bytes_accessed=10**9, transcendentals=10**6),
        name="filter",
    )(small, stack)
    gated, other_weight = pl.pallas_call(
        conv_kernel,
        out_shape=[jax.ShapeDtypeStruct((NBLK * CH, BLK), bf16),
                   jax.ShapeDtypeStruct(out_weight.shape, bf16)],
        in_specs=[pl.BlockSpec(memory_space=pltpu.VMEM)] * 3 + [far],
        scratch_shapes=[pltpu.VMEM((NBLK * CH, BLK), f32)] * 3
        + [pltpu.VMEM(((NBLK + 1) * CH, BLK), f32), pltpu.VMEM((4 * NBLK + CH, BLK), f32),
           pltpu.SemaphoreType.DMA],
        compiler_params=params,
        name="convolve",
    )(fields, wide, table, other_weight)
    on_chip = [[c * groups + x * cores + k for k in range(cores) for c in second_order()] for x in range(chips)]
    returned = lax.all_to_all(gated.reshape(NBLK * cores, CH // cores, BLK), ("ctx", "ch"), 0, 0,
                              tiled=True, axis_index_groups=on_chip)
    partial = pl.pallas_call(
        project_kernel,
        out_shape=jax.ShapeDtypeStruct((BLK // cores, dout), bf16),
        compiler_params=params,
        name="project",
    )(returned.reshape(NBLK * CH, BLK), own_weight, other_weight)
    along_x = [[(x ^ x // 2) * cores + k for x in range(chips)] for k in range(cores)]
    shares = lax.all_to_all(partial.reshape(chips, SHARE, dout), "ch", 0, 0, tiled=True,
                            axis_index_groups=along_x)
    return jnp.sum(shares.astype(f32), 0).astype(bf16)


def solution(mesh):
    return jax.shard_map(
        per_device,
        mesh=mesh,
        in_specs=(
            P("ctx", "ch"),
            P("ctx", "ch"),
            P("ctx", "ch"),
            P(None, None, "ch"),
            P(),
            P(),
            P(None, "ch"),
            P("ch"),
            P("ch"),
            P("ch", None),
        ),
        out_specs=P(("ctx", "ch"), None),
        check_vma=False,
    )
```

```python
import math

import jax
import jax.numpy as jnp
import numpy as np
from jax import lax
from jax.experimental import pallas as pl
from jax.experimental.pallas import tpu as pltpu
from jax.sharding import PartitionSpec as P

TOKENS = 8192
BLK = 128
NBLK = 64
CH = 8
BANDS = 16
FEAT = 33
FEAT_PAD = 48
HALF = 64
SHARE = 16
TAPS = 7
EDGE = TAPS - 1
PIECE = 20
FIRST = 13
SECOND = 11
UNITS = 64
CHUNK = 4096
PACK = (0, 64, 88, 96, 104, 112)
PACK_ROWS = 120
bf16 = jnp.bfloat16
f32 = jnp.float32
highest = lax.Precision.HIGHEST


def first_order():
    return [FIRST * n % NBLK for n in range(NBLK)]


def second_order():
    return [SECOND * n % NBLK for n in range(NBLK)]


def second_place(ctx):
    return pow(SECOND, -1, NBLK) * ctx % NBLK


def sine_coefs():
    grid = 0.25 * np.cos((np.arange(400) + 0.5) * math.pi / 400)
    grid = np.concatenate([grid, 0.5 * np.cos((np.arange(800) + 0.5) * math.pi / 800)])
    grid = grid[np.abs(grid) > 1e-3]
    powers = np.stack([grid ** (2 * k + 1) for k in range(7)], 1)
    coef, *_ = np.linalg.lstsq(powers, np.sin(2.0 * math.pi * grid), rcond=None)
    return [float(c) for c in coef]


SINE = sine_coefs()
NEAREST = 1.5 * 2.0**23


def sine_turns(turns):
    rest = turns - ((turns + NEAREST) - NEAREST)
    sq = rest * rest
    acc = sq * SINE[-1] + SINE[-2]
    for c in SINE[-3::-1]:
        acc = acc * sq + c
    return acc * rest


def split(value):
    top = value.astype(bf16)
    return top, (value - top.astype(f32)).astype(bf16)


def mm(left, right):
    return jnp.dot(left, right, preferred_element_type=f32)


def prep_kernel(query_hbm, key_hbm, value_hbm, w_in_hbm, w_mid_hbm, w_out_hbm, taps_hbm, rate_hbm,
                skip_hbm, out_ref, pack_ref, held, w_in_ref, w_mid_ref, w_out_ref, taps_ref, rate_ref,
                skip_ref, lead_ref, edge_ref, sems):
    sources = (taps_hbm, key_hbm, value_hbm, query_hbm, w_out_hbm, w_mid_hbm, w_in_hbm, rate_hbm, skip_hbm)
    targets = (taps_ref, held.at[1], held.at[2], held.at[0], w_out_ref, w_mid_ref, w_in_ref, rate_ref, skip_ref)
    copies = [pltpu.make_async_copy(src, dst, sems.at[n])
              for n, (src, dst) in enumerate(zip(sources, targets))]
    for copy in copies:
        copy.start()
    low_half = lax.broadcasted_iota(jnp.int32, (NBLK // 2, CH, BLK), 1) < 4
    half = edge_ref.shape[1]
    edge_ref[...] = jnp.zeros_like(edge_ref)
    copies[0].wait()
    mixed = []
    blocks = range(2 * half // BLK)
    for f in (1, 2):
        copies[f].wait()
        parts = []
        for n in blocks:
            lead = lead_ref.at[(f - 1) * len(blocks) + n]
            lanes = slice(n * BLK, (n + 1) * BLK)
            lead[0:8, :] = jnp.zeros((8, BLK), f32)
            lead[8:8 + BLK, :] = held[f, :, lanes].astype(f32)
            total = taps_ref[f, 0:1, lanes] * lead[8:8 + BLK, :]
            for j in range(1, TAPS):
                total = total + taps_ref[f, j:j + 1, lanes] * lead[8 - j:8 - j + BLK, :]
            parts.append(total.astype(bf16).astype(f32))
            at = n * BLK // half * HALF + (f - 1) * (HALF // 2)
            lanes = slice(n * BLK % half, n * BLK % half + BLK)
            edge_ref[at:at + EDGE, lanes] = lead[8 + BLK - EDGE:8 + BLK, :]
            edge_ref[at + EDGE:at + 2 * EDGE, lanes] = lead[8:8 + EDGE, :]
        mixed.append(jnp.concatenate(parts, 1))

    def pairs(field):
        rows = field.T.reshape(2, NBLK // 2, CH, BLK)
        up = pltpu.roll(rows[1], 4, 1)
        return jnp.where(low_half, rows[0], up), jnp.where(low_half, up, rows[0])

    prod_even, prod_odd = pairs(mixed[0] * mixed[1])
    copies[3].wait()
    query_even, query_odd = pairs(held[0].astype(f32))
    edges = edge_ref[...].T.reshape(NBLK // 2, CH, BLK)
    low = low_half[0]
    places = [second_place(ctx) for ctx in first_order()]
    for slot in range(0, NBLK, 4):
        rows = []
        for n in (slot, slot + 2):
            even, odd = places[n] // 2, places[n + 1] // 2
            rows += [prod_even[even], query_even[even], jnp.where(low, edges[even], prod_odd[odd]),
                     jnp.where(low, prod_odd[odd], query_odd[odd]), jnp.where(low, query_odd[odd], edges[odd])]
        out_ref[slot * PIECE:(slot + 4) * PIECE, :] = jnp.concatenate(rows, 0).astype(bf16)
    for copy in copies[4:]:
        copy.wait()
    chans = rate_ref.shape[1]
    at_out, at_taps, at_rate, at_skip, at_mid, at_in = PACK
    pack_ref[at_out:at_out + UNITS, :] = w_out_ref[...]
    for f in range(3):
        pack_ref[at_taps + f * 8:at_taps + f * 8 + TAPS, :] = taps_ref[f]
    pack_ref[at_rate:at_rate + 8, :] = jnp.broadcast_to(rate_ref[...], (8, chans))
    pack_ref[at_skip:at_skip + 8, :] = jnp.broadcast_to(skip_ref[...], (8, chans))
    for n in range(8):
        pack_ref[at_mid:at_mid + 8, n * UNITS:(n + 1) * UNITS] = w_mid_ref[n * 8:(n + 1) * 8, :]
    for n in range(4):
        pack_ref[at_in:at_in + 8, n * UNITS:(n + 1) * UNITS] = w_in_ref[n * 8:(n + 1) * 8, :]
    pack_ref[at_in:at_in + 1, 4 * UNITS:5 * UNITS] = w_in_ref[FEAT - 1:FEAT, :]


def forward(rows_ref, first_ref, tw_ref, mats_ref):
    cols = jnp.concatenate([rows_ref[pl.ds(c, NBLK, stride=CH), :] for c in range(CH)], 1)
    top, low = split(cols)
    outer = mm(first_ref[...], jnp.concatenate([top, low, top], 0))
    tw_re, tw_im = tw_ref[0][...], tw_ref[1][...]
    out = []
    for c in range(CH):
        lanes = slice(c * BLK, (c + 1) * BLK)
        re, im = outer[:NBLK, lanes], outer[NBLK:, lanes]
        out.append(jnp.concatenate([re * tw_re - im * tw_im, re * tw_im + im * tw_re], 1))
    return mm(jnp.concatenate(out, 0).astype(bf16), mats_ref[...])


def views(wide_ref, table_ref):
    half = 2 * BLK
    spec = wide_ref.at[0:CH * NBLK]
    tw = [wide_ref.at[CH * NBLK:CH * NBLK + NBLK, n * BLK:(n + 1) * BLK] for n in range(2)]
    par = wide_ref.at[CH * NBLK + NBLK:CH * NBLK + NBLK + CH, 0:BLK]
    mats = table_ref.at[0:half]
    first = table_ref.at[half:half + BLK, 0:3 * NBLK]
    last = [table_ref.at[half + BLK + n * NBLK:half + BLK + (n + 1) * NBLK, 0:3 * NBLK]
            for n in range(2)]
    return spec, tw, par, mats, first, last


def fill_tables(first_ref, last_ref, tw_ref, mats_ref):
    def grid(shape, axis):
        return lax.broadcasted_iota(jnp.int32, shape, axis)

    def wave(turns):
        turns = turns - jnp.round(turns)
        return sine_turns(turns + 0.25), sine_turns(turns)

    shape = (NBLK, NBLK)
    cos, sin = wave((grid(shape, 0).astype(f32) - 0.25) * grid(shape, 1).astype(f32) / NBLK)
    top, low = split(jnp.concatenate([cos, -sin], 0))
    first_ref[...] = jnp.concatenate([top, top, low], 1)
    cos, sin = wave((grid(shape, 1).astype(f32) - 0.25) * grid(shape, 0).astype(f32) / NBLK)
    top, low = split(jnp.concatenate([cos, -sin], 1) / TOKENS)
    wide = jnp.concatenate([top, top, low], 1)
    last_ref[0][...], last_ref[1][...] = wide[:, :3 * NBLK], wide[:, 3 * NBLK:]
    shape = (NBLK, BLK)
    shifted = grid(shape, 0).astype(f32) - 0.25
    cos, sin = wave(shifted * grid(shape, 1).astype(f32) / TOKENS)
    tw_ref[0][...], tw_ref[1][...] = cos, -sin
    shape = (BLK, BLK)
    cos, sin = wave((grid(shape, 0) * grid(shape, 1)).astype(f32) / BLK)
    mats = jnp.concatenate([jnp.concatenate([cos, -sin], 1), jnp.concatenate([sin, cos], 1)], 0)
    mats_ref[...] = mats.astype(bf16)


def weights_kernel(pack_ref, small_ref, stack_ref):
    at_out, at_taps, at_rate, at_skip, at_mid, at_in = PACK
    chans = pack_ref.shape[1]
    row = lax.broadcasted_iota(jnp.int32, (CH, chans), 0)
    wanted = second_place(lax.axis_index("ctx")) * 4 + row % 4 + row // 4 * (chans // 2)
    pick = (lax.broadcasted_iota(jnp.int32, (CH, chans), 1) == wanted).astype(f32)

    def stack(weights):
        top, low = split(weights)
        return jnp.concatenate([top, top, low], 1)

    mine = lax.dot_general(pick, pack_ref[:at_mid, :], (((1,), (1,)), ((), ())), precision=highest,
                           preferred_element_type=f32)
    per_turn = 1.0 / (2.0 * math.pi)
    w_in = jnp.concatenate([pack_ref[at_in:at_in + 8, n * UNITS:(n + 1) * UNITS] for n in range(4)]
                           + [pack_ref[at_in:at_in + 1, 4 * UNITS:5 * UNITS]], 0)
    padded = jnp.concatenate([w_in[1:FEAT], w_in[0:1], jnp.zeros((FEAT_PAD - FEAT, UNITS), f32)], 0)
    w_mid = jnp.concatenate([pack_ref[at_mid:at_mid + 8, n * UNITS:(n + 1) * UNITS] for n in range(8)], 0)
    small_ref[:, 0:at_mid] = mine
    stack_ref[0:UNITS, 0:3 * FEAT_PAD] = stack(padded.T * per_turn)
    stack_ref[UNITS:2 * UNITS, 0:3 * UNITS] = stack(w_mid.T * per_turn)
    wide = stack(mine[:, at_out:at_out + UNITS])
    stack_ref[2 * UNITS:2 * UNITS + 2 * CH, 0:3 * UNITS] = jnp.concatenate([wide, wide], 0)


def filter_kernel(small_ref, stack_ref, wide_ref, table_ref, rows_ref):
    at_out, at_taps, at_rate, at_skip, at_mid, at_in = PACK
    spec_ref, tw_ref, par_ref, mats_ref, first_ref, last_ref = views(wide_ref, table_ref)
    fill_tables(first_ref, last_ref, tw_ref, mats_ref)
    w_in = stack_ref[0:UNITS, 0:3 * FEAT_PAD]
    w_mid = stack_ref[UNITS:2 * UNITS, 0:3 * UNITS]
    w_out = stack_ref[2 * UNITS:2 * UNITS + 2 * CH, 0:3 * UNITS]
    taps = [small_ref[:, at_taps + f * 8:at_taps + f * 8 + TAPS] for f in range(3)]
    rate = small_ref[:, at_rate:at_rate + 1]
    skip = small_ref[:, at_skip:at_skip + 1]
    par_ref[...] = jnp.concatenate(taps + [jnp.zeros((CH, 128 - 3 * TAPS), f32)], 1)
    gain = jnp.sqrt(2.0 * rate)

    band = lax.broadcasted_iota(jnp.int32, (BANDS, BLK), 0).astype(f32)
    at = lax.broadcasted_iota(jnp.int32, (BANDS, BLK), 1).astype(f32)
    span = float((BANDS - 1) * (BANDS - 1))
    freq = 1.0 + jnp.floor((band * band * (TOKENS // 4 - 1) + 0.5) * (1.0 / span))
    inner = freq * at * (1.0 / TOKENS)
    inner = inner - jnp.round(inner)
    inner_cos, inner_sin = sine_turns(inner + 0.25), sine_turns(inner)
    outer = freq * at * (1.0 / NBLK)
    outer = outer - jnp.round(outer)
    outer_cos, outer_sin = sine_turns(outer + 0.25), sine_turns(outer)
    ramp_row = lax.broadcasted_iota(jnp.int32, (FEAT_PAD - 2 * BANDS, BLK), 0) == 0
    ramp_at = lax.broadcasted_iota(jnp.int32, (FEAT_PAD - 2 * BANDS, BLK), 1).astype(f32)

    def features(a):
        turn_cos, turn_sin = outer_cos[:, a:a + 1], outer_sin[:, a:a + 1]
        ramp = jnp.where(ramp_row, (ramp_at + float(a * BLK)) * (1.0 / TOKENS), 0.0)
        return jnp.concatenate([inner_cos * turn_cos - inner_sin * turn_sin,
                                inner_sin * turn_cos + inner_cos * turn_sin, ramp], 0)

    lane = lax.broadcasted_iota(jnp.int32, (CH, CHUNK), 1).astype(f32)
    per_chunk = CHUNK // BLK
    for chunk in range(TOKENS // CHUNK):
        feat = jnp.concatenate([features(chunk * per_chunk + n) for n in range(per_chunk)], 1)
        top, low = split(feat)
        one = sine_turns(mm(w_in, jnp.concatenate([top, low, top], 0)))
        top, low = split(one)
        two = sine_turns(mm(w_mid, jnp.concatenate([top, low, top], 0)))
        top = two.astype(bf16)
        shape = mm(jnp.concatenate([w_out[:CH, :UNITS], w_out[CH:, 2 * UNITS:]], 0), top)
        shape = shape[:CH] + shape[CH:]
        taper = gain * jnp.exp(-rate * (lane + float(chunk * CHUNK))) * shape
        for n in range(per_chunk):
            first_row = (chunk * per_chunk + n) * CH
            rows_ref[first_row:first_row + CH, :] = taper[:, n * BLK:(n + 1) * BLK]
    spec = forward(rows_ref, first_ref, tw_ref, mats_ref)
    direct = jnp.concatenate([jnp.broadcast_to(skip[c:c + 1], (NBLK, BLK)) for c in range(CH)], 0)
    spec_ref[:, :BLK] = spec[:, :BLK] + direct
    spec_ref[:, BLK:] = spec[:, BLK:]


def conv_kernel(field_ref, wide_ref, table_ref, other_hbm, out_ref, other_ref, query_ref, prod_ref,
                conv_ref, raw_ref, edge_ref, sem):
    swap = pltpu.make_async_copy(other_hbm, other_ref, sem)
    swap.start()
    spec_ref, tw_ref, par_ref, mats_ref, first_ref, last_ref = views(wide_ref, table_ref)
    par = par_ref[...]
    order = first_order()
    sub = lax.broadcasted_iota(jnp.int32, (CH, BLK), 0) < 4
    at_lane = lax.broadcasted_iota(jnp.int32, (CH, BLK), 1)
    raw_ref[0:CH, :] = jnp.zeros((CH, BLK), f32)
    edge_ref[0:CH, :] = jnp.zeros((CH, BLK), f32)
    for quad in range(0, NBLK, 4):
        rows = field_ref[quad * PIECE:(quad + 4) * PIECE, :].astype(f32)
        for pair in range(2):
            five = [rows[pair * 2 * PIECE + n * CH:pair * 2 * PIECE + (n + 1) * CH] for n in range(5)]
            even, odd = order[quad + pair * 2], order[quad + pair * 2 + 1]
            prod_ref[even * CH:(even + 1) * CH, :] = five[0]
            prod_ref[odd * CH:(odd + 1) * CH, :] = pltpu.roll(jnp.where(sub, five[3], five[2]), 4, 0)
            raw_ref[(even + 1) * CH:(even + 2) * CH, :] = five[1]
            raw_ref[(odd + 1) * CH:(odd + 2) * CH, :] = pltpu.roll(jnp.where(sub, five[4], five[3]), 4, 0)
            edge_ref[4 + even * 4:8 + even * 4, :] = five[2][0:4]
            edge_ref[4 + odd * 4:8 + odd * 4, :] = five[4][4:8]

    both_taps = []
    for j in range(TAPS):
        mine = jnp.where(at_lane % HALF < HALF // 2, par[:, TAPS + j:TAPS + j + 1],
                         par[:, 2 * TAPS + j:2 * TAPS + j + 1])
        both_taps.append(jnp.where(sub == (at_lane < HALF), mine, pltpu.roll(mine, 4, 0))[None])
    shape = (NBLK // 2, CH, BLK)
    from_past = lax.broadcasted_iota(jnp.int32, shape, 2) % (HALF // 2) < EDGE
    now = jnp.where(from_past, edge_ref[0:4 * NBLK, :].reshape(shape), edge_ref[4:4 + 4 * NBLK, :].reshape(shape))
    past = pltpu.roll(now, 1, 2)
    total = pltpu.roll(both_taps[6] * now, 2, 2) + (both_taps[4] * now + both_taps[5] * past)
    total = pltpu.roll(total, 2, 2) + (both_taps[2] * now + both_taps[3] * past)
    total = pltpu.roll(total, 2, 2) + (both_taps[0] * now + both_taps[1] * past)
    total = total.astype(bf16).astype(f32)
    total = total * pltpu.roll(total, BLK - HALF // 2, 2)
    left, right = pltpu.roll(total, BLK - EDGE, 2), pltpu.roll(total, BLK - HALF - EDGE, 2)
    subs = lax.broadcasted_iota(jnp.int32, shape, 1) < 4
    fixed = jnp.stack([jnp.where(subs, left, pltpu.roll(right, 4, 1)),
                       jnp.where(subs, pltpu.roll(left, 4, 1), right)], 1).reshape(NBLK * CH, BLK)
    head = lax.broadcasted_iota(jnp.int32, (NBLK * CH, BLK), 1) < EDGE
    prod_ref[...] = jnp.where(head, fixed, prod_ref[...])

    taps = [jnp.broadcast_to(par[:, n:n + 1], (CH, BLK))[None] for n in range(TAPS)]
    span = 8
    lane = lax.broadcasted_iota(jnp.int32, (span + 1, CH, BLK), 2)

    def later(value, steps):
        turned = pltpu.roll(value, steps, 2)
        return jnp.where(lane < steps, jnp.concatenate([turned[:1], turned[:-1]], 0), turned)

    for start in range(0, NBLK, span):
        now = raw_ref[start * CH:(start + span + 1) * CH, :].reshape(span + 1, CH, BLK)
        past = later(now, 1)
        total = later(taps[6] * now, 2) + (taps[4] * now + taps[5] * past)
        total = later(total, 2) + (taps[2] * now + taps[3] * past)
        total = later(total, 2) + (taps[0] * now + taps[1] * past)
        total = total[1:].astype(bf16).astype(f32)
        query_ref[start * CH:(start + span) * CH, :] = total.reshape(span * CH, BLK)
    spec = forward(prod_ref, first_ref, tw_ref, mats_ref)
    s_re, s_im = spec[:, :BLK], spec[:, BLK:]
    h_re, h_im = spec_ref[:, :BLK], spec_ref[:, BLK:]
    both = jnp.concatenate([s_re * h_re - s_im * h_im, -(s_re * h_im + s_im * h_re)], 1)
    back = mm(both.astype(bf16), mats_ref[...])
    tw_re, tw_im = tw_ref[0][...], tw_ref[1][...]
    cols = []
    for c in range(CH):
        re, im = back[c * NBLK:(c + 1) * NBLK, :BLK], back[c * NBLK:(c + 1) * NBLK, BLK:]
        cols.append(jnp.concatenate([re * tw_re - im * tw_im, -(re * tw_im + im * tw_re)], 0))
    top, low = split(jnp.concatenate(cols, 1))
    last = jnp.concatenate([last_ref[0][...], last_ref[1][...]], 1)
    conv = mm(last, jnp.concatenate([top, low, top], 0))
    for c in range(CH):
        conv_ref[pl.ds(c, NBLK, stride=CH), :] = conv[:, c * BLK:(c + 1) * BLK]
    order = second_order()
    same = sub == (at_lane < HALF)
    lane = lax.broadcasted_iota(jnp.int32, (BLK, BLK), 1)
    slot = lane % HALF // SHARE
    token = lane // HALF * SHARE + (slot ^ slot // 2) * (2 * SHARE) + lane % SHARE
    reorder = (lax.broadcasted_iota(jnp.int32, (BLK, BLK), 0) == token).astype(f32).astype(bf16)

    for slot in range(0, NBLK, 8):
        gated = []
        for ctx in order[slot:slot + 8]:
            rows = slice(ctx * CH, (ctx + 1) * CH)
            gated.append(query_ref[rows, :] * conv_ref[rows, :])
        gated = mm(jnp.concatenate(gated, 0).astype(bf16), reorder)
        tops, lows = [], []
        for n in range(0, 8, 2):
            pair = []
            for at in (n * CH, (n + 1) * CH):
                rows = gated[at:at + CH]
                pair.append(jnp.where(same, rows, pltpu.roll(pltpu.roll(rows, 4, 0), HALF, 1)))
            tops.append(jnp.where(sub, pair[0], pltpu.roll(pair[1], 4, 0)))
            lows.append(jnp.where(sub, pltpu.roll(pair[0], 4, 0), pair[1]))
        at = slot * 4
        out_ref[at:at + 32, :] = jnp.concatenate(tops, 0).astype(bf16)
        out_ref[at + NBLK * 4:at + NBLK * 4 + 32, :] = jnp.concatenate(lows, 0).astype(bf16)
    swap.wait()


def project_kernel(rows_ref, own_ref, other_ref, out_ref):
    core = lax.axis_index("ch") % 2
    depth = rows_ref.shape[0] // 2

    def turned(part):
        rows = rows_ref[pl.ds(pl.multiple_of(part * depth, depth), depth), :]
        return rows.astype(f32).T.astype(bf16)

    own, other = turned(core), turned(1 - core)
    total = mm(own[:HALF], own_ref[:depth, :]) + mm(own[HALF:], own_ref[depth:, :])
    total = total + mm(other[:HALF], other_ref[:depth, :]) + mm(other[HALF:], other_ref[depth:, :])
    out_ref[...] = total.astype(bf16)


def per_device(query_field, key_field, value_field, short_taps, filt_in, filt_mid, filt_out,
               decay_rate, skip_gain, out_weight):
    chans = query_field.shape[1]
    cores = 2
    groups = lax.axis_size("ch")
    chips = groups // cores
    dout = out_weight.shape[1]
    params = pltpu.CompilerParams(vmem_limit_bytes=32 * 1024 * 1024)
    far = pl.BlockSpec(memory_space=pltpu.HBM)
    operands = (query_field, key_field, value_field, filt_in, filt_mid, filt_out, short_taps,
                decay_rate.reshape(1, chans), skip_gain.reshape(1, chans))
    parts, pack = pl.pallas_call(
        prep_kernel,
        out_shape=[jax.ShapeDtypeStruct((NBLK * PIECE, BLK), bf16),
                   jax.ShapeDtypeStruct((PACK_ROWS, chans), f32)],
        in_specs=[far] * len(operands),
        scratch_shapes=[pltpu.VMEM((3,) + query_field.shape, bf16)]
        + [pltpu.VMEM(t.shape, t.dtype) for t in operands[3:]]
        + [pltpu.VMEM((2 * chans // BLK, 8 + BLK, BLK), f32), pltpu.VMEM((BLK, chans // 2), f32),
           pltpu.SemaphoreType.DMA((len(operands),))],
        compiler_params=pltpu.CompilerParams(vmem_limit_bytes=62 * 1024 * 1024),
        name="prep",
    )(*operands)
    fields = lax.all_to_all(parts.reshape(NBLK, PIECE // 4, 4, BLK), "ctx", 0, 0, tiled=True,
                            axis_index_groups=[first_order()]).reshape(NBLK * PIECE, BLK)
    small, stack = pl.pallas_call(
        weights_kernel,
        out_shape=[jax.ShapeDtypeStruct((CH, 128), f32),
                   jax.ShapeDtypeStruct((2 * UNITS + 2 * CH, 2 * BLK), bf16)],
        compiler_params=params,
        name="weights",
    )(pack)
    own_weight, small = lax.optimization_barrier((out_weight, small))
    other_weight = lax.ppermute(own_weight, "ch", [(d, d ^ 1) for d in range(groups)])
    wide, table = pl.pallas_call(
        filter_kernel,
        out_shape=[jax.ShapeDtypeStruct((CH * NBLK + NBLK + CH, 2 * BLK), f32),
                   jax.ShapeDtypeStruct((4 * BLK, 2 * BLK), bf16)],
        scratch_shapes=[pltpu.VMEM((NBLK * CH, BLK), f32)],
        compiler_params=params,
        cost_estimate=pl.CostEstimate(flops=10**11, bytes_accessed=10**9, transcendentals=10**6),
        name="filter",
    )(small, stack)
    gated, other_weight = pl.pallas_call(
        conv_kernel,
        out_shape=[jax.ShapeDtypeStruct((NBLK * CH, BLK), bf16),
                   jax.ShapeDtypeStruct(out_weight.shape, bf16)],
        in_specs=[pl.BlockSpec(memory_space=pltpu.VMEM)] * 3 + [far],
        scratch_shapes=[pltpu.VMEM((NBLK * CH, BLK), f32)] * 3
        + [pltpu.VMEM(((NBLK + 1) * CH, BLK), f32), pltpu.VMEM((4 * NBLK + CH, BLK), f32),
           pltpu.SemaphoreType.DMA],
        compiler_params=params,
        name="convolve",
    )(fields, wide, table, other_weight)
    on_chip = [[c * groups + x * cores + k for k in range(cores) for c in second_order()] for x in range(chips)]
    returned = lax.all_to_all(gated.reshape(NBLK * cores, CH // cores, BLK), ("ctx", "ch"), 0, 0,
                              tiled=True, axis_index_groups=on_chip)
    partial = pl.pallas_call(
        project_kernel,
        out_shape=jax.ShapeDtypeStruct((BLK // cores, dout), bf16),
        compiler_params=params,
        name="project",
    )(returned.reshape(NBLK * CH, BLK), own_weight, other_weight)
    along_x = [[(x ^ x // 2) * cores + k for x in range(chips)] for k in range(cores)]
    shares = lax.all_to_all(partial.reshape(chips, SHARE, dout), "ch", 0, 0, tiled=True,
                            axis_index_groups=along_x)
    return jnp.sum(shares.astype(f32), 0).astype(bf16)


def solution(mesh):
    return jax.shard_map(
        per_device,
        mesh=mesh,
        in_specs=(
            P("ctx", "ch"),
            P("ctx", "ch"),
            P("ctx", "ch"),
            P(None, None, "ch"),
            P(),
            P(),
            P(None, "ch"),
            P("ch"),
            P("ch"),
            P("ch", None),
        ),
        out_specs=P(("ctx", "ch"), None),
        check_vma=False,
    )
```

```python
import math

import jax
import jax.numpy as jnp
import numpy as np
from jax import lax
from jax.experimental import pallas as pl
from jax.experimental.pallas import tpu as pltpu
from jax.sharding import PartitionSpec as P

TOKENS = 8192
BLK = 128
NBLK = 64
CH = 8
BANDS = 16
FEAT = 33
FEAT_PAD = 48
HALF = 64
SHARE = 16
TAPS = 7
EDGE = TAPS - 1
PIECE = 20
FIRST = 13
SECOND = 11
UNITS = 64
CHUNK = 4096
PACK = (0, 64, 88, 96, 104, 112)
PACK_ROWS = 120
bf16 = jnp.bfloat16
f32 = jnp.float32
highest = lax.Precision.HIGHEST


def first_order():
    return [FIRST * n % NBLK for n in range(NBLK)]


def second_order():
    return [SECOND * n % NBLK for n in range(NBLK)]


def second_place(ctx):
    return pow(SECOND, -1, NBLK) * ctx % NBLK


def sine_coefs():
    grid = 0.25 * np.cos((np.arange(400) + 0.5) * math.pi / 400)
    grid = np.concatenate([grid, 0.5 * np.cos((np.arange(800) + 0.5) * math.pi / 800)])
    grid = grid[np.abs(grid) > 1e-3]
    powers = np.stack([grid ** (2 * k + 1) for k in range(7)], 1)
    coef, *_ = np.linalg.lstsq(powers, np.sin(2.0 * math.pi * grid), rcond=None)
    return [float(c) for c in coef]


SINE = sine_coefs()
NEAREST = 1.5 * 2.0**23


def sine_turns(turns):
    rest = turns - ((turns + NEAREST) - NEAREST)
    sq = rest * rest
    acc = sq * SINE[-1] + SINE[-2]
    for c in SINE[-3::-1]:
        acc = acc * sq + c
    return acc * rest


def split(value):
    top = value.astype(bf16)
    return top, (value - top.astype(f32)).astype(bf16)


def mm(left, right):
    return jnp.dot(left, right, preferred_element_type=f32)


def prep_kernel(query_hbm, key_hbm, value_hbm, w_in_hbm, w_mid_hbm, w_out_hbm, taps_hbm, rate_hbm,
                skip_hbm, out_ref, pack_ref, held, w_in_ref, w_mid_ref, w_out_ref, taps_ref, rate_ref,
                skip_ref, lead_ref, edge_ref, sems):
    sources = (taps_hbm, key_hbm, value_hbm, query_hbm, w_out_hbm, w_mid_hbm, w_in_hbm, rate_hbm, skip_hbm)
    targets = (taps_ref, held.at[1], held.at[2], held.at[0], w_out_ref, w_mid_ref, w_in_ref, rate_ref, skip_ref)
    copies = [pltpu.make_async_copy(src, dst, sems.at[n])
              for n, (src, dst) in enumerate(zip(sources, targets))]
    for copy in copies:
        copy.start()
    low_half = lax.broadcasted_iota(jnp.int32, (NBLK // 2, CH, BLK), 1) < 4
    half = edge_ref.shape[1]
    edge_ref[...] = jnp.zeros_like(edge_ref)
    copies[0].wait()
    mixed = []
    blocks = range(2 * half // BLK)
    for f in (1, 2):
        copies[f].wait()
        parts = []
        for n in blocks:
            lead = lead_ref.at[(f - 1) * len(blocks) + n]
            lanes = slice(n * BLK, (n + 1) * BLK)
            lead[0:8, :] = jnp.zeros((8, BLK), f32)
            lead[8:8 + BLK, :] = held[f, :, lanes].astype(f32)
            total = taps_ref[f, 0:1, lanes] * lead[8:8 + BLK, :]
            for j in range(1, TAPS):
                total = total + taps_ref[f, j:j + 1, lanes] * lead[8 - j:8 - j + BLK, :]
            parts.append(total.astype(bf16).astype(f32))
            at = n * BLK // half * HALF + (f - 1) * (HALF // 2)
            lanes = slice(n * BLK % half, n * BLK % half + BLK)
            edge_ref[at:at + EDGE, lanes] = lead[8 + BLK - EDGE:8 + BLK, :]
            edge_ref[at + EDGE:at + 2 * EDGE, lanes] = lead[8:8 + EDGE, :]
        mixed.append(jnp.concatenate(parts, 1))

    def pairs(field):
        rows = field.T.reshape(2, NBLK // 2, CH, BLK)
        up = pltpu.roll(rows[1], 4, 1)
        return jnp.where(low_half, rows[0], up), jnp.where(low_half, up, rows[0])

    prod_even, prod_odd = pairs(mixed[0] * mixed[1])
    copies[3].wait()
    query_even, query_odd = pairs(held[0].astype(f32))
    edges = edge_ref[...].T.reshape(NBLK // 2, CH, BLK)
    low = low_half[0]
    places = [second_place(ctx) for ctx in first_order()]
    for slot in range(0, NBLK, 4):
        rows = []
        for n in (slot, slot + 2):
            even, odd = places[n] // 2, places[n + 1] // 2
            rows += [prod_even[even], query_even[even], jnp.where(low, edges[even], prod_odd[odd]),
                     jnp.where(low, prod_odd[odd], query_odd[odd]), jnp.where(low, query_odd[odd], edges[odd])]
        out_ref[slot * PIECE:(slot + 4) * PIECE, :] = jnp.concatenate(rows, 0).astype(bf16)
    for copy in copies[4:]:
        copy.wait()
    chans = rate_ref.shape[1]
    at_out, at_taps, at_rate, at_skip, at_mid, at_in = PACK
    pack_ref[at_out:at_out + UNITS, :] = w_out_ref[...]
    for f in range(3):
        pack_ref[at_taps + f * 8:at_taps + f * 8 + TAPS, :] = taps_ref[f]
    pack_ref[at_rate:at_rate + 8, :] = jnp.broadcast_to(rate_ref[...], (8, chans))
    pack_ref[at_skip:at_skip + 8, :] = jnp.broadcast_to(skip_ref[...], (8, chans))
    for n in range(8):
        pack_ref[at_mid:at_mid + 8, n * UNITS:(n + 1) * UNITS] = w_mid_ref[n * 8:(n + 1) * 8, :]
    for n in range(4):
        pack_ref[at_in:at_in + 8, n * UNITS:(n + 1) * UNITS] = w_in_ref[n * 8:(n + 1) * 8, :]
    pack_ref[at_in:at_in + 1, 4 * UNITS:5 * UNITS] = w_in_ref[FEAT - 1:FEAT, :]


def forward(rows_ref, first_ref, tw_ref, mats_ref):
    cols = jnp.concatenate([rows_ref[pl.ds(c, NBLK, stride=CH), :] for c in range(CH)], 1)
    top = cols.astype(bf16)
    outer = mm(first_ref[...], jnp.concatenate([top, top], 0))
    tw_re, tw_im = tw_ref[0][...], tw_ref[1][...]
    out = []
    for c in range(CH):
        lanes = slice(c * BLK, (c + 1) * BLK)
        re, im = outer[:NBLK, lanes], outer[NBLK:, lanes]
        out.append(jnp.concatenate([re * tw_re - im * tw_im, re * tw_im + im * tw_re], 1))
    return mm(jnp.concatenate(out, 0).astype(bf16), mats_ref[...])


def views(wide_ref, table_ref):
    half = 2 * BLK
    spec = wide_ref.at[0:CH * NBLK]
    tw = [wide_ref.at[CH * NBLK:CH * NBLK + NBLK, n * BLK:(n + 1) * BLK] for n in range(2)]
    par = wide_ref.at[CH * NBLK + NBLK:CH * NBLK + NBLK + CH, 0:BLK]
    mats = table_ref.at[0:half]
    first = table_ref.at[half:half + BLK, 0:2 * NBLK]
    last = table_ref.at[half + BLK:half + BLK + NBLK, 0:4 * NBLK]
    return spec, tw, par, mats, first, last


def fill_tables(first_ref, last_ref, tw_ref, mats_ref):
    def grid(shape, axis):
        return lax.broadcasted_iota(jnp.int32, shape, axis)

    def wave(turns):
        turns = turns - jnp.round(turns)
        return sine_turns(turns + 0.25), sine_turns(turns)

    shape = (NBLK, NBLK)
    cos, sin = wave((grid(shape, 0).astype(f32) - 0.25) * grid(shape, 1).astype(f32) / NBLK)
    top, low = split(jnp.concatenate([cos, -sin], 0))
    first_ref[...] = jnp.concatenate([top, low], 1)
    cos, sin = wave((grid(shape, 1).astype(f32) - 0.25) * grid(shape, 0).astype(f32) / NBLK)
    top, low = split(jnp.concatenate([cos, -sin], 1) / TOKENS)
    last_ref[...] = jnp.concatenate([top, low], 1)
    shape = (NBLK, BLK)
    shifted = grid(shape, 0).astype(f32) - 0.25
    cos, sin = wave(shifted * grid(shape, 1).astype(f32) / TOKENS)
    tw_ref[0][...], tw_ref[1][...] = cos, -sin
    shape = (BLK, BLK)
    cos, sin = wave((grid(shape, 0) * grid(shape, 1)).astype(f32) / BLK)
    mats = jnp.concatenate([jnp.concatenate([cos, -sin], 1), jnp.concatenate([sin, cos], 1)], 0)
    mats_ref[...] = mats.astype(bf16)


def weights_kernel(pack_ref, small_ref, stack_ref):
    at_out, at_taps, at_rate, at_skip, at_mid, at_in = PACK
    chans = pack_ref.shape[1]
    row = lax.broadcasted_iota(jnp.int32, (CH, chans), 0)
    wanted = second_place(lax.axis_index("ctx")) * 4 + row % 4 + row // 4 * (chans // 2)
    pick = (lax.broadcasted_iota(jnp.int32, (CH, chans), 1) == wanted).astype(f32)

    def stack(weights):
        top, low = split(weights)
        return jnp.concatenate([top, top, low], 1)

    mine = lax.dot_general(pick, pack_ref[:at_mid, :], (((1,), (1,)), ((), ())), precision=highest,
                           preferred_element_type=f32)
    per_turn = 1.0 / (2.0 * math.pi)
    w_in = jnp.concatenate([pack_ref[at_in:at_in + 8, n * UNITS:(n + 1) * UNITS] for n in range(4)]
                           + [pack_ref[at_in:at_in + 1, 4 * UNITS:5 * UNITS]], 0)
    padded = jnp.concatenate([w_in[1:FEAT], w_in[0:1], jnp.zeros((FEAT_PAD - FEAT, UNITS), f32)], 0)
    w_mid = jnp.concatenate([pack_ref[at_mid:at_mid + 8, n * UNITS:(n + 1) * UNITS] for n in range(8)], 0)
    small_ref[:, 0:at_mid] = mine
    stack_ref[0:UNITS, 0:3 * FEAT_PAD] = stack(padded.T * per_turn)
    stack_ref[UNITS:2 * UNITS, 0:3 * UNITS] = stack(w_mid.T * per_turn)
    wide = stack(mine[:, at_out:at_out + UNITS])
    stack_ref[2 * UNITS:2 * UNITS + 2 * CH, 0:3 * UNITS] = jnp.concatenate([wide, wide], 0)


def filter_kernel(small_ref, stack_ref, wide_ref, table_ref, rows_ref):
    at_out, at_taps, at_rate, at_skip, at_mid, at_in = PACK
    spec_ref, tw_ref, par_ref, mats_ref, first_ref, last_ref = views(wide_ref, table_ref)
    fill_tables(first_ref, last_ref, tw_ref, mats_ref)
    w_in = stack_ref[0:UNITS, 0:3 * FEAT_PAD]
    w_mid = stack_ref[UNITS:2 * UNITS, 0:3 * UNITS]
    w_out = stack_ref[2 * UNITS:2 * UNITS + 2 * CH, 0:3 * UNITS]
    taps = [small_ref[:, at_taps + f * 8:at_taps + f * 8 + TAPS] for f in range(3)]
    rate = small_ref[:, at_rate:at_rate + 1]
    skip = small_ref[:, at_skip:at_skip + 1]
    par_ref[...] = jnp.concatenate(taps + [jnp.zeros((CH, 128 - 3 * TAPS), f32)], 1)
    gain = jnp.sqrt(2.0 * rate)

    band = lax.broadcasted_iota(jnp.int32, (BANDS, BLK), 0).astype(f32)
    at = lax.broadcasted_iota(jnp.int32, (BANDS, BLK), 1).astype(f32)
    span = float((BANDS - 1) * (BANDS - 1))
    freq = 1.0 + jnp.floor((band * band * (TOKENS // 4 - 1) + 0.5) * (1.0 / span))
    inner = freq * at * (1.0 / TOKENS)
    inner = inner - jnp.round(inner)
    inner_cos, inner_sin = sine_turns(inner + 0.25), sine_turns(inner)
    outer = freq * at * (1.0 / NBLK)
    outer = outer - jnp.round(outer)
    outer_cos, outer_sin = sine_turns(outer + 0.25), sine_turns(outer)
    ramp_row = lax.broadcasted_iota(jnp.int32, (FEAT_PAD - 2 * BANDS, BLK), 0) == 0
    ramp_at = lax.broadcasted_iota(jnp.int32, (FEAT_PAD - 2 * BANDS, BLK), 1).astype(f32)

    def features(a):
        turn_cos, turn_sin = outer_cos[:, a:a + 1], outer_sin[:, a:a + 1]
        ramp = jnp.where(ramp_row, (ramp_at + float(a * BLK)) * (1.0 / TOKENS), 0.0)
        return jnp.concatenate([inner_cos * turn_cos - inner_sin * turn_sin,
                                inner_sin * turn_cos + inner_cos * turn_sin, ramp], 0)

    lane = lax.broadcasted_iota(jnp.int32, (CH, CHUNK), 1).astype(f32)
    per_chunk = CHUNK // BLK
    for chunk in range(TOKENS // CHUNK):
        feat = jnp.concatenate([features(chunk * per_chunk + n) for n in range(per_chunk)], 1)
        top, low = split(feat)
        one = sine_turns(mm(w_in, jnp.concatenate([top, low, top], 0)))
        top, low = split(one)
        two = sine_turns(mm(w_mid, jnp.concatenate([top, low, top], 0)))
        top = two.astype(bf16)
        shape = mm(jnp.concatenate([w_out[:CH, :UNITS], w_out[CH:, 2 * UNITS:]], 0), top)
        shape = shape[:CH] + shape[CH:]
        taper = gain * jnp.exp(-rate * (lane + float(chunk * CHUNK))) * shape
        for n in range(per_chunk):
            first_row = (chunk * per_chunk + n) * CH
            rows_ref[first_row:first_row + CH, :] = taper[:, n * BLK:(n + 1) * BLK]
    spec = forward(rows_ref, first_ref, tw_ref, mats_ref)
    direct = jnp.concatenate([jnp.broadcast_to(skip[c:c + 1], (NBLK, BLK)) for c in range(CH)], 0)
    spec_ref[:, :BLK] = spec[:, :BLK] + direct
    spec_ref[:, BLK:] = spec[:, BLK:]


def conv_kernel(field_ref, wide_ref, table_ref, other_hbm, out_ref, other_ref, query_ref, prod_ref,
                conv_ref, raw_ref, edge_ref, sem):
    swap = pltpu.make_async_copy(other_hbm, other_ref, sem)
    swap.start()
    spec_ref, tw_ref, par_ref, mats_ref, first_ref, last_ref = views(wide_ref, table_ref)
    par = par_ref[...]
    order = first_order()
    sub = lax.broadcasted_iota(jnp.int32, (CH, BLK), 0) < 4
    at_lane = lax.broadcasted_iota(jnp.int32, (CH, BLK), 1)
    raw_ref[0:CH, :] = jnp.zeros((CH, BLK), f32)
    edge_ref[0:CH, :] = jnp.zeros((CH, BLK), f32)
    for quad in range(0, NBLK, 4):
        rows = field_ref[quad * PIECE:(quad + 4) * PIECE, :].astype(f32)
        for pair in range(2):
            five = [rows[pair * 2 * PIECE + n * CH:pair * 2 * PIECE + (n + 1) * CH] for n in range(5)]
            even, odd = order[quad + pair * 2], order[quad + pair * 2 + 1]
            prod_ref[even * CH:(even + 1) * CH, :] = five[0]
            prod_ref[odd * CH:(odd + 1) * CH, :] = pltpu.roll(jnp.where(sub, five[3], five[2]), 4, 0)
            raw_ref[(even + 1) * CH:(even + 2) * CH, :] = five[1]
            raw_ref[(odd + 1) * CH:(odd + 2) * CH, :] = pltpu.roll(jnp.where(sub, five[4], five[3]), 4, 0)
            edge_ref[4 + even * 4:8 + even * 4, :] = five[2][0:4]
            edge_ref[4 + odd * 4:8 + odd * 4, :] = five[4][4:8]

    both_taps = []
    for j in range(TAPS):
        mine = jnp.where(at_lane % HALF < HALF // 2, par[:, TAPS + j:TAPS + j + 1],
                         par[:, 2 * TAPS + j:2 * TAPS + j + 1])
        both_taps.append(jnp.where(sub == (at_lane < HALF), mine, pltpu.roll(mine, 4, 0))[None])
    shape = (NBLK // 2, CH, BLK)
    from_past = lax.broadcasted_iota(jnp.int32, shape, 2) % (HALF // 2) < EDGE
    now = jnp.where(from_past, edge_ref[0:4 * NBLK, :].reshape(shape), edge_ref[4:4 + 4 * NBLK, :].reshape(shape))
    past = pltpu.roll(now, 1, 2)
    total = pltpu.roll(both_taps[6] * now, 2, 2) + (both_taps[4] * now + both_taps[5] * past)
    total = pltpu.roll(total, 2, 2) + (both_taps[2] * now + both_taps[3] * past)
    total = pltpu.roll(total, 2, 2) + (both_taps[0] * now + both_taps[1] * past)
    total = total.astype(bf16).astype(f32)
    total = total * pltpu.roll(total, BLK - HALF // 2, 2)
    left, right = pltpu.roll(total, BLK - EDGE, 2), pltpu.roll(total, BLK - HALF - EDGE, 2)
    subs = lax.broadcasted_iota(jnp.int32, shape, 1) < 4
    fixed = jnp.stack([jnp.where(subs, left, pltpu.roll(right, 4, 1)),
                       jnp.where(subs, pltpu.roll(left, 4, 1), right)], 1).reshape(NBLK * CH, BLK)
    head = lax.broadcasted_iota(jnp.int32, (NBLK * CH, BLK), 1) < EDGE
    prod_ref[...] = jnp.where(head, fixed, prod_ref[...])

    taps = [jnp.broadcast_to(par[:, n:n + 1], (CH, BLK))[None] for n in range(TAPS)]
    span = 8
    lane = lax.broadcasted_iota(jnp.int32, (span + 1, CH, BLK), 2)

    def later(value, steps):
        turned = pltpu.roll(value, steps, 2)
        return jnp.where(lane < steps, jnp.concatenate([turned[:1], turned[:-1]], 0), turned)

    for start in range(0, NBLK, span):
        now = raw_ref[start * CH:(start + span + 1) * CH, :].reshape(span + 1, CH, BLK)
        past = later(now, 1)
        total = later(taps[6] * now, 2) + (taps[4] * now + taps[5] * past)
        total = later(total, 2) + (taps[2] * now + taps[3] * past)
        total = later(total, 2) + (taps[0] * now + taps[1] * past)
        total = total[1:].astype(bf16).astype(f32)
        query_ref[start * CH:(start + span) * CH, :] = total.reshape(span * CH, BLK)
    spec = forward(prod_ref, first_ref, tw_ref, mats_ref)
    s_re, s_im = spec[:, :BLK], spec[:, BLK:]
    h_re, h_im = spec_ref[:, :BLK], spec_ref[:, BLK:]
    both = jnp.concatenate([s_re * h_re - s_im * h_im, -(s_re * h_im + s_im * h_re)], 1)
    back = mm(both.astype(bf16), mats_ref[...])
    tw_re, tw_im = tw_ref[0][...], tw_ref[1][...]
    cols = []
    for c in range(CH):
        re, im = back[c * NBLK:(c + 1) * NBLK, :BLK], back[c * NBLK:(c + 1) * NBLK, BLK:]
        cols.append(jnp.concatenate([re * tw_re - im * tw_im, -(re * tw_im + im * tw_re)], 0))
    top = jnp.concatenate(cols, 1).astype(bf16)
    conv = mm(last_ref[...], jnp.concatenate([top, top], 0))
    for c in range(CH):
        conv_ref[pl.ds(c, NBLK, stride=CH), :] = conv[:, c * BLK:(c + 1) * BLK]
    order = second_order()
    same = sub == (at_lane < HALF)
    lane = lax.broadcasted_iota(jnp.int32, (BLK, BLK), 1)
    slot = lane % HALF // SHARE
    token = lane // HALF * SHARE + (slot ^ slot // 2) * (2 * SHARE) + lane % SHARE
    reorder = (lax.broadcasted_iota(jnp.int32, (BLK, BLK), 0) == token).astype(f32).astype(bf16)

    for slot in range(0, NBLK, 8):
        gated = []
        for ctx in order[slot:slot + 8]:
            rows = slice(ctx * CH, (ctx + 1) * CH)
            gated.append(query_ref[rows, :] * conv_ref[rows, :])
        gated = mm(jnp.concatenate(gated, 0).astype(bf16), reorder)
        tops, lows = [], []
        for n in range(0, 8, 2):
            pair = []
            for at in (n * CH, (n + 1) * CH):
                rows = gated[at:at + CH]
                pair.append(jnp.where(same, rows, pltpu.roll(pltpu.roll(rows, 4, 0), HALF, 1)))
            tops.append(jnp.where(sub, pair[0], pltpu.roll(pair[1], 4, 0)))
            lows.append(jnp.where(sub, pltpu.roll(pair[0], 4, 0), pair[1]))
        at = slot * 4
        out_ref[at:at + 32, :] = jnp.concatenate(tops, 0).astype(bf16)
        out_ref[at + NBLK * 4:at + NBLK * 4 + 32, :] = jnp.concatenate(lows, 0).astype(bf16)
    swap.wait()


def project_kernel(rows_ref, own_ref, other_ref, out_ref):
    core = lax.axis_index("ch") % 2
    depth = rows_ref.shape[0] // 2

    def turned(part):
        rows = rows_ref[pl.ds(pl.multiple_of(part * depth, depth), depth), :]
        return rows.astype(f32).T.astype(bf16)

    own, other = turned(core), turned(1 - core)
    total = mm(own[:HALF], own_ref[:depth, :]) + mm(own[HALF:], own_ref[depth:, :])
    total = total + mm(other[:HALF], other_ref[:depth, :]) + mm(other[HALF:], other_ref[depth:, :])
    out_ref[...] = total.astype(bf16)


def per_device(query_field, key_field, value_field, short_taps, filt_in, filt_mid, filt_out,
               decay_rate, skip_gain, out_weight):
    chans = query_field.shape[1]
    cores = 2
    groups = lax.axis_size("ch")
    chips = groups // cores
    dout = out_weight.shape[1]
    params = pltpu.CompilerParams(vmem_limit_bytes=32 * 1024 * 1024)
    far = pl.BlockSpec(memory_space=pltpu.HBM)
    operands = (query_field, key_field, value_field, filt_in, filt_mid, filt_out, short_taps,
                decay_rate.reshape(1, chans), skip_gain.reshape(1, chans))
    parts, pack = pl.pallas_call(
        prep_kernel,
        out_shape=[jax.ShapeDtypeStruct((NBLK * PIECE, BLK), bf16),
                   jax.ShapeDtypeStruct((PACK_ROWS, chans), f32)],
        in_specs=[far] * len(operands),
        scratch_shapes=[pltpu.VMEM((3,) + query_field.shape, bf16)]
        + [pltpu.VMEM(t.shape, t.dtype) for t in operands[3:]]
        + [pltpu.VMEM((2 * chans // BLK, 8 + BLK, BLK), f32), pltpu.VMEM((BLK, chans // 2), f32),
           pltpu.SemaphoreType.DMA((len(operands),))],
        compiler_params=pltpu.CompilerParams(vmem_limit_bytes=62 * 1024 * 1024),
        name="prep",
    )(*operands)
    fields = lax.all_to_all(parts.reshape(NBLK, PIECE // 4, 4, BLK), "ctx", 0, 0, tiled=True,
                            axis_index_groups=[first_order()]).reshape(NBLK * PIECE, BLK)
    small, stack = pl.pallas_call(
        weights_kernel,
        out_shape=[jax.ShapeDtypeStruct((CH, 128), f32),
                   jax.ShapeDtypeStruct((2 * UNITS + 2 * CH, 2 * BLK), bf16)],
        compiler_params=params,
        name="weights",
    )(pack)
    own_weight, small = lax.optimization_barrier((out_weight, small))
    other_weight = lax.ppermute(own_weight, "ch", [(d, d ^ 1) for d in range(groups)])
    wide, table = pl.pallas_call(
        filter_kernel,
        out_shape=[jax.ShapeDtypeStruct((CH * NBLK + NBLK + CH, 2 * BLK), f32),
                   jax.ShapeDtypeStruct((4 * BLK, 2 * BLK), bf16)],
        scratch_shapes=[pltpu.VMEM((NBLK * CH, BLK), f32)],
        compiler_params=params,
        cost_estimate=pl.CostEstimate(flops=10**11, bytes_accessed=10**9, transcendentals=10**6),
        name="filter",
    )(small, stack)
    gated, other_weight = pl.pallas_call(
        conv_kernel,
        out_shape=[jax.ShapeDtypeStruct((NBLK * CH, BLK), bf16),
                   jax.ShapeDtypeStruct(out_weight.shape, bf16)],
        in_specs=[pl.BlockSpec(memory_space=pltpu.VMEM)] * 3 + [far],
        scratch_shapes=[pltpu.VMEM((NBLK * CH, BLK), f32)] * 3
        + [pltpu.VMEM(((NBLK + 1) * CH, BLK), f32), pltpu.VMEM((4 * NBLK + CH, BLK), f32),
           pltpu.SemaphoreType.DMA],
        compiler_params=params,
        name="convolve",
    )(fields, wide, table, other_weight)
    on_chip = [[c * groups + x * cores + k for k in range(cores) for c in second_order()] for x in range(chips)]
    returned = lax.all_to_all(gated.reshape(NBLK * cores, CH // cores, BLK), ("ctx", "ch"), 0, 0,
                              tiled=True, axis_index_groups=on_chip)
    partial = pl.pallas_call(
        project_kernel,
        out_shape=jax.ShapeDtypeStruct((BLK // cores, dout), bf16),
        compiler_params=params,
        name="project",
    )(returned.reshape(NBLK * CH, BLK), own_weight, other_weight)
    along_x = [[(x ^ x // 2) * cores + k for x in range(chips)] for k in range(cores)]
    shares = lax.all_to_all(partial.reshape(chips, SHARE, dout), "ch", 0, 0, tiled=True,
                            axis_index_groups=along_x)
    return jnp.sum(shares.astype(f32), 0).astype(bf16)


def solution(mesh):
    return jax.shard_map(
        per_device,
        mesh=mesh,
        in_specs=(
            P("ctx", "ch"),
            P("ctx", "ch"),
            P("ctx", "ch"),
            P(None, None, "ch"),
            P(),
            P(),
            P(None, "ch"),
            P("ch"),
            P("ch"),
            P("ch", None),
        ),
        out_specs=P(("ctx", "ch"), None),
        check_vma=False,
    )
```

```python
import math

import jax
import jax.numpy as jnp
import numpy as np
from jax import lax
from jax.experimental import pallas as pl
from jax.experimental.pallas import tpu as pltpu
from jax.sharding import PartitionSpec as P

TOKENS = 8192
BLK = 128
NBLK = 64
CH = 8
BANDS = 16
FEAT = 33
FEAT_PAD = 48
HALF = 64
SHARE = 16
TAPS = 7
EDGE = TAPS - 1
PIECE = 20
FIRST = 13
SECOND = 43
UNITS = 64
CHUNK = 4096
PACK = (0, 64, 88, 96, 104, 112)
PACK_ROWS = 120
bf16 = jnp.bfloat16
f32 = jnp.float32
highest = lax.Precision.HIGHEST


def first_order():
    return [FIRST * n % NBLK for n in range(NBLK)]


def second_order():
    return [SECOND * n % NBLK for n in range(NBLK)]


def second_place(ctx):
    return pow(SECOND, -1, NBLK) * ctx % NBLK


def sine_coefs():
    grid = 0.25 * np.cos((np.arange(400) + 0.5) * math.pi / 400)
    grid = np.concatenate([grid, 0.5 * np.cos((np.arange(800) + 0.5) * math.pi / 800)])
    grid = grid[np.abs(grid) > 1e-3]
    powers = np.stack([grid ** (2 * k + 1) for k in range(7)], 1)
    coef, *_ = np.linalg.lstsq(powers, np.sin(2.0 * math.pi * grid), rcond=None)
    return [float(c) for c in coef]


SINE = sine_coefs()
NEAREST = 1.5 * 2.0**23


def sine_turns(turns):
    rest = turns - ((turns + NEAREST) - NEAREST)
    sq = rest * rest
    acc = sq * SINE[-1] + SINE[-2]
    for c in SINE[-3::-1]:
        acc = acc * sq + c
    return acc * rest


def split(value):
    top = value.astype(bf16)
    return top, (value - top.astype(f32)).astype(bf16)


def mm(left, right):
    return jnp.dot(left, right, preferred_element_type=f32)


def prep_kernel(query_hbm, key_hbm, value_hbm, w_in_hbm, w_mid_hbm, w_out_hbm, taps_hbm, rate_hbm,
                skip_hbm, out_ref, pack_ref, held, w_in_ref, w_mid_ref, w_out_ref, taps_ref, rate_ref,
                skip_ref, lead_ref, edge_ref, sems):
    sources = (taps_hbm, key_hbm, value_hbm, query_hbm, w_out_hbm, w_mid_hbm, w_in_hbm, rate_hbm, skip_hbm)
    targets = (taps_ref, held.at[1], held.at[2], held.at[0], w_out_ref, w_mid_ref, w_in_ref, rate_ref, skip_ref)
    copies = [pltpu.make_async_copy(src, dst, sems.at[n])
              for n, (src, dst) in enumerate(zip(sources, targets))]
    for copy in copies:
        copy.start()
    low_half = lax.broadcasted_iota(jnp.int32, (NBLK // 2, CH, BLK), 1) < 4
    half = edge_ref.shape[1]
    edge_ref[...] = jnp.zeros_like(edge_ref)
    copies[0].wait()
    mixed = []
    blocks = range(2 * half // BLK)
    for f in (1, 2):
        copies[f].wait()
        parts = []
        for n in blocks:
            lead = lead_ref.at[(f - 1) * len(blocks) + n]
            lanes = slice(n * BLK, (n + 1) * BLK)
            lead[0:8, :] = jnp.zeros((8, BLK), f32)
            lead[8:8 + BLK, :] = held[f, :, lanes].astype(f32)
            total = taps_ref[f, 0:1, lanes] * lead[8:8 + BLK, :]
            for j in range(1, TAPS):
                total = total + taps_ref[f, j:j + 1, lanes] * lead[8 - j:8 - j + BLK, :]
            parts.append(total.astype(bf16).astype(f32))
            at = n * BLK // half * HALF + (f - 1) * (HALF // 2)
            lanes = slice(n * BLK % half, n * BLK % half + BLK)
            edge_ref[at:at + EDGE, lanes] = lead[8 + BLK - EDGE:8 + BLK, :]
            edge_ref[at + EDGE:at + 2 * EDGE, lanes] = lead[8:8 + EDGE, :]
        mixed.append(jnp.concatenate(parts, 1))

    def pairs(field):
        rows = field.T.reshape(2, NBLK // 2, CH, BLK)
        up = pltpu.roll(rows[1], 4, 1)
        return jnp.where(low_half, rows[0], up), jnp.where(low_half, up, rows[0])

    prod_even, prod_odd = pairs(mixed[0] * mixed[1])
    copies[3].wait()
    query_even, query_odd = pairs(held[0].astype(f32))
    edges = edge_ref[...].T.reshape(NBLK // 2, CH, BLK)
    low = low_half[0]
    places = [second_place(ctx) for ctx in first_order()]
    for slot in range(0, NBLK, 4):
        rows = []
        for n in (slot, slot + 2):
            even, odd = places[n] // 2, places[n + 1] // 2
            rows += [prod_even[even], query_even[even], jnp.where(low, edges[even], prod_odd[odd]),
                     jnp.where(low, prod_odd[odd], query_odd[odd]), jnp.where(low, query_odd[odd], edges[odd])]
        out_ref[slot * PIECE:(slot + 4) * PIECE, :] = jnp.concatenate(rows, 0).astype(bf16)
    for copy in copies[4:]:
        copy.wait()
    chans = rate_ref.shape[1]
    at_out, at_taps, at_rate, at_skip, at_mid, at_in = PACK
    pack_ref[at_out:at_out + UNITS, :] = w_out_ref[...]
    for f in range(3):
        pack_ref[at_taps + f * 8:at_taps + f * 8 + TAPS, :] = taps_ref[f]
    pack_ref[at_rate:at_rate + 8, :] = jnp.broadcast_to(rate_ref[...], (8, chans))
    pack_ref[at_skip:at_skip + 8, :] = jnp.broadcast_to(skip_ref[...], (8, chans))
    for n in range(8):
        pack_ref[at_mid:at_mid + 8, n * UNITS:(n + 1) * UNITS] = w_mid_ref[n * 8:(n + 1) * 8, :]
    for n in range(4):
        pack_ref[at_in:at_in + 8, n * UNITS:(n + 1) * UNITS] = w_in_ref[n * 8:(n + 1) * 8, :]
    pack_ref[at_in:at_in + 1, 4 * UNITS:5 * UNITS] = w_in_ref[FEAT - 1:FEAT, :]


def forward(rows_ref, first_ref, tw_ref, mats_ref):
    cols = jnp.concatenate([rows_ref[pl.ds(c, NBLK, stride=CH), :] for c in range(CH)], 1)
    top, low = split(cols)
    outer = mm(first_ref[...], jnp.concatenate([top, low, top], 0))
    tw_re, tw_im = tw_ref[0][...], tw_ref[1][...]
    out = []
    for c in range(CH):
        lanes = slice(c * BLK, (c + 1) * BLK)
        re, im = outer[:NBLK, lanes], outer[NBLK:, lanes]
        out.append(jnp.concatenate([re * tw_re - im * tw_im, re * tw_im + im * tw_re], 1))
    return mm(jnp.concatenate(out, 0).astype(bf16), mats_ref[...])


def views(wide_ref, table_ref):
    half = 2 * BLK
    spec = wide_ref.at[0:CH * NBLK]
    tw = [wide_ref.at[CH * NBLK:CH * NBLK + NBLK, n * BLK:(n + 1) * BLK] for n in range(2)]
    par = wide_ref.at[CH * NBLK + NBLK:CH * NBLK + NBLK + CH, 0:BLK]
    mats = table_ref.at[0:half]
    first = table_ref.at[half:half + BLK, 0:3 * NBLK]
    last = [table_ref.at[half + BLK + n * NBLK:half + BLK + (n + 1) * NBLK, 0:3 * NBLK]
            for n in range(2)]
    return spec, tw, par, mats, first, last


def fill_tables(first_ref, last_ref, tw_ref, mats_ref):
    def grid(shape, axis):
        return lax.broadcasted_iota(jnp.int32, shape, axis)

    def wave(turns):
        turns = turns - jnp.round(turns)
        return sine_turns(turns + 0.25), sine_turns(turns)

    shape = (NBLK, NBLK)
    cos, sin = wave((grid(shape, 0).astype(f32) - 0.25) * grid(shape, 1).astype(f32) / NBLK)
    top, low = split(jnp.concatenate([cos, -sin], 0))
    first_ref[...] = jnp.concatenate([top, top, low], 1)
    cos, sin = wave((grid(shape, 1).astype(f32) - 0.25) * grid(shape, 0).astype(f32) / NBLK)
    top, low = split(jnp.concatenate([cos, -sin], 1) / TOKENS)
    wide = jnp.concatenate([top, top, low], 1)
    last_ref[0][...], last_ref[1][...] = wide[:, :3 * NBLK], wide[:, 3 * NBLK:]
    shape = (NBLK, BLK)
    shifted = grid(shape, 0).astype(f32) - 0.25
    cos, sin = wave(shifted * grid(shape, 1).astype(f32) / TOKENS)
    tw_ref[0][...], tw_ref[1][...] = cos, -sin
    shape = (BLK, BLK)
    cos, sin = wave((grid(shape, 0) * grid(shape, 1)).astype(f32) / BLK)
    mats = jnp.concatenate([jnp.concatenate([cos, -sin], 1), jnp.concatenate([sin, cos], 1)], 0)
    mats_ref[...] = mats.astype(bf16)


def weights_kernel(pack_ref, small_ref, stack_ref):
    at_out, at_taps, at_rate, at_skip, at_mid, at_in = PACK
    chans = pack_ref.shape[1]
    row = lax.broadcasted_iota(jnp.int32, (CH, chans), 0)
    wanted = second_place(lax.axis_index("ctx")) * 4 + row % 4 + row // 4 * (chans // 2)
    pick = (lax.broadcasted_iota(jnp.int32, (CH, chans), 1) == wanted).astype(f32)

    def stack(weights):
        top, low = split(weights)
        return jnp.concatenate([top, top, low], 1)

    mine = lax.dot_general(pick, pack_ref[:at_mid, :], (((1,), (1,)), ((), ())), precision=highest,
                           preferred_element_type=f32)
    per_turn = 1.0 / (2.0 * math.pi)
    w_in = jnp.concatenate([pack_ref[at_in:at_in + 8, n * UNITS:(n + 1) * UNITS] for n in range(4)]
                           + [pack_ref[at_in:at_in + 1, 4 * UNITS:5 * UNITS]], 0)
    padded = jnp.concatenate([w_in[1:FEAT], w_in[0:1], jnp.zeros((FEAT_PAD - FEAT, UNITS), f32)], 0)
    w_mid = jnp.concatenate([pack_ref[at_mid:at_mid + 8, n * UNITS:(n + 1) * UNITS] for n in range(8)], 0)
    small_ref[:, 0:at_mid] = mine
    stack_ref[0:UNITS, 0:3 * FEAT_PAD] = stack(padded.T * per_turn)
    stack_ref[UNITS:2 * UNITS, 0:3 * UNITS] = stack(w_mid.T * per_turn)
    wide = stack(mine[:, at_out:at_out + UNITS])
    stack_ref[2 * UNITS:2 * UNITS + 2 * CH, 0:3 * UNITS] = jnp.concatenate([wide, wide], 0)


def filter_kernel(small_ref, stack_ref, wide_ref, table_ref, rows_ref):
    at_out, at_taps, at_rate, at_skip, at_mid, at_in = PACK
    spec_ref, tw_ref, par_ref, mats_ref, first_ref, last_ref = views(wide_ref, table_ref)
    fill_tables(first_ref, last_ref, tw_ref, mats_ref)
    w_in = stack_ref[0:UNITS, 0:3 * FEAT_PAD]
    w_mid = stack_ref[UNITS:2 * UNITS, 0:3 * UNITS]
    w_out = stack_ref[2 * UNITS:2 * UNITS + 2 * CH, 0:3 * UNITS]
    taps = [small_ref[:, at_taps + f * 8:at_taps + f * 8 + TAPS] for f in range(3)]
    rate = small_ref[:, at_rate:at_rate + 1]
    skip = small_ref[:, at_skip:at_skip + 1]
    par_ref[...] = jnp.concatenate(taps + [jnp.zeros((CH, 128 - 3 * TAPS), f32)], 1)
    gain = jnp.sqrt(2.0 * rate)

    band = lax.broadcasted_iota(jnp.int32, (BANDS, BLK), 0).astype(f32)
    at = lax.broadcasted_iota(jnp.int32, (BANDS, BLK), 1).astype(f32)
    span = float((BANDS - 1) * (BANDS - 1))
    freq = 1.0 + jnp.floor((band * band * (TOKENS // 4 - 1) + 0.5) * (1.0 / span))
    inner = freq * at * (1.0 / TOKENS)
    inner = inner - jnp.round(inner)
    inner_cos, inner_sin = sine_turns(inner + 0.25), sine_turns(inner)
    outer = freq * at * (1.0 / NBLK)
    outer = outer - jnp.round(outer)
    outer_cos, outer_sin = sine_turns(outer + 0.25), sine_turns(outer)
    ramp_row = lax.broadcasted_iota(jnp.int32, (FEAT_PAD - 2 * BANDS, BLK), 0) == 0
    ramp_at = lax.broadcasted_iota(jnp.int32, (FEAT_PAD - 2 * BANDS, BLK), 1).astype(f32)

    def features(a):
        turn_cos, turn_sin = outer_cos[:, a:a + 1], outer_sin[:, a:a + 1]
        ramp = jnp.where(ramp_row, (ramp_at + float(a * BLK)) * (1.0 / TOKENS), 0.0)
        return jnp.concatenate([inner_cos * turn_cos - inner_sin * turn_sin,
                                inner_sin * turn_cos + inner_cos * turn_sin, ramp], 0)

    lane = lax.broadcasted_iota(jnp.int32, (CH, CHUNK), 1).astype(f32)
    per_chunk = CHUNK // BLK
    for chunk in range(TOKENS // CHUNK):
        feat = jnp.concatenate([features(chunk * per_chunk + n) for n in range(per_chunk)], 1)
        top, low = split(feat)
        one = sine_turns(mm(w_in, jnp.concatenate([top, low, top], 0)))
        top, low = split(one)
        two = sine_turns(mm(w_mid, jnp.concatenate([top, low, top], 0)))
        top = two.astype(bf16)
        shape = mm(jnp.concatenate([w_out[:CH, :UNITS], w_out[CH:, 2 * UNITS:]], 0), top)
        shape = shape[:CH] + shape[CH:]
        taper = gain * jnp.exp(-rate * (lane + float(chunk * CHUNK))) * shape
        for n in range(per_chunk):
            first_row = (chunk * per_chunk + n) * CH
            rows_ref[first_row:first_row + CH, :] = taper[:, n * BLK:(n + 1) * BLK]
    spec = forward(rows_ref, first_ref, tw_ref, mats_ref)
    direct = jnp.concatenate([jnp.broadcast_to(skip[c:c + 1], (NBLK, BLK)) for c in range(CH)], 0)
    spec_ref[:, :BLK] = spec[:, :BLK] + direct
    spec_ref[:, BLK:] = spec[:, BLK:]


def conv_kernel(field_ref, wide_ref, table_ref, other_hbm, out_ref, other_ref, query_ref, prod_ref,
                conv_ref, raw_ref, edge_ref, sem):
    swap = pltpu.make_async_copy(other_hbm, other_ref, sem)
    swap.start()
    spec_ref, tw_ref, par_ref, mats_ref, first_ref, last_ref = views(wide_ref, table_ref)
    par = par_ref[...]
    order = first_order()
    sub = lax.broadcasted_iota(jnp.int32, (CH, BLK), 0) < 4
    at_lane = lax.broadcasted_iota(jnp.int32, (CH, BLK), 1)
    raw_ref[0:CH, :] = jnp.zeros((CH, BLK), f32)
    edge_ref[0:CH, :] = jnp.zeros((CH, BLK), f32)
    for quad in range(0, NBLK, 4):
        rows = field_ref[quad * PIECE:(quad + 4) * PIECE, :].astype(f32)
        for pair in range(2):
            five = [rows[pair * 2 * PIECE + n * CH:pair * 2 * PIECE + (n + 1) * CH] for n in range(5)]
            even, odd = order[quad + pair * 2], order[quad + pair * 2 + 1]
            prod_ref[even * CH:(even + 1) * CH, :] = five[0]
            prod_ref[odd * CH:(odd + 1) * CH, :] = pltpu.roll(jnp.where(sub, five[3], five[2]), 4, 0)
            raw_ref[(even + 1) * CH:(even + 2) * CH, :] = five[1]
            raw_ref[(odd + 1) * CH:(odd + 2) * CH, :] = pltpu.roll(jnp.where(sub, five[4], five[3]), 4, 0)
            edge_ref[4 + even * 4:8 + even * 4, :] = five[2][0:4]
            edge_ref[4 + odd * 4:8 + odd * 4, :] = five[4][4:8]

    both_taps = []
    for j in range(TAPS):
        mine = jnp.where(at_lane % HALF < HALF // 2, par[:, TAPS + j:TAPS + j + 1],
                         par[:, 2 * TAPS + j:2 * TAPS + j + 1])
        both_taps.append(jnp.where(sub == (at_lane < HALF), mine, pltpu.roll(mine, 4, 0))[None])
    shape = (NBLK // 2, CH, BLK)
    from_past = lax.broadcasted_iota(jnp.int32, shape, 2) % (HALF // 2) < EDGE
    now = jnp.where(from_past, edge_ref[0:4 * NBLK, :].reshape(shape), edge_ref[4:4 + 4 * NBLK, :].reshape(shape))
    past = pltpu.roll(now, 1, 2)
    total = pltpu.roll(both_taps[6] * now, 2, 2) + (both_taps[4] * now + both_taps[5] * past)
    total = pltpu.roll(total, 2, 2) + (both_taps[2] * now + both_taps[3] * past)
    total = pltpu.roll(total, 2, 2) + (both_taps[0] * now + both_taps[1] * past)
    total = total.astype(bf16).astype(f32)
    total = total * pltpu.roll(total, BLK - HALF // 2, 2)
    left, right = pltpu.roll(total, BLK - EDGE, 2), pltpu.roll(total, BLK - HALF - EDGE, 2)
    subs = lax.broadcasted_iota(jnp.int32, shape, 1) < 4
    fixed = jnp.stack([jnp.where(subs, left, pltpu.roll(right, 4, 1)),
                       jnp.where(subs, pltpu.roll(left, 4, 1), right)], 1).reshape(NBLK * CH, BLK)
    head = lax.broadcasted_iota(jnp.int32, (NBLK * CH, BLK), 1) < EDGE
    prod_ref[...] = jnp.where(head, fixed, prod_ref[...])

    taps = [jnp.broadcast_to(par[:, n:n + 1], (CH, BLK))[None] for n in range(TAPS)]
    span = 8
    lane = lax.broadcasted_iota(jnp.int32, (span + 1, CH, BLK), 2)

    def later(value, steps):
        turned = pltpu.roll(value, steps, 2)
        return jnp.where(lane < steps, jnp.concatenate([turned[:1], turned[:-1]], 0), turned)

    for start in range(0, NBLK, span):
        now = raw_ref[start * CH:(start + span + 1) * CH, :].reshape(span + 1, CH, BLK)
        past = later(now, 1)
        total = later(taps[6] * now, 2) + (taps[4] * now + taps[5] * past)
        total = later(total, 2) + (taps[2] * now + taps[3] * past)
        total = later(total, 2) + (taps[0] * now + taps[1] * past)
        total = total[1:].astype(bf16).astype(f32)
        query_ref[start * CH:(start + span) * CH, :] = total.reshape(span * CH, BLK)
    spec = forward(prod_ref, first_ref, tw_ref, mats_ref)
    s_re, s_im = spec[:, :BLK], spec[:, BLK:]
    h_re, h_im = spec_ref[:, :BLK], spec_ref[:, BLK:]
    both = jnp.concatenate([s_re * h_re - s_im * h_im, -(s_re * h_im + s_im * h_re)], 1)
    back = mm(both.astype(bf16), mats_ref[...])
    tw_re, tw_im = tw_ref[0][...], tw_ref[1][...]
    cols = []
    for c in range(CH):
        re, im = back[c * NBLK:(c + 1) * NBLK, :BLK], back[c * NBLK:(c + 1) * NBLK, BLK:]
        cols.append(jnp.concatenate([re * tw_re - im * tw_im, -(re * tw_im + im * tw_re)], 0))
    top, low = split(jnp.concatenate(cols, 1))
    last = jnp.concatenate([last_ref[0][...], last_ref[1][...]], 1)
    conv = mm(last, jnp.concatenate([top, low, top], 0))
    for c in range(CH):
        conv_ref[pl.ds(c, NBLK, stride=CH), :] = conv[:, c * BLK:(c + 1) * BLK]
    order = second_order()
    same = sub == (at_lane < HALF)
    lane = lax.broadcasted_iota(jnp.int32, (BLK, BLK), 1)
    slot = lane % HALF // SHARE
    token = lane // HALF * SHARE + (slot ^ slot // 2) * (2 * SHARE) + lane % SHARE
    reorder = (lax.broadcasted_iota(jnp.int32, (BLK, BLK), 0) == token).astype(f32).astype(bf16)

    for slot in range(0, NBLK, 8):
        gated = []
        for ctx in order[slot:slot + 8]:
            rows = slice(ctx * CH, (ctx + 1) * CH)
            gated.append(query_ref[rows, :] * conv_ref[rows, :])
        gated = mm(jnp.concatenate(gated, 0).astype(bf16), reorder)
        tops, lows = [], []
        for n in range(0, 8, 2):
            pair = []
            for at in (n * CH, (n + 1) * CH):
                rows = gated[at:at + CH]
                pair.append(jnp.where(same, rows, pltpu.roll(pltpu.roll(rows, 4, 0), HALF, 1)))
            tops.append(jnp.where(sub, pair[0], pltpu.roll(pair[1], 4, 0)))
            lows.append(jnp.where(sub, pltpu.roll(pair[0], 4, 0), pair[1]))
        at = slot * 4
        out_ref[at:at + 32, :] = jnp.concatenate(tops, 0).astype(bf16)
        out_ref[at + NBLK * 4:at + NBLK * 4 + 32, :] = jnp.concatenate(lows, 0).astype(bf16)
    swap.wait()


def project_kernel(rows_ref, own_ref, other_ref, out_ref):
    core = lax.axis_index("ch") % 2
    depth = rows_ref.shape[0] // 2

    def turned(part):
        rows = rows_ref[pl.ds(pl.multiple_of(part * depth, depth), depth), :]
        return rows.astype(f32).T.astype(bf16)

    own, other = turned(core), turned(1 - core)
    total = mm(own[:HALF], own_ref[:depth, :]) + mm(own[HALF:], own_ref[depth:, :])
    total = total + mm(other[:HALF], other_ref[:depth, :]) + mm(other[HALF:], other_ref[depth:, :])
    out_ref[...] = total.astype(bf16)


def per_device(query_field, key_field, value_field, short_taps, filt_in, filt_mid, filt_out,
               decay_rate, skip_gain, out_weight):
    chans = query_field.shape[1]
    cores = 2
    groups = lax.axis_size("ch")
    chips = groups // cores
    dout = out_weight.shape[1]
    params = pltpu.CompilerParams(vmem_limit_bytes=32 * 1024 * 1024)
    far = pl.BlockSpec(memory_space=pltpu.HBM)
    operands = (query_field, key_field, value_field, filt_in, filt_mid, filt_out, short_taps,
                decay_rate.reshape(1, chans), skip_gain.reshape(1, chans))
    parts, pack = pl.pallas_call(
        prep_kernel,
        out_shape=[jax.ShapeDtypeStruct((NBLK * PIECE, BLK), bf16),
                   jax.ShapeDtypeStruct((PACK_ROWS, chans), f32)],
        in_specs=[far] * len(operands),
        scratch_shapes=[pltpu.VMEM((3,) + query_field.shape, bf16)]
        + [pltpu.VMEM(t.shape, t.dtype) for t in operands[3:]]
        + [pltpu.VMEM((2 * chans // BLK, 8 + BLK, BLK), f32), pltpu.VMEM((BLK, chans // 2), f32),
           pltpu.SemaphoreType.DMA((len(operands),))],
        compiler_params=pltpu.CompilerParams(vmem_limit_bytes=62 * 1024 * 1024),
        name="prep",
    )(*operands)
    fields = lax.all_to_all(parts.reshape(NBLK, PIECE // 4, 4, BLK), "ctx", 0, 0, tiled=True,
                            axis_index_groups=[first_order()]).reshape(NBLK * PIECE, BLK)
    small, stack = pl.pallas_call(
        weights_kernel,
        out_shape=[jax.ShapeDtypeStruct((CH, 128), f32),
                   jax.ShapeDtypeStruct((2 * UNITS + 2 * CH, 2 * BLK), bf16)],
        compiler_params=params,
        name="weights",
    )(pack)
    own_weight, small = lax.optimization_barrier((out_weight, small))
    other_weight = lax.ppermute(own_weight, "ch", [(d, d ^ 1) for d in range(groups)])
    wide, table = pl.pallas_call(
        filter_kernel,
        out_shape=[jax.ShapeDtypeStruct((CH * NBLK + NBLK + CH, 2 * BLK), f32),
                   jax.ShapeDtypeStruct((4 * BLK, 2 * BLK), bf16)],
        scratch_shapes=[pltpu.VMEM((NBLK * CH, BLK), f32)],
        compiler_params=params,
        cost_estimate=pl.CostEstimate(flops=10**11, bytes_accessed=10**9, transcendentals=10**6),
        name="filter",
    )(small, stack)
    gated, other_weight = pl.pallas_call(
        conv_kernel,
        out_shape=[jax.ShapeDtypeStruct((NBLK * CH, BLK), bf16),
                   jax.ShapeDtypeStruct(out_weight.shape, bf16)],
        in_specs=[pl.BlockSpec(memory_space=pltpu.VMEM)] * 3 + [far],
        scratch_shapes=[pltpu.VMEM((NBLK * CH, BLK), f32)] * 3
        + [pltpu.VMEM(((NBLK + 1) * CH, BLK), f32), pltpu.VMEM((4 * NBLK + CH, BLK), f32),
           pltpu.SemaphoreType.DMA],
        compiler_params=params,
        name="convolve",
    )(fields, wide, table, other_weight)
    on_chip = [[c * groups + x * cores + k for k in range(cores) for c in second_order()] for x in range(chips)]
    returned = lax.all_to_all(gated.reshape(NBLK * cores, CH // cores, BLK), ("ctx", "ch"), 0, 0,
                              tiled=True, axis_index_groups=on_chip)
    partial = pl.pallas_call(
        project_kernel,
        out_shape=jax.ShapeDtypeStruct((BLK // cores, dout), bf16),
        compiler_params=params,
        name="project",
    )(returned.reshape(NBLK * CH, BLK), own_weight, other_weight)
    along_x = [[(x ^ x // 2) * cores + k for x in range(chips)] for k in range(cores)]
    shares = lax.all_to_all(partial.reshape(chips, SHARE, dout), "ch", 0, 0, tiled=True,
                            axis_index_groups=along_x)
    return jnp.sum(shares.astype(f32), 0).astype(bf16)


def solution(mesh):
    return jax.shard_map(
        per_device,
        mesh=mesh,
        in_specs=(
            P("ctx", "ch"),
            P("ctx", "ch"),
            P("ctx", "ch"),
            P(None, None, "ch"),
            P(),
            P(),
            P(None, "ch"),
            P("ch"),
            P("ch"),
            P("ch", None),
        ),
        out_specs=P(("ctx", "ch"), None),
        check_vma=False,
    )
```
